32 devices in a mesh: groups: 2 (over y), ra: 4 (over z), dec: 2 (over x), band: 2 (over core).
Axes of the slice: x: 2, y: 2, z: 4, core: 2. Of those that a mesh axis runs over, the one named last changes fastest.
Arguments:
- sky_maps: bfloat16 [512, 312, 256], P(('groups', 'band'), 'ra', 'dec'), parts along dimension 0, may hold values from -12 to 12
- radii: int32 [512], P(('groups', 'band')), parts along dimension 0, may hold values from 1 to 17, as said below
- valid: int32 [624, 256], P(('groups', 'ra'), 'dec'), parts along dimension 0, may hold values from 0 to 1, as said below
Outputs:
- smoothed: bfloat16 [512, 312, 256], P(('groups', 'band'), 'ra', 'dec'), parts along dimension 0
- channel_mean: float32 [512], P(('groups', 'band')), parts along dimension 0
- covariance: float32 [512, 256], P('groups', 'band'), parts along dimension 0
The draws below stay inside these ranges and needn't reach their ends.
There are 2 independent parts, one for each index of `groups`. The reference program is written for one: setup_inputs(seed, part) draws one part's arguments, and reference() takes and returns one part's arrays. A program takes and returns all parts, laid end to end along the dimension named above; each array names one. Nothing has to cross between parts.
Inputs may be any that keep to these rules, and one draw needn't show every extreme that they name: `radii`: some channel has half-width exactly 17. 1 marks a pixel that enters the statistics; the pixel with declination index 0 is valid in every row.
All inputs are finite; a program needn't handle non-finite values.
Results may differ from the reference program's by a relative error of at most 0.012.
The reference program's roundings to bfloat16 on the way count: a program that leaves them out, or rounds other values in their place, can miss the bound.
Values may be sent and summed in bfloat16 or wider, within the bound.
No kernel may reach another device: no remote copies, remote signals or barrier semaphores. Data moves between devices by JAX's collectives and lax.ppermute only.
A program may use at most 64 MiB of HBM per device.

```python
import jax
import jax.numpy as jnp
from jax import lax

CHANNELS = 256
RMAX = 17
NRA = 312
NDEC = 256


def draw_sky_maps(key, part):
    noise_key = jax.random.fold_in(key, 11)
    full_shape = (CHANNELS, NRA, NDEC)
    values = jax.random.normal(noise_key, full_shape, jnp.float32)
    return jnp.clip(values, -12.0, 12.0).astype(jnp.bfloat16)


def draw_radii(key, part):
    pick_key = jax.random.fold_in(key, 21)
    place_key = jax.random.fold_in(key, 22)
    values = jax.random.randint(pick_key, (CHANNELS,), 1, RMAX + 1)
    place = jax.random.randint(place_key, (), 0, CHANNELS)
    return jnp.where(jnp.arange(CHANNELS) == place, RMAX, values).astype(jnp.int32)


def draw_valid(key, part):
    full_shape = (NRA, NDEC)
    along = lax.broadcasted_iota(jnp.int32, full_shape, 0)
    down = lax.broadcasted_iota(jnp.int32, full_shape, 1)
    chance = 200 + 400 * along // NRA + 300 * down // NDEC
    coins = jax.random.randint(jax.random.fold_in(key, 31), full_shape, 0, 1000)
    picked = (coins < chance) | (down == 0)
    return jnp.where(picked, 1, 0).astype(jnp.int32)


def setup_inputs(seed: int = 0, part: int = 0) -> dict:
    seeds = jax.random.split(jax.random.key(seed), 4)
    part_keys = jax.random.split(jax.random.fold_in(seeds[3], part), 4)
    return {
        "sky_maps": draw_sky_maps(jax.random.fold_in(jax.random.fold_in(seeds[3], part), 71), part),
        "radii": draw_radii(jax.random.fold_in(jax.random.fold_in(seeds[3], part), 71), part),
        "valid": draw_valid(jax.random.fold_in(jax.random.fold_in(seeds[3], part), 71), part),
    }


def beam_taps(radii, offsets):
    radius = radii.astype(jnp.float32)
    lead_shape = (radii.shape[0],) + (1,) * offsets.ndim
    radius = radius.reshape(lead_shape)
    spread = 0.5 * radius
    inside = jnp.abs(offsets)[None] <= radius
    return jnp.where(inside, jnp.exp(-(offsets * offsets)[None] / (2.0 * spread * spread)), 0.0)


def reference(sky_maps, radii, valid):
    raw_taps = beam_taps(radii, jnp.arange(-RMAX, RMAX + 1).astype(jnp.float32))
    kernel_taps = (raw_taps / jnp.sum(raw_taps, axis=1)[:, None]).astype(jnp.bfloat16)

    def smooth_one(item):
        plane, weights = item
        values = plane.astype(jnp.float32)
        kernel = weights.astype(jnp.float32)
        padded = jnp.pad(values, ((0, 0), (RMAX, RMAX)))
        across = jnp.zeros(values.shape, jnp.float32)
        for index in range(2 * RMAX + 1):
            across = across + kernel[index] * padded[:, index:index + NDEC]
        across = lax.optimization_barrier(across.astype(jnp.bfloat16)).astype(jnp.float32)
        result = jnp.zeros(values.shape, jnp.float32)
        for index in range(2 * RMAX + 1):
            result = result + kernel[index] * jnp.roll(across, -(index - RMAX), axis=0)
        return result.astype(jnp.bfloat16)

    smoothed = lax.map(smooth_one, (sky_maps, kernel_taps))
    flat = smoothed.reshape(smoothed.shape[0], -1)
    weights = valid.reshape(-1).astype(jnp.float32)
    masked = flat * weights.astype(jnp.bfloat16)[None]
    sums = jnp.sum(masked.astype(jnp.float32), axis=1)
    count = jnp.sum(weights)
    channel_mean = sums / count
    gram = lax.dot_general(masked, masked, (((1,), (1,)), ((), ())), preferred_element_type=jnp.float32)
    covariance = (gram - count * channel_mean[:, None] * channel_mean[None, :]) / (count - 1.0)
    return smoothed, channel_mean, covariance
```

```python
import functools

import jax
import jax.numpy as jnp
from jax import lax
from jax.experimental import pallas as pl
from jax.experimental.pallas import tpu as pltpu
from jax.sharding import PartitionSpec as P

RMAX = 17
LANES = 128
SLOTS = LANES // RMAX
VMEM_LIMIT = 60 * 1024 * 1024
BF16, F32 = jnp.bfloat16, jnp.float32


def row_groups(rows):
    edge = -(-RMAX // SLOTS)
    head = [(g * SLOTS, SLOTS) for g in range(edge)]
    tail = [(rows - (edge - g) * SLOTS, SLOTS) for g in range(edge)]
    middle, start, stop = [], edge * SLOTS, rows - edge * SLOTS
    while start < stop:
        count = min(SLOTS, stop - start)
        middle.append((start, count))
        start += count
    return head + middle + tail, edge


def taps_at(radius, offsets, total):
    spread = 0.5 * radius
    inside = jnp.abs(offsets) <= radius
    raw = jnp.where(inside, jnp.exp(-(offsets * offsets) / (2.0 * spread * spread)), 0.0)
    return raw if total is None else raw / total


def prepare_kernel(rows, sides, x_ref, dec_ref, ra_ref, *edge_refs):
    cols = x_ref.shape[2]
    dec = lax.axis_index("dec")
    line = lax.broadcasted_iota(jnp.int32, (8, LANES), 1) - RMAX
    z = lax.broadcasted_iota(jnp.int32, (2 * LANES, cols), 0)
    y = lax.broadcasted_iota(jnp.int32, (2 * LANES, cols), 1)
    before, after = z - LANES - RMAX, z - 2 * LANES - RMAX + LANES + cols
    if sides == 1:
        column = jnp.where(z < LANES, z, jnp.where(dec == 0, z - LANES + cols, before))
        used = z < LANES + RMAX
    else:
        column = jnp.where(z < LANES, z, jnp.where(z < LANES + RMAX, before, after))
        used = z < LANES + 2 * RMAX
    dec_offset = jnp.where(used, column - y, 2 * LANES).astype(F32)
    out = lax.broadcasted_iota(jnp.int32, ra_ref.shape[1:], 0)
    source = lax.broadcasted_iota(jnp.int32, ra_ref.shape[1:], 1)
    ra_offset = (source - out - RMAX).astype(F32)

    def one_radius(index, carry):
        radius = index.astype(F32)
        total = jnp.sum(taps_at(radius, line.astype(F32), None)) / 8.0
        dec_ref[index] = taps_at(radius, dec_offset, total).astype(BF16)
        ra_ref[index] = taps_at(radius, ra_offset, total).astype(BF16)
        return carry

    lax.fori_loop(1, RMAX + 1, one_radius, 0)
    lane = lax.broadcasted_iota(jnp.int32, x_ref.shape[1:], 1)
    groups, _ = row_groups(rows)
    for side, edge_ref in enumerate(edge_refs):
        if sides == 1:
            first = jnp.where(dec == 0, cols - RMAX, 0)
        else:
            first = cols - RMAX if side == 0 else 0
        for g, (start, count) in enumerate(groups):
            packed = jnp.zeros(x_ref.shape[1:], F32)
            for j in range(count):
                shift = lax.rem(RMAX * j - first + 2 * LANES, LANES)
                piece = pltpu.roll(x_ref[start + j].astype(F32), shift, 1)
                packed = piece if j == 0 else jnp.where(lane < RMAX * j, packed, piece)
            edge_ref[g] = packed.astype(BF16)


def prepare(x, sides):
    rows, chans, cols = x.shape
    count = len(row_groups(rows)[0])
    out_rows = -(-rows // 16) * 16
    shapes = [
        jax.ShapeDtypeStruct((RMAX + 1, 2 * LANES, cols), BF16),
        jax.ShapeDtypeStruct((RMAX + 1, out_rows, rows + 2 * RMAX), BF16),
    ] + [jax.ShapeDtypeStruct((count, chans, LANES), BF16)] * sides
    return pl.pallas_call(
        functools.partial(prepare_kernel, rows, sides),
        out_shape=shapes,
        in_specs=[pl.BlockSpec(memory_space=pltpu.VMEM)],
        out_specs=[pl.BlockSpec(memory_space=pltpu.VMEM)] * len(shapes),
        compiler_params=pltpu.CompilerParams(vmem_limit_bytes=VMEM_LIMIT),
        cost_estimate=pl.CostEstimate(flops=10**7, bytes_accessed=6 * 10**6, transcendentals=10**6),
    )(x)


def smooth_kernel(sides, rad_ref, x_ref, before_ref, after_ref, dec_ref, ra_ref, *refs):
    edge_refs, out_ref, own, halo, result = refs[:3 * sides], *refs[3 * sides:]
    rows, chans, _ = x_ref.shape
    frame = rows + 2 * RMAX

    def put(row, value):
        own[pl.ds(row * chans, chans), :] = value.astype(F32)

    def copy_rows(ref, base, count):
        def body(i, carry):
            put(base + i, ref[i])
            return carry

        lax.fori_loop(0, count, body, 0)

    copy_rows(before_ref, 0, RMAX)
    copy_rows(x_ref, RMAX, rows)
    copy_rows(after_ref, RMAX + rows, RMAX)

    lane = lax.broadcasted_iota(jnp.int32, (chans, LANES), 1)
    groups, edge = row_groups(rows)

    def unpack(row, part, g, j):
        value = None
        for side in range(sides):
            tile = edge_refs[3 * side + part][g].astype(F32)
            shift = (RMAX * side - RMAX * j) % LANES
            tile = tile if shift == 0 else pltpu.roll(tile, shift, 1)
            value = tile if side == 0 else jnp.where(lane < RMAX, value, tile)
        halo[pl.ds(row * chans, chans), :] = value

    for g, (start, count) in enumerate(groups):
        for j in range(count):
            unpack(RMAX + start + j, 0, g, j)
    for g, (start, count) in enumerate(groups[-edge:]):
        for j in range(count):
            if start + j >= rows - RMAX:
                unpack(start + j - (rows - RMAX), 1, g, j)
    for g, (start, count) in enumerate(groups[:edge]):
        for j in range(count):
            if start + j < RMAX:
                unpack(RMAX + rows + start + j, 2, g, j)

    def one_channel(c, carry):
        radius = rad_ref[c]
        picked = pl.ds(c, frame, stride=chans)
        lhs = jnp.concatenate([own[picked, :].astype(BF16), halo[picked, :].astype(BF16)], axis=1)
        partial = jnp.dot(lhs, dec_ref[radius], preferred_element_type=F32).astype(BF16)
        smoothed = jnp.dot(ra_ref[radius], partial, preferred_element_type=F32)
        result[pl.ds(c, rows, stride=chans), :] = smoothed[:rows]
        return carry

    lax.fori_loop(0, chans, one_channel, 0, unroll=8)

    def store(i, carry):
        out_ref[i] = result[pl.ds(i * chans, chans), :].astype(BF16)
        return carry

    lax.fori_loop(0, rows, store, 0)


def smooth(radii, x, before, after, dec_table, ra_table, edges):
    rows, chans, cols = x.shape
    frame = rows + 2 * RMAX
    operands = [x, before, after, dec_table, ra_table] + [part for side in edges for part in side]
    return pl.pallas_call(
        functools.partial(smooth_kernel, len(edges)),
        out_shape=jax.ShapeDtypeStruct(x.shape, BF16),
        in_specs=[pl.BlockSpec(memory_space=pltpu.SMEM)] + [pl.BlockSpec(memory_space=pltpu.VMEM)] * len(operands),
        out_specs=pl.BlockSpec(memory_space=pltpu.VMEM),
        scratch_shapes=[
            pltpu.VMEM((frame * chans, cols), F32),
            pltpu.VMEM((frame * chans, LANES), F32),
            pltpu.VMEM((rows * chans, cols), F32),
        ],
        compiler_params=pltpu.CompilerParams(vmem_limit_bytes=VMEM_LIMIT),
        cost_estimate=pl.CostEstimate(flops=4 * 10**9, bytes_accessed=10**7, transcendentals=0),
    )(radii, *operands)


ROWS_OF_SUMS = 8


def gram_kernel(own_ref, other_ref, valid_ref, out_ref):
    rows, chans, cols = own_ref.shape
    band = lax.axis_index("band")
    weights = valid_ref[...].astype(F32)

    def nt(a, b):
        return lax.dot_general(a, b, (((1,), (1,)), ((), ())), preferred_element_type=F32)

    def body(i, carry):
        own_gram, other_gram, own_sum, other_sum = carry
        w = valid_ref[pl.ds(i, 1), :].astype(BF16)
        wide = jnp.broadcast_to(w, (ROWS_OF_SUMS, cols))
        own, other = own_ref[i], other_ref[i]
        masked = own * w
        return (
            own_gram + nt(own, masked),
            other_gram + nt(other, masked),
            own_sum + nt(wide, own),
            other_sum + nt(wide, other),
        )

    square = jnp.zeros((chans, chans), F32)
    line = jnp.zeros((ROWS_OF_SUMS, chans), F32)
    own_gram, other_gram, own_sum, other_sum = lax.fori_loop(0, rows, body, (square, square, line, line))
    out_ref[pl.ds(pl.multiple_of(band * chans, chans), chans), :] = own_gram
    out_ref[pl.ds(pl.multiple_of((1 - band) * chans, chans), chans), :] = other_gram
    row = lax.broadcasted_iota(jnp.int32, (ROWS_OF_SUMS, chans), 0)
    sums = jnp.where(row == band, own_sum, other_sum)
    out_ref[2 * chans:, :] = jnp.where(row == 2, jnp.sum(weights), sums)


def gram(own, other, valid):
    chans = own.shape[1]
    return pl.pallas_call(
        gram_kernel,
        out_shape=jax.ShapeDtypeStruct((2 * chans + ROWS_OF_SUMS, chans), F32),
        in_specs=[pl.BlockSpec(memory_space=pltpu.VMEM)] * 3,
        out_specs=pl.BlockSpec(memory_space=pltpu.VMEM),
        compiler_params=pltpu.CompilerParams(vmem_limit_bytes=VMEM_LIMIT),
    )(own, other, valid)


def finish_kernel(mine_ref, theirs_ref, mean_ref, cov_ref):
    chans = mine_ref.shape[1]
    band = lax.axis_index("band")
    block = mine_ref[:2 * chans, :] + theirs_ref[:2 * chans, :]
    tail = mine_ref[2 * chans:, :] + theirs_ref[2 * chans:, :]
    count = tail[2:3, 0:1]
    means = tail / count
    own = jnp.where(band == 0, means[0:1, :], means[1:2, :])
    mean_ref[...] = own
    for b in range(2):
        column = jnp.transpose(jnp.broadcast_to(means[b:b + 1, :], (chans, chans)))
        part = block[b * chans:(b + 1) * chans]
        cov_ref[b * chans:(b + 1) * chans, :] = (part - count * column * own) / (count - 1.0)


def finish(mine, theirs):
    chans = mine.shape[1]
    mean, covariance = pl.pallas_call(
        finish_kernel,
        out_shape=[jax.ShapeDtypeStruct((1, chans), F32), jax.ShapeDtypeStruct((2 * chans, chans), F32)],
        in_specs=[pl.BlockSpec(memory_space=pltpu.VMEM)] * 2,
        out_specs=[pl.BlockSpec(memory_space=pltpu.VMEM)] * 2,
        compiler_params=pltpu.CompilerParams(vmem_limit_bytes=VMEM_LIMIT),
    )(mine, theirs)
    return mean.reshape(chans), covariance


def swap(array, axis, step):
    size = lax.axis_size(axis)
    return lax.ppermute(array, axis, [(i, i ^ step) for i in range(size)])


def per_device(sky_maps, radii, valid):
    x = jnp.transpose(sky_maps, (1, 0, 2))
    rows = x.shape[0]
    ra_size, dec_size = lax.axis_size("ra"), lax.axis_size("dec")
    up = [(i, (i + 1) % ra_size) for i in range(ra_size)]
    down = [(j, i) for i, j in up]
    before = lax.ppermute(x[rows - RMAX:], "ra", up)
    after = lax.ppermute(x[:RMAX], "ra", down)

    sides = 1 if dec_size == 2 else 2
    dec_table, ra_table, *packed = prepare(x, sides)
    if sides == 1:
        halos = [swap(packed[0], "dec", 1)]
    else:
        right = [(i, i + 1) for i in range(dec_size - 1)]
        left = [(j, i) for i, j in right]
        halos = [lax.ppermute(p, "dec", perm) for p, perm in zip(packed, (right, left))]
    edge = row_groups(rows)[1]
    edges = [(h, lax.ppermute(h[-edge:], "ra", up), lax.ppermute(h[:edge], "ra", down)) for h in halos]

    smoothed = smooth(radii, x, before, after, dec_table, ra_table, edges)
    total = gram(smoothed, swap(smoothed, "band", 1), valid)
    steps = [("dec", 1 << b) for b in range(dec_size.bit_length() - 1)]
    steps += [("ra", 1 << b) for b in range(ra_size.bit_length() - 1)]
    for axis, step in steps[:-1]:
        total = total + swap(total, axis, step)
    mean, covariance = finish(total, swap(total, *steps[-1]))
    return (jnp.transpose(smoothed, (1, 0, 2)), mean, covariance)


def solution(mesh):
    return jax.shard_map(
        per_device,
        mesh=mesh,
        in_specs=(
            P(("groups", "band"), "ra", "dec"),
            P(("groups", "band")),
            P(("groups", "ra"), "dec"),
        ),
        out_specs=(P(("groups", "band"), "ra", "dec"), P(("groups", "band")), P("groups", "band")),
        check_vma=False,
    )
```

```python
import functools

import jax
import jax.numpy as jnp
from jax import lax
from jax.experimental import pallas as pl
from jax.experimental.pallas import tpu as pltpu
from jax.sharding import PartitionSpec as P

RMAX = 17
LANES = 128
SLOTS = LANES // RMAX
EDGE = -(-RMAX // SLOTS)
PAD = 8
BATCH = 16
CHUNKS = 1
VMEM_LIMIT = 60 * 1024 * 1024
BF16, F32 = jnp.bfloat16, jnp.float32
VMEM = pl.BlockSpec(memory_space=pltpu.VMEM)
SMEM = pl.BlockSpec(memory_space=pltpu.SMEM)
PARAMS = pltpu.CompilerParams(vmem_limit_bytes=VMEM_LIMIT)


def row_groups(rows):
    head = [(g * SLOTS, SLOTS) for g in range(EDGE)]
    tail = [(rows - (EDGE - g) * SLOTS, SLOTS) for g in range(EDGE)]
    middle, start, stop = [], EDGE * SLOTS, rows - EDGE * SLOTS
    while start < stop:
        count = min(SLOTS, stop - start)
        middle.append((start, count))
        start += count
    return head + middle + tail


def taps_at(radius, offsets, total):
    spread = 0.5 * radius
    inside = jnp.abs(offsets) <= radius
    raw = jnp.where(inside, jnp.exp(-(offsets * offsets) / (2.0 * spread * spread)), 0.0)
    return raw if total is None else raw / total


def tables_kernel(sides, dec_ref, ra_ref):
    cols = dec_ref.shape[2]
    dec = lax.axis_index("dec")
    line = lax.broadcasted_iota(jnp.int32, (8, LANES), 1) - RMAX
    z = lax.broadcasted_iota(jnp.int32, dec_ref.shape[1:], 0)
    y = lax.broadcasted_iota(jnp.int32, dec_ref.shape[1:], 1)
    before, after = z - cols - RMAX, z
    if sides == 1:
        column = jnp.where(z < cols, z, jnp.where(dec == 0, after, before))
    else:
        column = jnp.where(z < cols, z, jnp.where(z < cols + RMAX, before, after - RMAX))
    used = z < cols + sides * RMAX
    dec_offset = jnp.where(used, column - y, 2 * LANES).astype(F32)
    out = lax.broadcasted_iota(jnp.int32, ra_ref.shape[1:], 0)
    source = lax.broadcasted_iota(jnp.int32, ra_ref.shape[1:], 1)
    ra_offset = (source - out - RMAX).astype(F32)

    def one_radius(index, carry):
        radius = index.astype(F32)
        total = jnp.sum(taps_at(radius, line.astype(F32), None)) / 8.0
        dec_ref[index] = taps_at(radius, dec_offset, total).astype(BF16)
        ra_ref[index] = taps_at(radius, ra_offset, total).astype(BF16)
        return carry

    lax.fori_loop(1, RMAX + 1, one_radius, 0)


def tables(rows, cols, sides):
    out_rows = -(-rows // 16) * 16
    return pl.pallas_call(
        functools.partial(tables_kernel, sides),
        out_shape=[
            jax.ShapeDtypeStruct((RMAX + 1, cols + LANES, cols), BF16),
            jax.ShapeDtypeStruct((RMAX + 1, out_rows, rows + 2 * RMAX), BF16),
        ],
        out_specs=[VMEM, VMEM],
        compiler_params=PARAMS,
        cost_estimate=pl.CostEstimate(flops=10**7, bytes_accessed=2 * 10**6, transcendentals=10**6),
    )()


def pack_kernel(sides, x_ref, *edge_refs):
    rows, chans, cols = x_ref.shape
    dec = lax.axis_index("dec")
    lane = lax.broadcasted_iota(jnp.int32, (chans, LANES), 1)
    for side, edge_ref in enumerate(edge_refs):
        if sides == 1:
            first = jnp.where(dec == 0, cols - RMAX, 0)
        else:
            first = cols - RMAX if side == 0 else 0
        for g, (start, count) in enumerate(row_groups(rows)):
            for j in range(count):
                shift = lax.rem(RMAX * j - first + 2 * LANES, LANES)
                piece = pltpu.roll(x_ref[start + j].astype(F32), shift, 1)
                packed = piece if j == 0 else jnp.where(lane < RMAX * j, packed, piece)
            edge_ref[g] = packed.astype(BF16)


def pack(x, sides):
    rows, chans, _ = x.shape
    shape = jax.ShapeDtypeStruct((len(row_groups(rows)), chans, LANES), BF16)
    return pl.pallas_call(
        functools.partial(pack_kernel, sides),
        out_shape=[shape] * sides,
        in_specs=[VMEM],
        out_specs=[VMEM] * sides,
        compiler_params=PARAMS,
        cost_estimate=pl.CostEstimate(flops=10**6, bytes_accessed=3 * 10**6, transcendentals=0),
    )(x)


def smooth_kernel(sides, first, rad_ref, x_ref, before_ref, after_ref, dec_ref, ra_ref, *refs):
    edge_refs, (out_ref, own, halo, result) = refs[:3 * sides], refs[3 * sides:]
    rows, chans, _ = x_ref.shape
    frame = rows + 2 * RMAX
    pitch = chans + PAD

    def copy_rows(ref, base, count):
        def body(i, carry):
            own[pl.ds((base + i) * pitch, chans), :] = ref[i].astype(F32)
            return carry

        lax.fori_loop(0, count, body, 0)

    copy_rows(before_ref, 0, RMAX)
    copy_rows(x_ref, RMAX, rows)
    copy_rows(after_ref, RMAX + rows, RMAX)

    lane = lax.broadcasted_iota(jnp.int32, (chans, LANES), 1)
    groups = row_groups(rows)

    def unpack(row, part, g, j):
        for side in range(sides):
            tile = edge_refs[3 * side + part][g].astype(F32)
            shift = (RMAX * side - RMAX * j) % LANES
            tile = tile if shift == 0 else pltpu.roll(tile, shift, 1)
            value = tile if side == 0 else jnp.where(lane < RMAX, value, tile)
        halo[pl.ds(row * pitch, chans), :] = value

    for g, (start, count) in enumerate(groups):
        for j in range(count):
            unpack(RMAX + start + j, 0, g, j)
    for g, (start, count) in enumerate(groups[-EDGE:]):
        for j in range(count):
            if start + j >= rows - RMAX:
                unpack(start + j - (rows - RMAX), 1, g, j)
    for g, (start, count) in enumerate(groups[:EDGE]):
        for j in range(count):
            if start + j < RMAX:
                unpack(RMAX + rows + start + j, 2, g, j)

    def some_channels(i, carry):
        chosen = [i * BATCH + j for j in range(BATCH)]
        radii = [rad_ref[first + c] for c in chosen]
        partials = []
        for c, radius in zip(chosen, radii):
            picked = pl.ds(c, frame, stride=pitch)
            lhs = jnp.concatenate([own[picked, :].astype(BF16), halo[picked, :].astype(BF16)], axis=1)
            partials.append(jnp.dot(lhs, dec_ref[radius], preferred_element_type=F32).astype(BF16))
        for c, radius, partial in zip(chosen, radii, partials):
            smoothed = jnp.dot(ra_ref[radius], partial, preferred_element_type=F32)
            result[pl.ds(c, rows, stride=pitch), :] = smoothed[:rows]
        return carry

    lax.fori_loop(0, chans // BATCH, some_channels, 0)

    def store(i, carry):
        out_ref[i] = result[pl.ds(i * pitch, chans), :].astype(BF16)
        return carry

    lax.fori_loop(0, rows, store, 0)


def smooth(radii, x, chunk, before, after, dec_table, ra_table, edges):
    rows, _, cols = x.shape
    chans = before.shape[1]
    pitch, frame = chans + PAD, rows + 2 * RMAX
    operands = [x, before, after, dec_table, ra_table] + [part for side in edges for part in side]

    def ranged(array):
        if array.shape[1] == chans or array is dec_table or array is ra_table:
            return pl.BlockSpec(array.shape, lambda i: (0, 0, 0))
        return pl.BlockSpec((array.shape[0], chans, array.shape[2]), lambda i: (0, chunk, 0))

    return pl.pallas_call(
        functools.partial(smooth_kernel, len(edges), chunk * chans),
        out_shape=jax.ShapeDtypeStruct((rows, chans, cols), BF16),
        grid=(1,),
        in_specs=[SMEM] + [ranged(a) for a in operands],
        out_specs=pl.BlockSpec((rows, chans, cols), lambda i: (0, 0, 0)),
        scratch_shapes=[
            pltpu.VMEM((frame * pitch, cols), F32),
            pltpu.VMEM((frame * pitch, LANES), F32),
            pltpu.VMEM((rows * pitch, cols), F32),
        ],
        compiler_params=PARAMS,
        cost_estimate=pl.CostEstimate(flops=4 * 10**9 // CHUNKS, bytes_accessed=10**7 // CHUNKS, transcendentals=0),
    )(radii, *operands)


SUM_ROWS = 8


def gram_kernel(parts, *refs):
    own_refs, other_refs, (valid_ref, out_ref, smoothed_ref, total, sems) = refs[:parts], refs[parts:2 * parts], refs[2 * parts:]
    rows, part, cols = own_refs[0].shape
    chans = parts * part
    band = lax.axis_index("band")
    copies = [
        pltpu.make_async_copy(ref, smoothed_ref.at[:, pl.ds(i * part, part), :], sems.at[i])
        for i, ref in enumerate(own_refs)
    ]
    for copy in copies:
        copy.start()
    depth = max(d for d in range(1, 27) if rows % d == 0)

    def nt(a, b):
        return lax.dot_general(a, b, (((1,), (1,)), ((), ())), preferred_element_type=F32)

    def body(i, carry):
        picked = [i * depth + j for j in range(depth)]
        weights = [valid_ref[pl.ds(r, 1), :].astype(BF16) for r in picked]

        def wide(refs):
            return jnp.concatenate([jnp.concatenate([ref[r] for ref in refs], 0) for r in picked], 1)

        own, other = wide(own_refs), wide(other_refs)
        line = jnp.concatenate(weights, 1)
        both = jnp.concatenate([own, other], 0)
        total[:2 * chans, :] += nt(both, own * line)
        sums = nt(jnp.broadcast_to(line, (16, line.shape[1])), both)[:SUM_ROWS]
        total[2 * chans:2 * chans + SUM_ROWS, :] += sums[:, :chans]
        total[2 * chans + SUM_ROWS:, :] += sums[:, chans:]
        return carry

    total[...] = jnp.zeros_like(total)
    lax.fori_loop(0, rows // depth, body, 0)
    out_ref[pl.ds(pl.multiple_of(band * chans, chans), chans), :] = total[:chans, :]
    out_ref[pl.ds(pl.multiple_of((1 - band) * chans, chans), chans), :] = total[chans:2 * chans, :]
    row = lax.broadcasted_iota(jnp.int32, (SUM_ROWS, chans), 0)
    own_sum, other_sum = total[2 * chans:2 * chans + SUM_ROWS, :], total[2 * chans + SUM_ROWS:, :]
    sums = jnp.where(row == band, own_sum, other_sum)
    out_ref[2 * chans:, :] = jnp.where(row == 2, jnp.sum(valid_ref[...].astype(F32)), sums)
    for copy in copies:
        copy.wait()


def gram(own, other, valid):
    rows, part, cols = own[0].shape
    parts = len(own)
    chans = parts * part
    return pl.pallas_call(
        functools.partial(gram_kernel, parts),
        out_shape=[
            jax.ShapeDtypeStruct((2 * chans + SUM_ROWS, chans), F32),
            jax.ShapeDtypeStruct((rows, chans, cols), BF16),
        ],
        in_specs=[VMEM] * (2 * parts + 1),
        out_specs=[VMEM, pl.BlockSpec(memory_space=pl.ANY)],
        scratch_shapes=[pltpu.VMEM((2 * chans + 2 * SUM_ROWS, chans), F32), pltpu.SemaphoreType.DMA((parts,))],
        compiler_params=PARAMS,
    )(*own, *other, valid)


def finish_kernel(mine_ref, theirs_ref, mean_ref, cov_ref):
    chans = mine_ref.shape[1]
    band = lax.axis_index("band")
    block = mine_ref[:2 * chans, :] + theirs_ref[:2 * chans, :]
    tail = mine_ref[2 * chans:, :] + theirs_ref[2 * chans:, :]
    count = tail[2:3, 0:1]
    means = tail / count
    own = jnp.where(band == 0, means[0:1, :], means[1:2, :])
    mean_ref[...] = own
    for b in range(2):
        column = jnp.transpose(jnp.broadcast_to(means[b:b + 1, :], (chans, chans)))
        part = block[b * chans:(b + 1) * chans]
        cov_ref[b * chans:(b + 1) * chans, :] = (part - count * column * own) / (count - 1.0)


def finish(mine, theirs):
    chans = mine.shape[1]
    mean, covariance = pl.pallas_call(
        finish_kernel,
        out_shape=[jax.ShapeDtypeStruct((1, chans), F32), jax.ShapeDtypeStruct((2 * chans, chans), F32)],
        in_specs=[VMEM] * 2,
        out_specs=[VMEM] * 2,
        compiler_params=PARAMS,
    )(mine, theirs)
    return mean.reshape(chans), covariance


def swap(array, axis, step):
    size = lax.axis_size(axis)
    return lax.ppermute(array, axis, [(i, i ^ step) for i in range(size)])


def diagonal(array, ra_step, dec_pairs):
    ra_size, dec_size = lax.axis_size("ra"), lax.axis_size("dec")
    pairs = [
        (i * dec_size + a, (i + ra_step) % ra_size * dec_size + b) for i in range(ra_size) for a, b in dec_pairs
    ]
    return lax.ppermute(array, ("ra", "dec"), pairs)


def per_device(sky_maps, radii, valid):
    x = jnp.transpose(sky_maps, (1, 0, 2))
    rows, chans, cols = x.shape
    ra_size, dec_size = lax.axis_size("ra"), lax.axis_size("dec")
    up = [(i, (i + 1) % ra_size) for i in range(ra_size)]
    down = [(j, i) for i, j in up]
    part = chans // CHUNKS
    ranges = [slice(i * part, (i + 1) * part) for i in range(CHUNKS)]
    frames = [
        (lax.ppermute(x[rows - RMAX:, r], "ra", up), lax.ppermute(x[:RMAX, r], "ra", down)) for r in ranges
    ]
    right = [(i, i + 1) for i in range(dec_size - 1)]
    left = [(j, i) for i, j in right]
    sides = [right + left] if dec_size == 2 else [right, left]
    edges = [
        (lax.ppermute(p, "dec", pairs), diagonal(p[-EDGE:], 1, pairs), diagonal(p[:EDGE], -1, pairs))
        for p, pairs in zip(pack(x, len(sides)), sides)
    ]
    dec_table, ra_table = tables(rows, cols, len(sides))

    own = [smooth(radii, x, i, *frame, dec_table, ra_table, edges) for i, frame in enumerate(frames)]
    other = [swap(a, "band", 1) for a in own]
    total, smoothed = gram(own, other, valid)
    steps = [("dec", 1 << b) for b in range(dec_size.bit_length() - 1)]
    steps += [("ra", 1 << b) for b in range(ra_size.bit_length() - 1)]
    for axis, step in steps[:-1]:
        total = total + swap(total, axis, step)
    mean, covariance = finish(total, swap(total, *steps[-1]))
    return (jnp.transpose(smoothed, (1, 0, 2)), mean, covariance)


def solution(mesh):
    return jax.shard_map(
        per_device,
        mesh=mesh,
        in_specs=(
            P(("groups", "band"), "ra", "dec"),
            P(("groups", "band")),
            P(("groups", "ra"), "dec"),
        ),
        out_specs=(P(("groups", "band"), "ra", "dec"), P(("groups", "band")), P("groups", "band")),
        check_vma=False,
    )
```

```python
import functools

import jax
import jax.numpy as jnp
from jax import lax
from jax.experimental import pallas as pl
from jax.experimental.pallas import tpu as pltpu
from jax.sharding import PartitionSpec as P

RMAX = 17
LANES = 128
SLOTS = LANES // RMAX
EDGE = -(-RMAX // SLOTS)
PAD = 8
HALO = 24
BATCH = 16
VMEM_LIMIT = 32 * 1024 * 1024
BF16, F32 = jnp.bfloat16, jnp.float32
VMEM = pl.BlockSpec(memory_space=pltpu.VMEM)
SMEM = pl.BlockSpec(memory_space=pltpu.SMEM)
PARAMS = pltpu.CompilerParams(vmem_limit_bytes=VMEM_LIMIT)


def row_groups(rows):
    head = [(g * SLOTS, SLOTS) for g in range(EDGE)]
    tail = [(rows - (EDGE - g) * SLOTS, SLOTS) for g in range(EDGE)]
    middle, start, stop = [], EDGE * SLOTS, rows - EDGE * SLOTS
    while start < stop:
        count = min(SLOTS, stop - start)
        middle.append((start, count))
        start += count
    return head + middle + tail


def tables_kernel(sides, rows, dec_ref, inner_ref, outer_ref, *offset_refs):
    cols = dec_ref.shape[2]
    dec = lax.axis_index("dec")

    def offsets(offset_ref, used, offset):
        offset_ref[...] = jnp.where(used, offset, 2 * LANES).astype(F32)

    def grid(ref):
        return [lax.broadcasted_iota(jnp.int32, ref.shape, d) for d in (0, 1)]

    z, y = grid(offset_refs[0])
    before, after = z - cols - RMAX, z
    if sides == 1:
        column = jnp.where(z < cols, z, jnp.where(dec == 0, after, before))
    else:
        column = jnp.where(z < cols, z, jnp.where(z < cols + RMAX, before, after - RMAX))
    offsets(offset_refs[0], z < cols + sides * RMAX, column - y)
    out, source = grid(offset_refs[1])
    offsets(offset_refs[1], source < rows, source - out - RMAX)
    out, source = grid(offset_refs[2])
    own = outer_ref.shape[2] - 2 * HALO
    head, tail = source - own, source - own - HALO
    row = jnp.where(source < own, source, jnp.where(head < HALO, head - RMAX, tail + rows))
    used = (source < rows) | ((head >= 0) & (head < RMAX)) | ((tail >= 0) & (tail < RMAX))
    offsets(offset_refs[2], used, row - jnp.where(out < HALO, out, out - HALO + rows - RMAX))
    line = (lax.broadcasted_iota(jnp.int32, (8, LANES), 1) - RMAX).astype(F32)

    def one_radius(index, carry):
        radius = jnp.full((8, LANES), index, jnp.int32).astype(F32)
        spread = 0.5 * radius
        scale = -1.0 / (2.0 * spread * spread)
        raw = jnp.where(jnp.abs(line) <= radius, jnp.exp(line * line * scale), 0.0)
        inverse = 1.0 / jnp.sum(raw, axis=1, keepdims=True)
        limit, scale, inverse = radius[:1, :1], scale[:1, :1], inverse[:1]
        for ref, offset_ref in zip((dec_ref, inner_ref, outer_ref), offset_refs):
            offset = offset_ref[...]
            taps = jnp.where(jnp.abs(offset) <= limit, jnp.exp(offset * offset * scale) * inverse, 0.0)
            ref[index] = taps.astype(BF16)
        return carry

    lax.fori_loop(1, RMAX + 1, one_radius, 0)


def tables(rows, cols, sides):
    own = -(-rows // 16) * 16
    shapes = [(cols + LANES, cols), (-(-(rows - 2 * RMAX) // 16) * 16, own), (2 * HALO, own + 2 * HALO)]
    return pl.pallas_call(
        functools.partial(tables_kernel, sides, rows),
        out_shape=[pltpu.VMEM((RMAX + 1, *shape), BF16) for shape in shapes],
        out_specs=[VMEM] * 3,
        scratch_shapes=[pltpu.VMEM(shape, F32) for shape in shapes],
        compiler_params=PARAMS,
        cost_estimate=pl.CostEstimate(flops=10**5, bytes_accessed=10**5, transcendentals=0),
    )()


def edges_kernel(sides, rad_ref, source_ref, x_ref, *refs):
    (up_ref, up_rest_ref, down_ref, down_rest_ref), refs = refs[:4], refs[4:]
    edge_refs, (low_wide, high_wide, low_packed, high_packed, sems) = refs[:sides], refs[sides:]
    rows, chans, cols = x_ref.shape
    pitch = chans + PAD
    cap, full = up_ref.shape[0], RMAX * chans
    spans = ((0, RMAX), (rows - RMAX, RMAX), (RMAX, rows - 2 * RMAX))
    copies = [
        pltpu.make_async_copy(source_ref.at[pl.ds(start, n)], x_ref.at[pl.ds(start, n)], sems.at[i])
        for i, (start, n) in enumerate(spans)
    ]
    for copy in copies:
        copy.start()
    low_packed[...] = jnp.zeros_like(low_packed)
    high_packed[...] = jnp.zeros_like(high_packed)
    for copy in copies[:2]:
        copy.wait()
    for i in range(RMAX):
        low_wide[pl.ds(i * pitch, chans), :] = x_ref[i].astype(F32)
        high_wide[pl.ds(i * pitch, chans), :] = x_ref[rows - RMAX + i].astype(F32)

    def upward(c, offset):
        low_packed[pl.ds(HALO + offset, RMAX), :] = low_wide[pl.ds(c, RMAX, stride=pitch), :]
        return offset + rad_ref[c]

    total = lax.fori_loop(0, chans, upward, 0, unroll=8)

    def downward(i, stop):
        c = chans - 1 - i
        high_packed[pl.ds(HALO + stop - RMAX, RMAX), :] = high_wide[pl.ds(c, RMAX, stride=pitch), :]
        return stop - rad_ref[c]

    lax.fori_loop(0, chans, downward, total, unroll=8)
    for packed, ref, rest_ref in ((low_packed, down_ref, down_rest_ref), (high_packed, up_ref, up_rest_ref)):
        ref[...] = packed[HALO:HALO + cap, :].astype(BF16)
        rest_ref[...] = packed[HALO + cap:HALO + full, :].astype(BF16)

    copies[2].wait()
    dec = lax.axis_index("dec")
    lane = lax.broadcasted_iota(jnp.int32, (chans, LANES), 1)
    for side, edge_ref in enumerate(edge_refs):
        if sides == 1:
            first = jnp.where(dec == 0, cols - RMAX, 0)
        else:
            first = cols - RMAX if side == 0 else 0
        for g, (start, count) in enumerate(row_groups(rows)):
            for j in range(count):
                shift = lax.rem(RMAX * j - first + 2 * LANES, LANES)
                piece = pltpu.roll(x_ref[start + j].astype(F32), shift, 1)
                packed = piece if j == 0 else jnp.where(lane < RMAX * j, packed, piece)
            edge_ref[g] = packed.astype(BF16)


def cap_of(chans):
    return RMAX * chans * 5 // 8 // 16 * 16


def edges_of(radii, x, sides):
    rows, chans, cols = x.shape
    full, cap = RMAX * chans, cap_of(chans)
    head, rest = (pltpu.VMEM((n, cols), BF16) for n in (cap, full - cap))
    packed = pltpu.VMEM((len(row_groups(rows)), chans, LANES), BF16)
    return pl.pallas_call(
        functools.partial(edges_kernel, sides),
        out_shape=[pltpu.VMEM(x.shape, BF16), head, rest, head, rest] + [packed] * sides,
        in_specs=[SMEM, pl.BlockSpec(memory_space=pl.ANY)],
        out_specs=[VMEM] * (5 + sides),
        scratch_shapes=[pltpu.VMEM((RMAX * (chans + PAD), cols), F32)] * 2
        + [pltpu.VMEM((full + 2 * HALO, cols), F32)] * 2
        + [pltpu.SemaphoreType.DMA((3,))],
        compiler_params=PARAMS,
        cost_estimate=pl.CostEstimate(flops=10**6, bytes_accessed=5 * 10**6, transcendentals=0),
    )(radii, x)


def widen(tile, j, side_tiles):
    lane = lax.broadcasted_iota(jnp.int32, tile.shape, 1)
    value = None
    for side, part in enumerate(side_tiles):
        shift = (RMAX * side - RMAX * j) % LANES
        part = part if shift == 0 else pltpu.roll(part, shift, 1)
        value = part if side == 0 else jnp.where(lane < RMAX, value, part)
    return value


def inner_kernel(sides, rad_ref, x_ref, dec_ref, ra_ref, *refs):
    edge_refs, (partial_ref, out_ref, own, halo, result) = refs[:sides], refs[sides:]
    rows, chans, cols = x_ref.shape
    pitch = chans + PAD
    own_rows, inner = partial_ref.shape[1], rows - 2 * RMAX

    def copy_row(i, carry):
        own[pl.ds(i * pitch, chans), :] = x_ref[i].astype(F32)
        return carry

    lax.fori_loop(0, rows, copy_row, 0)
    for i in range(rows, own_rows):
        own[pl.ds(i * pitch, chans), :] = jnp.zeros((chans, cols), F32)
        halo[pl.ds(i * pitch, chans), :] = jnp.zeros((chans, cols), F32)
    for g, (start, count) in enumerate(row_groups(rows)):
        tiles = [ref[g].astype(F32) for ref in edge_refs]
        for j in range(count):
            halo[pl.ds((start + j) * pitch, chans), :] = widen(tiles[0], j, tiles)

    def some_channels(i, carry):
        chosen = [i * BATCH + j for j in range(BATCH)]
        radii = [rad_ref[c] for c in chosen]
        partials = []
        for c, radius in zip(chosen, radii):
            picked = pl.ds(c, own_rows, stride=pitch)
            lhs = jnp.concatenate([own[picked, :].astype(BF16), halo[picked, :].astype(BF16)], 1)
            partials.append(jnp.dot(lhs, dec_ref[radius], preferred_element_type=F32).astype(BF16))
        for c, radius, partial in zip(chosen, radii, partials):
            partial_ref[c] = partial
            smoothed = jnp.dot(ra_ref[radius], partial, preferred_element_type=F32)
            result[pl.ds(c, inner, stride=pitch), :] = smoothed[:inner]
        return carry

    lax.fori_loop(0, chans // BATCH, some_channels, 0)

    def store(i, carry):
        out_ref[i] = result[pl.ds(i * pitch, chans), :].astype(BF16)
        return carry

    lax.fori_loop(0, inner, store, 0)


def smooth_inner(radii, x, halos, dec_table, ra_table):
    rows, chans, cols = x.shape
    pitch, own_rows, inner = chans + PAD, ra_table.shape[2], rows - 2 * RMAX
    operands = [x, dec_table, ra_table, *halos]
    return pl.pallas_call(
        functools.partial(inner_kernel, len(halos)),
        out_shape=[
            pltpu.VMEM((chans, own_rows, cols), BF16),
            pltpu.VMEM((inner, chans, cols), BF16),
        ],
        in_specs=[SMEM] + [VMEM] * len(operands),
        out_specs=[VMEM] * 2,
        scratch_shapes=[
            pltpu.VMEM((own_rows * pitch, cols), F32),
            pltpu.VMEM((own_rows * pitch, LANES), F32),
            pltpu.VMEM((inner * pitch, cols), F32),
        ],
        compiler_params=PARAMS,
        cost_estimate=pl.CostEstimate(flops=4 * 10**9, bytes_accessed=10**7, transcendentals=0),
    )(radii, *operands)


def outer_kernel(sides, rows, rad_ref, partial_ref, *refs):
    before_refs, after_refs, (dec_ref, ra_ref), refs = refs[:2], refs[2:4], refs[4:6], refs[6:]
    corner_refs, (out_ref, halo, before, after, result) = refs[:2 * sides], refs[2 * sides:]
    chans, _, cols = partial_ref.shape
    pitch = chans + PAD

    for packed, parts in ((before, before_refs), (after, after_refs)):
        packed[:HALO, :] = jnp.zeros((HALO, cols), F32)
        packed[packed.shape[0] - HALO:, :] = jnp.zeros((HALO, cols), F32)
        start = HALO
        for part in parts:
            packed[start:start + part.shape[0], :] = part[...].astype(F32)
            start += part.shape[0]

    groups = row_groups(rows)
    for part, base in ((0, 0), (1, HALO)):
        for g, (start, count) in enumerate(groups[:EDGE] if part else groups[-EDGE:]):
            tiles = [corner_refs[2 * side + part][g].astype(F32) for side in range(sides)]
            for j in range(count):
                row = start + j if part else start + j - (rows - RMAX)
                if 0 <= row < RMAX:
                    halo[pl.ds((base + row) * pitch, chans), :] = widen(tiles[0], j, tiles)
        for row in range(RMAX, HALO):
            halo[pl.ds((base + row) * pitch, chans), :] = jnp.zeros((chans, LANES), F32)

    def some_channels(i, offset):
        chosen = [i * BATCH + j for j in range(BATCH)]
        radii = [rad_ref[c] for c in chosen]
        partials = []
        for c, radius in zip(chosen, radii):
            planes = [
                before[pl.ds(HALO - RMAX + offset + radius, HALO), :],
                after[pl.ds(HALO + offset, HALO), :],
            ]
            picked = pl.ds(c, 2 * HALO, stride=pitch)
            lhs = jnp.concatenate([jnp.concatenate(planes, 0).astype(BF16), halo[picked, :].astype(BF16)], 1)
            partials.append(jnp.dot(lhs, dec_ref[radius], preferred_element_type=F32).astype(BF16))
            offset = offset + radius
        for c, radius, partial in zip(chosen, radii, partials):
            smoothed = jnp.dot(
                ra_ref[radius], jnp.concatenate([partial_ref[c], partial], 0), preferred_element_type=F32
            )
            result[pl.ds(c, RMAX, stride=pitch), :] = smoothed[:RMAX]
            result[pl.ds(RMAX * pitch + c, RMAX, stride=pitch), :] = smoothed[HALO:HALO + RMAX]
        return offset

    lax.fori_loop(0, chans // BATCH, some_channels, 0)

    def store(i, carry):
        out_ref[i] = result[pl.ds(i * pitch, chans), :].astype(BF16)
        return carry

    lax.fori_loop(0, 2 * RMAX, store, 0)


def smooth_outer(radii, rows, partial, before, after, dec_table, ra_table, corners):
    chans, _, cols = partial.shape
    pitch = chans + PAD
    operands = [partial, *before, *after, dec_table, ra_table] + [part for side in corners for part in side]
    return pl.pallas_call(
        functools.partial(outer_kernel, len(corners), rows),
        out_shape=pltpu.VMEM((2 * RMAX, chans, cols), BF16),
        in_specs=[SMEM] + [VMEM] * len(operands),
        out_specs=VMEM,
        scratch_shapes=[
            pltpu.VMEM((2 * HALO * pitch, LANES), F32),
            pltpu.VMEM((RMAX * chans + 2 * HALO, cols), F32),
            pltpu.VMEM((RMAX * chans + 2 * HALO, cols), F32),
            pltpu.VMEM((2 * RMAX * pitch, cols), F32),
        ],
        compiler_params=PARAMS,
        cost_estimate=pl.CostEstimate(flops=2 * 10**9, bytes_accessed=5 * 10**6, transcendentals=0),
    )(radii, *operands)


SUM_ROWS = 8


def add_products(total, own_ref, other_ref, valid_ref, first_row, rows):
    chans = own_ref.shape[1]
    depth = max(d for d in range(1, 27) if rows % d == 0)

    def nt(a, b):
        return lax.dot_general(a, b, (((1,), (1,)), ((), ())), preferred_element_type=F32)

    def body(i, carry):
        picked = [i * depth + j for j in range(depth)]
        line = jnp.concatenate([valid_ref[pl.ds(first_row(r), 1), :].astype(BF16) for r in picked], 1)
        own, other = (jnp.concatenate([ref[r] for r in picked], 1) for ref in (own_ref, other_ref))
        both = jnp.concatenate([own, other], 0)
        total[:2 * chans, :] += nt(both, own * line)
        sums = nt(jnp.broadcast_to(line, (16, line.shape[1])), both)[:SUM_ROWS]
        total[2 * chans:2 * chans + SUM_ROWS, :] += sums[:, :chans]
        total[2 * chans + SUM_ROWS:, :] += sums[:, chans:]
        return carry

    lax.fori_loop(0, rows // depth, body, 0)


def inner_gram_kernel(own_ref, other_ref, valid_ref, total_ref):
    total_ref[...] = jnp.zeros_like(total_ref)
    add_products(total_ref, own_ref, other_ref, valid_ref, lambda r: r + RMAX, own_ref.shape[0])


def inner_gram(own, other, valid):
    chans = own.shape[1]
    return pl.pallas_call(
        inner_gram_kernel,
        out_shape=pltpu.VMEM((2 * chans + 2 * SUM_ROWS, chans), F32),
        in_specs=[VMEM] * 3,
        out_specs=VMEM,
        compiler_params=PARAMS,
        cost_estimate=pl.CostEstimate(flops=10**9, bytes_accessed=3 * 10**6, transcendentals=0),
    )(own, other, valid)


def gram_kernel(inner_ref, own_ref, other_ref, valid_ref, inner_own_ref, out_ref, smoothed_ref, total, sems):
    rows, chans = valid_ref.shape[0], own_ref.shape[1]
    band = lax.axis_index("band")
    copies = [
        pltpu.make_async_copy(source, smoothed_ref.at[pl.ds(start, source.shape[0])], sems.at[i])
        for i, (source, start) in enumerate((
            (inner_own_ref, RMAX),
            (own_ref.at[pl.ds(0, RMAX)], 0),
            (own_ref.at[pl.ds(RMAX, RMAX)], rows - RMAX),
        ))
    ]
    for copy in copies:
        copy.start()
    total[...] = inner_ref[...]
    add_products(
        total, own_ref, other_ref, valid_ref, lambda r: jnp.where(r < RMAX, r, r + rows - 2 * RMAX), 2 * RMAX
    )
    out_ref[pl.ds(pl.multiple_of(band * chans, chans), chans), :] = total[:chans, :]
    out_ref[pl.ds(pl.multiple_of((1 - band) * chans, chans), chans), :] = total[chans:2 * chans, :]
    row = lax.broadcasted_iota(jnp.int32, (SUM_ROWS, chans), 0)
    own_sum, other_sum = total[2 * chans:2 * chans + SUM_ROWS, :], total[2 * chans + SUM_ROWS:, :]
    sums = jnp.where(row == band, own_sum, other_sum)
    out_ref[2 * chans:, :] = jnp.where(row == 2, jnp.sum(valid_ref[...].astype(F32)), sums)
    for copy in copies:
        copy.wait()


def gram(inner, own, other, valid, inner_own):
    _, chans, cols = own.shape
    return pl.pallas_call(
        gram_kernel,
        out_shape=[
            pltpu.VMEM((2 * chans + SUM_ROWS, chans), F32),
            jax.ShapeDtypeStruct((valid.shape[0], chans, cols), BF16),
        ],
        in_specs=[VMEM] * 5,
        out_specs=[VMEM, pl.BlockSpec(memory_space=pl.ANY)],
        scratch_shapes=[pltpu.VMEM(inner.shape, F32), pltpu.SemaphoreType.DMA((3,))],
        compiler_params=PARAMS,
    )(inner, own, other, valid, inner_own)


def finish_kernel(mine_ref, theirs_ref, mean_ref, cov_ref):
    chans = mine_ref.shape[1]
    band = lax.axis_index("band")
    block = mine_ref[:2 * chans, :] + theirs_ref[:2 * chans, :]
    tail = mine_ref[2 * chans:, :] + theirs_ref[2 * chans:, :]
    count = tail[2:3, 0:1]
    means = tail / count
    own = jnp.where(band == 0, means[0:1, :], means[1:2, :])
    mean_ref[...] = own
    for b in range(2):
        column = jnp.transpose(jnp.broadcast_to(means[b:b + 1, :], (chans, chans)))
        part = block[b * chans:(b + 1) * chans]
        cov_ref[b * chans:(b + 1) * chans, :] = (part - count * column * own) / (count - 1.0)


def finish(mine, theirs):
    chans = mine.shape[1]
    mean, covariance = pl.pallas_call(
        finish_kernel,
        out_shape=[jax.ShapeDtypeStruct((1, chans), F32), jax.ShapeDtypeStruct((2 * chans, chans), F32)],
        in_specs=[VMEM] * 2,
        out_specs=[VMEM] * 2,
        compiler_params=PARAMS,
    )(mine, theirs)
    return mean.reshape(chans), covariance


def swap(array, axis, step):
    size = lax.axis_size(axis)
    return lax.ppermute(array, axis, [(i, i ^ step) for i in range(size)])


def diagonal(array, ra_step, dec_pairs):
    ra_size, dec_size = lax.axis_size("ra"), lax.axis_size("dec")
    pairs = [
        (i * dec_size + a, (i + ra_step) % ra_size * dec_size + b) for i in range(ra_size) for a, b in dec_pairs
    ]
    return lax.ppermute(array, ("ra", "dec"), pairs)


def per_device(sky_maps, radii, valid):
    x = jnp.transpose(sky_maps, (1, 0, 2))
    rows, chans, cols = x.shape
    ra_size, dec_size = lax.axis_size("ra"), lax.axis_size("dec")
    up = [(i, (i + 1) % ra_size) for i in range(ra_size)]
    down = [(j, i) for i, j in up]
    right = [(i, i + 1) for i in range(dec_size - 1)]
    left = [(j, i) for i, j in right]
    sides = [right + left] if dec_size == 2 else [right, left]
    x, up_head, up_rest, down_head, down_rest, *packed = edges_of(radii, x, len(sides))
    over = jnp.sum(radii) > cap_of(chans)
    before_rest, after_rest = lax.cond(
        over,
        lambda a, b: (lax.ppermute(a, "ra", up), lax.ppermute(b, "ra", down)),
        lambda a, b: (a, b),
        up_rest, down_rest,
    )
    before_rest, after_rest, up_head, down_head = lax.optimization_barrier((before_rest, after_rest, up_head, down_head))
    before, after = lax.ppermute(up_head, "ra", up), lax.ppermute(down_head, "ra", down)
    halos = [lax.ppermute(p, "dec", pairs) for p, pairs in zip(packed, sides)]
    corners = [
        (diagonal(p[-EDGE:], 1, pairs), diagonal(p[:EDGE], -1, pairs)) for p, pairs in zip(packed, sides)
    ]
    dec_table, inner_table, outer_table = tables(rows, cols, len(sides))
    halos, corners = lax.optimization_barrier((halos, corners))
    partial, inner = smooth_inner(radii, x, halos, dec_table, inner_table)
    outer = smooth_outer(
        radii, rows, partial, (before, before_rest), (after, after_rest), dec_table, outer_table, corners
    )
    inner_total = inner_gram(inner, swap(inner, "band", 1), valid)
    total, smoothed = gram(inner_total, outer, swap(outer, "band", 1), valid, inner)
    steps = [("dec", 1 << b) for b in range(dec_size.bit_length() - 1)]
    steps += [("ra", 1 << b) for b in range(ra_size.bit_length() - 1)]
    for axis, step in steps[:-1]:
        total = total + swap(total, axis, step)
    mean, covariance = finish(total, swap(total, *steps[-1]))
    return (jnp.transpose(smoothed, (1, 0, 2)), mean, covariance)


def solution(mesh):
    return jax.shard_map(
        per_device,
        mesh=mesh,
        in_specs=(
            P(("groups", "band"), "ra", "dec"),
            P(("groups", "band")),
            P(("groups", "ra"), "dec"),
        ),
        out_specs=(P(("groups", "band"), "ra", "dec"), P(("groups", "band")), P("groups", "band")),
        check_vma=False,
    )
```

```python
import functools

import jax
import jax.numpy as jnp
from jax import lax
from jax.experimental import pallas as pl
from jax.experimental.pallas import tpu as pltpu
from jax.sharding import PartitionSpec as P

RMAX = 17
LANES = 128
SLOTS = LANES // RMAX
EDGE = -(-RMAX // SLOTS)
PAD = 8
HALO = 24
VMEM_LIMIT = 32 * 1024 * 1024
BF16, F32 = jnp.bfloat16, jnp.float32
VMEM = pl.BlockSpec(memory_space=pltpu.VMEM)
SMEM = pl.BlockSpec(memory_space=pltpu.SMEM)
HBM = pl.BlockSpec(memory_space=pltpu.HBM)
PARAMS = pltpu.CompilerParams(vmem_limit_bytes=VMEM_LIMIT)


SPARE = LANES - SLOTS * RMAX


def row_groups(rows):
    middle = rows - 2 * EDGE * SLOTS
    count = min(n for n in range(middle + 1) if middle - n * SLOTS <= n // 2)
    first = EDGE * SLOTS
    starts = [g * SLOTS for g in range(EDGE + count)] + [rows - (EDGE - g) * SLOTS for g in range(EDGE)]
    left_over = [(first + count * SLOTS + i, EDGE + 2 * i) for i in range(max(0, middle - count * SLOTS))]
    return starts, left_over


def tables_kernel(sides, rows, order_ref, dec_ref, inner_ref, outer_ref, *offset_refs):
    cols = dec_ref.shape[2]
    dec = lax.axis_index("dec")

    def offsets(offset_ref, used, offset):
        offset_ref[...] = jnp.where(used, offset, 2 * LANES).astype(F32)

    def grid(ref):
        return [lax.broadcasted_iota(jnp.int32, ref.shape, d) for d in (0, 1)]

    z, y = grid(offset_refs[0])
    before, after = z - cols - RMAX, z
    if sides == 1:
        column = jnp.where(z < cols, z, jnp.where(dec == 0, after, before))
    else:
        column = jnp.where(z < cols, z, jnp.where(z < cols + RMAX, before, after - RMAX))
    offsets(offset_refs[0], z < cols + sides * RMAX, column - y)
    out, source = grid(offset_refs[1])
    edge = out - (offset_refs[1].shape[0] - 2 * HALO)
    row = jnp.where(edge < 0, out + RMAX, jnp.where(edge < HALO, edge, edge - HALO + rows - RMAX))
    offsets(offset_refs[1], source < rows, source - row)
    out, source = grid(offset_refs[2])
    row = jnp.where(out < HALO, out, out - HALO + rows - RMAX)
    tail = source - HALO
    offsets(
        offset_refs[2], (source < RMAX) | ((tail >= 0) & (tail < RMAX)), jnp.where(tail < 0, source - RMAX, tail + rows) - row
    )
    line = (lax.broadcasted_iota(jnp.int32, (8, LANES), 1) - RMAX).astype(F32)

    def one_radius(index, carry):
        radius = jnp.full((8, LANES), index, jnp.int32).astype(F32)
        spread = 0.5 * radius
        scale = -1.0 / (2.0 * spread * spread)
        raw = jnp.where(jnp.abs(line) <= radius, jnp.exp(line * line * scale), 0.0)
        inverse = 1.0 / jnp.sum(raw, axis=1, keepdims=True)
        limit, scale, inverse = radius[:1, :1], scale[:1, :1], inverse[:1]
        for ref, offset_ref in zip((dec_ref, inner_ref, outer_ref), offset_refs):
            offset = offset_ref[...]
            taps = jnp.where(jnp.abs(offset) <= limit, jnp.exp(offset * offset * scale) * inverse, 0.0)
            ref[index] = taps.astype(BF16)
        return carry

    lax.fori_loop(1, RMAX + 1, one_radius, 0)


def tables(rows, cols, sides, order):
    own = -(-rows // 16) * 16
    inner = -(-(rows - 2 * RMAX) // 16) * 16
    shapes = [(cols + LANES, cols), (inner + 2 * HALO, own), (2 * HALO, 2 * HALO)]
    return pl.pallas_call(
        functools.partial(tables_kernel, sides, rows),
        out_shape=[pltpu.VMEM((RMAX + 1, *shape), BF16) for shape in shapes],
        in_specs=[pl.BlockSpec(memory_space=pl.ANY)],
        out_specs=[VMEM] * 3,
        scratch_shapes=[pltpu.VMEM(shape, F32) for shape in shapes],
        compiler_params=PARAMS,
        cost_estimate=pl.CostEstimate(flops=10**5, bytes_accessed=10**5, transcendentals=0),
    )(order)


def edges_kernel(sides, rad_ref, source_ref, *refs):
    (over_ref, up_ref, up_rest_ref, down_ref, down_rest_ref), refs = refs[:5], refs[5:]
    edge_refs, refs = refs[:3 * sides], refs[3 * sides:]
    x_ref, low_wide, high_wide, low_packed, high_packed, low_rest, high_rest, sems = refs
    rows, chans, cols = x_ref.shape
    pitch = chans + PAD
    cap, full = up_ref.shape[0], RMAX * chans
    spans = ((0, RMAX), (rows - RMAX, RMAX), (RMAX, rows - 2 * RMAX))
    copies = [
        pltpu.make_async_copy(source_ref.at[pl.ds(start, n)], x_ref.at[pl.ds(start, n)], sems.at[i])
        for i, (start, n) in enumerate(spans)
    ]
    for copy in copies:
        copy.start()
    low_packed[...] = jnp.zeros_like(low_packed)
    high_packed[...] = jnp.zeros_like(high_packed)
    for copy in copies[:2]:
        copy.wait()
    for i in range(RMAX):
        low_wide[pl.ds(i * pitch, chans), :] = x_ref[i].astype(F32)
        high_wide[pl.ds(i * pitch, chans), :] = x_ref[rows - RMAX + i].astype(F32)

    total = 0
    for c in range(chans):
        total = total + rad_ref[c]

    def both_ways(i, carry):
        start, stop = carry
        c = chans - 1 - i
        low_packed[pl.ds(HALO + start, RMAX), :] = low_wide[pl.ds(i, RMAX, stride=pitch), :]
        high_packed[pl.ds(HALO + stop - RMAX, RMAX), :] = high_wide[pl.ds(c, RMAX, stride=pitch), :]
        return start + rad_ref[i], stop - rad_ref[c]

    lax.fori_loop(0, chans, both_ways, (0, total), unroll=16)
    rests = []
    for i, (packed, ref, rest, rest_ref) in enumerate((
        (low_packed, down_ref, low_rest, down_rest_ref), (high_packed, up_ref, high_rest, up_rest_ref)
    )):
        ref[...] = packed[HALO:HALO + cap, :].astype(BF16)
        rest[...] = packed[HALO + cap:HALO + full, :].astype(BF16)
        rests.append(pltpu.make_async_copy(rest, rest_ref, sems.at[3 + i]))
        rests[-1].start()
    over_ref[0] = jnp.where(total > cap, 1, 0)

    copies[2].wait()
    dec = lax.axis_index("dec")
    lane = lax.broadcasted_iota(jnp.int32, (chans, LANES), 1)
    for side in range(sides):
        edge_ref, low_ref, high_ref = edge_refs[3 * side:3 * side + 3]
        if sides == 1:
            first = jnp.where(dec == 0, cols - RMAX, 0)
        else:
            first = cols - RMAX if side == 0 else 0
        starts, left_over = row_groups(rows)

        def moved(row, lane_of_first):
            return pltpu.roll(x_ref[row].astype(F32), lax.rem(lane_of_first - first + 2 * LANES, LANES), 1)

        tiles = []
        for g, start in enumerate(starts):
            packed = moved(start, 0)
            for j in range(1, SLOTS):
                packed = jnp.where(lane < RMAX * j, packed, moved(start + j, RMAX * j))
            for row, tile in left_over:
                if g in (tile, tile + 1):
                    packed = jnp.where(lane < LANES - SPARE, packed, moved(row, LANES - SPARE - SPARE * (g - tile)))
            edge_ref[g] = packed.astype(BF16)
            tiles.append(packed)
        half = chans // 2
        shared = [jnp.where(
            (lane[:half] < LANES // 2) == (part is tiles[EDGE - 1]), part[:half], pltpu.roll(part[half:], LANES // 2, 1)
        ) for part in (tiles[EDGE - 1], tiles[-EDGE])]
        for ref, whole, part in ((low_ref, tiles[:EDGE - 1], shared[0]), (high_ref, tiles[1 - EDGE:], shared[1])):
            for i, tile in enumerate(whole):
                ref[i * chans:(i + 1) * chans, :] = tile.astype(BF16)
            ref[(EDGE - 1) * chans:, :] = part.astype(BF16)
    for copy in rests:
        copy.wait()


def cap_of(chans):
    return RMAX * chans * 5 // 8 // 16 * 16


def edges_of(radii, x, sides):
    rows, chans, cols = x.shape
    full, cap = RMAX * chans, cap_of(chans)
    head, rest = pltpu.VMEM((cap, cols), BF16), jax.ShapeDtypeStruct((full - cap, cols), BF16)
    packed = [pltpu.VMEM((len(row_groups(rows)[0]), chans, LANES), BF16)]
    packed += [pltpu.VMEM(((EDGE - 1) * chans + chans // 2, LANES), BF16)] * 2
    return pl.pallas_call(
        functools.partial(edges_kernel, sides),
        out_shape=[pltpu.SMEM((1,), jnp.int32), head, rest, head, rest] + packed * sides,
        in_specs=[SMEM, HBM],
        out_specs=[SMEM] + [VMEM, HBM] * 2 + [VMEM] * (3 * sides),
        scratch_shapes=[pltpu.VMEM(x.shape, BF16)] + [pltpu.VMEM((RMAX * (chans + PAD), cols), F32)] * 2
        + [pltpu.VMEM((full + 2 * HALO, cols), F32)] * 2
        + [pltpu.VMEM(rest.shape, BF16)] * 2
        + [pltpu.SemaphoreType.DMA((5,))],
        compiler_params=PARAMS,
        cost_estimate=pl.CostEstimate(flops=10**6, bytes_accessed=5 * 10**6, transcendentals=0),
    )(radii, x)


def widen(tiles, j):
    lane = lax.broadcasted_iota(jnp.int32, tiles[0].shape, 1)
    value = None
    for side, part in enumerate(tiles):
        shift = (RMAX * side - RMAX * j) % LANES
        part = part if shift == 0 else pltpu.roll(part, shift, 1)
        value = part if side == 0 else jnp.where(lane < RMAX, value, part)
    return value


def inner_kernel(sides, rad_ref, x_ref, dec_ref, ra_ref, *refs):
    edge_refs, (out_ref, begun, x, own, halo, result, sem) = refs[:sides], refs[sides:]
    rows, chans, cols = x_ref.shape
    load = pltpu.make_async_copy(x_ref, x, sem)
    load.start()
    pitch = chans + PAD
    own_rows, inner = ra_ref.shape[2], rows - 2 * RMAX
    base = ra_ref.shape[1] - 2 * HALO

    starts, left_over = row_groups(rows)
    for g, start in enumerate(starts):
        tiles = [ref[g].astype(F32) for ref in edge_refs]
        for j in range(SLOTS):
            halo[pl.ds((start + j) * pitch, chans), :] = widen(tiles, j)
    lane = lax.broadcasted_iota(jnp.int32, (chans, LANES), 1)
    for row, g in left_over:
        tiles = []
        for ref in edge_refs:
            begin, end = (pltpu.roll(ref[g + i].astype(F32), SPARE * (1 + i), 1) for i in range(2))
            tiles.append(jnp.where(lane < SPARE, begin, end))
        halo[pl.ds(row * pitch, chans), :] = widen(tiles, 0)

    def copy_row(i, carry):
        own[pl.ds(i * pitch, chans), :] = x[i].astype(F32)
        return carry

    load.wait()
    lax.fori_loop(0, rows, copy_row, 0)
    for i in range(rows, own_rows):
        own[pl.ds(i * pitch, chans), :] = jnp.zeros((chans, cols), F32)
        halo[pl.ds(i * pitch, chans), :] = jnp.zeros((chans, cols), F32)

    radii = [rad_ref[c] for c in range(chans)]
    partials = []
    for c, radius in enumerate(radii):
        picked = pl.ds(c, own_rows, stride=pitch)
        lhs = jnp.concatenate([own[picked, :].astype(BF16), halo[picked, :].astype(BF16)], 1)
        partials.append(jnp.dot(lhs, dec_ref[radius], preferred_element_type=F32).astype(BF16))
    for c, (radius, partial) in enumerate(zip(radii, partials)):
        smoothed = jnp.dot(ra_ref[radius], partial, preferred_element_type=F32)
        result[pl.ds(c, inner, stride=pitch), :] = smoothed[:inner]
        begun[pl.ds(c, RMAX, stride=pitch), :] = smoothed[base:base + RMAX]
        begun[pl.ds(RMAX * pitch + c, RMAX, stride=pitch), :] = smoothed[base + HALO:base + HALO + RMAX]

    def store(i, carry):
        out_ref[i] = result[pl.ds(i * pitch, chans), :].astype(BF16)
        return carry

    lax.fori_loop(0, inner, store, 0)


def smooth_inner(radii, x, halos, dec_table, ra_table):
    rows, chans, cols = x.shape
    pitch, own_rows, inner = chans + PAD, ra_table.shape[2], rows - 2 * RMAX
    operands = [x, dec_table, ra_table, *halos]
    return pl.pallas_call(
        functools.partial(inner_kernel, len(halos)),
        out_shape=[
            pltpu.VMEM((inner, chans, cols), BF16),
            pltpu.VMEM((2 * RMAX * pitch, cols), F32),
        ],
        in_specs=[SMEM, HBM] + [VMEM] * (len(operands) - 1),
        out_specs=[VMEM] * 2,
        scratch_shapes=[
            pltpu.VMEM(x.shape, BF16),
            pltpu.VMEM((own_rows * pitch, cols), F32),
            pltpu.VMEM((own_rows * pitch, LANES), F32),
            pltpu.VMEM((inner * pitch, cols), F32),
            pltpu.SemaphoreType.DMA,
        ],
        compiler_params=PARAMS,
        cost_estimate=pl.CostEstimate(flops=1, bytes_accessed=1, transcendentals=0),
    )(radii, *operands)


def outer_kernel(sides, rad_ref, begun, before_ref, before_rest, after_ref, after_rest, dec_ref, ra_ref, *refs):
    corner_refs, (out_ref, corner, before, after, result) = refs[:2 * sides], refs[2 * sides:]
    rows, chans, cols = out_ref.shape
    pitch = chans + PAD

    for part, base in ((0, 0), (1, HALO)):
        starts = [g * SLOTS if part else g * SLOTS + RMAX - EDGE * SLOTS for g in range(EDGE)]
        shared = EDGE - 1 if part else 0
        order = [*range(EDGE - 1), EDGE - 1] if part else [EDGE - 1, *range(EDGE - 1)]
        for g, (start, place) in enumerate(zip(starts, order)):
            tiles = []
            for ref in corner_refs[part::2]:
                tile = ref[place * chans:min(place * chans + chans, ref.shape[0]), :].astype(F32)
                if g == shared:
                    tile = jnp.concatenate([tile, pltpu.roll(tile, LANES // 2, 1)], 0)
                tiles.append(tile)
            for j in range(SLOTS):
                if 0 <= start + j < RMAX:
                    corner[pl.ds((base + start + j) * pitch, chans), :] = widen(tiles, j)
        for row in range(RMAX, HALO):
            corner[pl.ds((base + row) * pitch, chans), :] = jnp.zeros((chans, LANES), F32)

    for packed, parts in ((before, (before_ref, before_rest)), (after, (after_ref, after_rest))):
        packed[:HALO, :] = jnp.zeros((HALO, cols), F32)
        packed[packed.shape[0] - HALO:, :] = jnp.zeros((HALO, cols), F32)
        start = HALO
        for part in parts:
            packed[start:start + part.shape[0], :] = part[...].astype(F32)
            start += part.shape[0]

    radii = [rad_ref[c] for c in range(chans)]
    partials = []
    offset = 0
    for c, radius in enumerate(radii):
        planes = [
            before[pl.ds(HALO - RMAX + offset + radius, HALO), :],
            after[pl.ds(HALO + offset, HALO), :],
        ]
        picked = pl.ds(c, 2 * HALO, stride=pitch)
        lhs = jnp.concatenate([jnp.concatenate(planes, 0).astype(BF16), corner[picked, :].astype(BF16)], 1)
        partials.append(jnp.dot(lhs, dec_ref[radius], preferred_element_type=F32).astype(BF16))
        offset = offset + radius
    for c, (radius, partial) in enumerate(zip(radii, partials)):
        smoothed = jnp.dot(ra_ref[radius], partial, preferred_element_type=F32)
        result[pl.ds(c, RMAX, stride=pitch), :] = smoothed[:RMAX]
        result[pl.ds(RMAX * pitch + c, RMAX, stride=pitch), :] = smoothed[HALO:HALO + RMAX]

    def store(i, carry):
        picked = pl.ds(i * pitch, chans)
        out_ref[i] = (begun[picked, :] + result[picked, :]).astype(BF16)
        return carry

    lax.fori_loop(0, rows, store, 0)


def smooth_outer(radii, begun, before, after, dec_table, ra_table, corners):
    chans, cols = radii.shape[0], begun.shape[1]
    pitch = chans + PAD
    operands = [begun, *before, *after, dec_table, ra_table] + [part for side in corners for part in side]
    return pl.pallas_call(
        functools.partial(outer_kernel, len(corners)),
        out_shape=pltpu.VMEM((2 * RMAX, chans, cols), BF16),
        in_specs=[SMEM] + [VMEM] * len(operands),
        out_specs=VMEM,
        scratch_shapes=[
            pltpu.VMEM((2 * HALO * pitch, LANES), F32),
            pltpu.VMEM((RMAX * chans + 2 * HALO, cols), F32),
            pltpu.VMEM((RMAX * chans + 2 * HALO, cols), F32),
            pltpu.VMEM((2 * RMAX * pitch, cols), F32),
        ],
        compiler_params=PARAMS,
        cost_estimate=pl.CostEstimate(flops=10000000000, bytes_accessed=5 * 10**6, transcendentals=0),
    )(radii, *operands)


SUM_ROWS = 8


def add_products(total, own_ref, other_ref, valid_ref, first_row, rows):
    chans = own_ref.shape[1]
    depth = max(d for d in range(1, 27) if rows % d == 0)

    def nt(a, b):
        return lax.dot_general(a, b, (((1,), (1,)), ((), ())), preferred_element_type=F32)

    def body(i, carry):
        picked = [i * depth + j for j in range(depth)]
        line = jnp.concatenate([valid_ref[pl.ds(first_row(r), 1), :].astype(BF16) for r in picked], 1)
        own, other = (jnp.concatenate([ref[r] for r in picked], 1) for ref in (own_ref, other_ref))
        both = jnp.concatenate([own, other], 0)
        total[:2 * chans, :] += nt(both, own * line)
        total[2 * chans:, :] += nt(jnp.broadcast_to(line, (16, line.shape[1])), own)[:SUM_ROWS]
        return carry

    lax.fori_loop(0, rows // depth, body, 0)


def inner_gram_kernel(own_ref, other_ref, valid_ref, total_ref):
    total_ref[...] = jnp.zeros_like(total_ref)
    add_products(total_ref, own_ref, other_ref, valid_ref, lambda r: r + RMAX, own_ref.shape[0])


def inner_gram(own, other, valid):
    chans = own.shape[1]
    return pl.pallas_call(
        inner_gram_kernel,
        out_shape=pltpu.VMEM((2 * chans + SUM_ROWS, chans), F32),
        in_specs=[VMEM] * 3,
        out_specs=VMEM,
        compiler_params=PARAMS,
        cost_estimate=pl.CostEstimate(flops=10**9, bytes_accessed=3 * 10**6, transcendentals=0),
    )(own, other, valid)


def gram_kernel(inner_ref, own_ref, other_ref, valid_ref, inner_own_ref, out_ref, smoothed_ref, total, sems):
    rows, chans = valid_ref.shape[0], own_ref.shape[1]
    half = chans // 2
    band = lax.axis_index("band")
    copies = [
        pltpu.make_async_copy(source, smoothed_ref.at[pl.ds(start, source.shape[0])], sems.at[i])
        for i, (source, start) in enumerate((
            (inner_own_ref, RMAX),
            (own_ref.at[pl.ds(0, RMAX)], 0),
            (own_ref.at[pl.ds(RMAX, RMAX)], rows - RMAX),
        ))
    ]
    for copy in copies:
        copy.start()
    total[...] = inner_ref[...]
    add_products(
        total, own_ref, other_ref, valid_ref, lambda r: jnp.where(r < RMAX, r, r + rows - 2 * RMAX), 2 * RMAX
    )
    low = pltpu.roll(total[half:chans, :], half, 1)
    row = lax.broadcasted_iota(jnp.int32, (half, chans), 0)
    lane = lax.broadcasted_iota(jnp.int32, (half, chans), 1)
    out_ref[:half, :] = jnp.where(lane < row, low, total[:half, :])
    cross = total[chans:2 * chans, :]
    out_ref[half:chans, :] = jnp.where(band == 0, cross[:half], jnp.transpose(cross)[half:])
    diagonal = jnp.sum(jnp.where(lane == row, low, 0.0), axis=0, keepdims=True)
    row = lax.broadcasted_iota(jnp.int32, (SUM_ROWS, chans), 0)
    tail = jnp.where(row == 1, diagonal, total[2 * chans:, :])
    out_ref[chans:, :] = jnp.where(row == 2, jnp.sum(valid_ref[...].astype(F32)), tail)
    for copy in copies:
        copy.wait()


def gram(inner, own, other, valid, inner_own):
    _, chans, cols = own.shape
    return pl.pallas_call(
        gram_kernel,
        out_shape=[
            pltpu.VMEM((chans + SUM_ROWS, chans), F32),
            jax.ShapeDtypeStruct((valid.shape[0], chans, cols), BF16),
        ],
        in_specs=[VMEM] * 5,
        out_specs=[VMEM, pl.BlockSpec(memory_space=pl.ANY)],
        scratch_shapes=[pltpu.VMEM(inner.shape, F32), pltpu.SemaphoreType.DMA((3,))],
        compiler_params=PARAMS,
    )(inner, own, other, valid, inner_own)


def finish_kernel(mine_ref, theirs_ref, mean_ref, cov_ref):
    chans = mine_ref.shape[1]
    half = chans // 2
    band = lax.axis_index("band")
    count = mine_ref[chans + 2:chans + 3, :1]
    folded = mine_ref[:half, :]
    mirror = jnp.transpose(jnp.concatenate([folded, jnp.zeros((half, chans), F32)], 0))
    row = lax.broadcasted_iota(jnp.int32, (half, chans), 0)
    lane = lax.broadcasted_iota(jnp.int32, (half, chans), 1)
    upper = jnp.where(lane < row, mirror[:half], folded)
    column = lane - half
    corner = jnp.where(column < row, pltpu.roll(folded, half, 1), pltpu.roll(mirror[:half], half, 1))
    corner = jnp.where(column == row, pltpu.roll(mine_ref[chans:chans + SUM_ROWS, :], half, 1)[1:2, :], corner)
    own = jnp.concatenate([upper, jnp.where(column < 0, mirror[half:], corner)], 0)
    mine, theirs = mine_ref[half:chans, :], theirs_ref[half:chans, :]
    cross = jnp.concatenate([jnp.where(band == 0, mine, theirs), jnp.where(band == 0, theirs, mine)], 0)
    cross = jnp.where(band == 0, cross, jnp.transpose(cross))
    mean = mine_ref[chans:chans + 1, :] / count
    other_mean = theirs_ref[chans:chans + 1, :] / count
    mean_ref[...] = mean
    for block, left, b in ((own, mean, band), (cross, other_mean, 1 - band)):
        left = jnp.transpose(jnp.broadcast_to(left, (chans, chans)))
        cov_ref[pl.ds(pl.multiple_of(b * chans, chans), chans), :] = (block - count * left * mean) / (count - 1.0)


def finish(mine, theirs):
    chans = mine.shape[1]
    mean, covariance = pl.pallas_call(
        finish_kernel,
        out_shape=[jax.ShapeDtypeStruct((1, chans), F32), jax.ShapeDtypeStruct((2 * chans, chans), F32)],
        in_specs=[VMEM] * 2,
        out_specs=[VMEM] * 2,
        compiler_params=PARAMS,
    )(mine, theirs)
    return mean.reshape(chans), covariance


def swap(array, axis, step):
    size = lax.axis_size(axis)
    return lax.ppermute(array, axis, [(i, i ^ step) for i in range(size)])


def diagonal(array, ra_step, dec_pairs):
    ra_size, dec_size = lax.axis_size("ra"), lax.axis_size("dec")
    pairs = [
        (i * dec_size + a, (i + ra_step) % ra_size * dec_size + b) for i in range(ra_size) for a, b in dec_pairs
    ]
    return lax.ppermute(array, ("ra", "dec"), pairs)


def per_device(sky_maps, radii, valid):
    x = jnp.transpose(sky_maps, (1, 0, 2))
    radii = pltpu.with_memory_space_constraint(radii, pltpu.HBM)
    x = pltpu.with_memory_space_constraint(x, pltpu.HBM)
    rows, chans, cols = x.shape
    ra_size, dec_size = lax.axis_size("ra"), lax.axis_size("dec")
    up = [(i, (i + 1) % ra_size) for i in range(ra_size)]
    down = [(j, i) for i, j in up]
    right = [(i, i + 1) for i in range(dec_size - 1)]
    left = [(j, i) for i, j in right]
    sides = [right + left] if dec_size == 2 else [right, left]
    over, up_head, up_rest, down_head, down_rest, *packed = edges_of(radii, x, len(sides))
    before_rest, after_rest = lax.switch(
        over[0],
        [lambda a, b: (a, b), lambda a, b: (lax.ppermute(a, "ra", up), lax.ppermute(b, "ra", down))],
        up_rest, down_rest,
    )
    before, after = lax.ppermute(up_head, "ra", up), lax.ppermute(down_head, "ra", down)
    packed = [packed[3 * i:3 * i + 3] for i in range(len(sides))]
    halos = [lax.ppermute(p, "dec", pairs) for (p, _, _), pairs in zip(packed, sides)]
    corners = [
        (diagonal(high, 1, pairs), diagonal(low, -1, pairs)) for (_, low, high), pairs in zip(packed, sides)
    ]
    dec_table, inner_table, outer_table = tables(rows, cols, len(sides), before_rest)
    inner, begun = smooth_inner(radii, x, halos, dec_table, inner_table)
    outer = smooth_outer(
        radii, begun, (before, before_rest), (after, after_rest), dec_table, outer_table, corners
    )
    inner_total = inner_gram(inner, swap(inner, "band", 1), valid)
    total, smoothed = gram(inner_total, outer, swap(outer, "band", 1), valid, inner)
    steps = [("dec", 1 << b) for b in range(dec_size.bit_length() - 1)]
    steps += [("ra", 1 << b) for b in range(ra_size.bit_length() - 1)]
    for axis, step in steps:
        total = total + swap(total, axis, step)
    mean, covariance = finish(total, swap(total, "band", 1))
    return (jnp.transpose(smoothed, (1, 0, 2)), mean, covariance)


def solution(mesh):
    return jax.shard_map(
        per_device,
        mesh=mesh,
        in_specs=(
            P(("groups", "band"), "ra", "dec"),
            P(("groups", "band")),
            P(("groups", "ra"), "dec"),
        ),
        out_specs=(P(("groups", "band"), "ra", "dec"), P(("groups", "band")), P("groups", "band")),
        check_vma=False,
    )
```

```python
import functools

import jax
import jax.numpy as jnp
from jax import lax
from jax.experimental import pallas as pl
from jax.experimental.pallas import tpu as pltpu
from jax.sharding import PartitionSpec as P

RMAX = 17
LANES = 128
SLOTS = LANES // RMAX
EDGE = -(-RMAX // SLOTS)
PAD = 8
HALO = 24
VMEM_LIMIT = 32 * 1024 * 1024
BF16, F32 = jnp.bfloat16, jnp.float32
VMEM = pl.BlockSpec(memory_space=pltpu.VMEM)
SMEM = pl.BlockSpec(memory_space=pltpu.SMEM)
HBM = pl.BlockSpec(memory_space=pltpu.HBM)
PARAMS = pltpu.CompilerParams(vmem_limit_bytes=VMEM_LIMIT)


SPARE = LANES - SLOTS * RMAX


def row_groups(rows):
    middle = rows - 2 * EDGE * SLOTS
    small = LANES // 2 // RMAX
    count = min(n for n in range(middle + 1) if middle - n * SLOTS <= (2 * EDGE + n) // 2 + small)
    starts = [g * SLOTS for g in range(EDGE + count)] + [rows - (EDGE - g) * SLOTS for g in range(EDGE)]
    rest = list(range((EDGE + count) * SLOTS, rows - EDGE * SLOTS))
    left_over = [(row, 2 * i) for i, row in enumerate(rest[small:])]
    return starts, left_over, rest[:small]


def tables_kernel(sides, rows, order_ref, dec_ref, inner_ref, outer_ref, *offset_refs):
    cols = dec_ref.shape[2]
    dec = lax.axis_index("dec")

    def offsets(offset_ref, used, offset):
        offset_ref[...] = jnp.where(used, offset, 2 * LANES).astype(F32)

    def grid(ref):
        return [lax.broadcasted_iota(jnp.int32, ref.shape, d) for d in (0, 1)]

    z, y = grid(offset_refs[0])
    before, after = z - cols - RMAX, z
    if sides == 1:
        column = jnp.where(z < cols, z, jnp.where(dec == 0, after, before))
    else:
        column = jnp.where(z < cols, z, jnp.where(z < cols + RMAX, before, after - RMAX))
    offsets(offset_refs[0], z < cols + sides * RMAX, column - y)
    out, source = grid(offset_refs[1])
    edge = out - (offset_refs[1].shape[0] - 2 * HALO)
    row = jnp.where(edge < 0, out + RMAX, jnp.where(edge < HALO, edge, edge - HALO + rows - RMAX))
    offsets(offset_refs[1], source < rows, source - row)
    out, source = grid(offset_refs[2])
    row = jnp.where(out < HALO, out, out - HALO + rows - RMAX)
    tail = source - HALO
    offsets(
        offset_refs[2], (source < RMAX) | ((tail >= 0) & (tail < RMAX)), jnp.where(tail < 0, source - RMAX, tail + rows) - row
    )
    line = (lax.broadcasted_iota(jnp.int32, (8, LANES), 1) - RMAX).astype(F32)

    def one_radius(index, carry):
        radius = jnp.full((8, LANES), index, jnp.int32).astype(F32)
        spread = 0.5 * radius
        scale = -1.0 / (2.0 * spread * spread)
        raw = jnp.where(jnp.abs(line) <= radius, jnp.exp(line * line * scale), 0.0)
        inverse = 1.0 / jnp.sum(raw, axis=1, keepdims=True)
        limit, scale, inverse = radius[:1, :1], scale[:1, :1], inverse[:1]
        for ref, offset_ref in zip((dec_ref, inner_ref, outer_ref), offset_refs):
            offset = offset_ref[...]
            taps = jnp.where(jnp.abs(offset) <= limit, jnp.exp(offset * offset * scale) * inverse, 0.0)
            ref[index] = taps.astype(BF16)
        return carry

    lax.fori_loop(1, RMAX + 1, one_radius, 0)


def tables(rows, cols, sides, order):
    own = -(-rows // 16) * 16
    inner = -(-(rows - 2 * RMAX) // 16) * 16
    shapes = [(cols + LANES, cols), (inner + 2 * HALO, own), (2 * HALO, 2 * HALO)]
    return pl.pallas_call(
        functools.partial(tables_kernel, sides, rows),
        out_shape=[pltpu.VMEM((RMAX + 1, *shape), BF16) for shape in shapes],
        in_specs=[pl.BlockSpec(memory_space=pl.ANY)],
        out_specs=[VMEM] * 3,
        scratch_shapes=[pltpu.VMEM(shape, F32) for shape in shapes],
        compiler_params=PARAMS,
        cost_estimate=pl.CostEstimate(flops=10**5, bytes_accessed=10**5, transcendentals=0),
    )(order)


def edges_kernel(sides, rad_ref, source_ref, *refs):
    (over_ref, up_ref, up_rest_ref, down_ref, down_rest_ref), refs = refs[:5], refs[5:]
    edge_refs, refs = refs[:3 * sides], refs[3 * sides:]
    x_ref, low_wide, high_wide, low_packed, high_packed, low_rest, high_rest, sems = refs
    rows, chans, cols = x_ref.shape
    pitch = chans + PAD
    cap, full = up_ref.shape[0], RMAX * chans
    spans = ((0, RMAX), (rows - RMAX, RMAX), (RMAX, rows - 2 * RMAX))
    copies = [
        pltpu.make_async_copy(source_ref.at[pl.ds(start, n)], x_ref.at[pl.ds(start, n)], sems.at[i])
        for i, (start, n) in enumerate(spans)
    ]
    for copy in copies:
        copy.start()
    for copy in copies[:2]:
        copy.wait()
    for i in range(RMAX):
        low_wide[pl.ds(i * pitch, chans), :] = x_ref[i].astype(F32)
        high_wide[pl.ds(i * pitch, chans), :] = x_ref[rows - RMAX + i].astype(F32)

    total = 0
    for c in range(chans):
        total = total + rad_ref[c]

    def both_ways(i, carry):
        start, stop = carry
        c = chans - 1 - i
        low_packed[pl.ds(HALO + start, RMAX), :] = low_wide[pl.ds(i, RMAX, stride=pitch), :]
        high_packed[pl.ds(HALO + stop - RMAX, RMAX), :] = high_wide[pl.ds(c, RMAX, stride=pitch), :]
        return start + rad_ref[i], stop - rad_ref[c]

    lax.fori_loop(0, chans, both_ways, (0, total), unroll=16)
    rests = []
    for i, (packed, ref, rest, rest_ref) in enumerate((
        (low_packed, down_ref, low_rest, down_rest_ref), (high_packed, up_ref, high_rest, up_rest_ref)
    )):
        packed[pl.ds(HALO + total, HALO), :] = jnp.zeros((HALO, cols), F32)
        ref[...] = packed[HALO:HALO + cap, :].astype(BF16)
        rests.append(pltpu.make_async_copy(rest, rest_ref, sems.at[3 + i]))

    @pl.when(total > cap)
    def _():
        for packed, rest, copy in ((low_packed, low_rest, rests[0]), (high_packed, high_rest, rests[1])):
            rest[...] = packed[HALO + cap:HALO + full, :].astype(BF16)
            copy.start()
            copy.wait()

    over_ref[0] = jnp.where(total > cap, 1, 0)

    copies[2].wait()
    dec = lax.axis_index("dec")
    lane = lax.broadcasted_iota(jnp.int32, (chans, LANES), 1)
    for side in range(sides):
        edge_ref, low_ref, high_ref = edge_refs[3 * side:3 * side + 3]
        if sides == 1:
            first = jnp.where(dec == 0, cols - RMAX, 0)
        else:
            first = cols - RMAX if side == 0 else 0
        starts, left_over, shared = row_groups(rows)

        def moved(row, lane_of_first):
            return pltpu.roll(x_ref[row].astype(F32), lax.rem(lane_of_first - first + 2 * LANES, LANES), 1)

        tiles = []
        for g, start in enumerate(starts):
            packed = moved(start, 0)
            for j in range(1, SLOTS):
                packed = jnp.where(lane < RMAX * j, packed, moved(start + j, RMAX * j))
            for row, tile in left_over:
                if g in (tile, tile + 1):
                    packed = jnp.where(lane < LANES - SPARE, packed, moved(row, LANES - SPARE - SPARE * (g - tile)))
            edge_ref[g * chans:(g + 1) * chans, :] = packed.astype(BF16)
            tiles.append(packed)
        half = chans // 2

        def beside(part, low):
            return jnp.where((lane[:half] < LANES // 2) == low, part[:half], pltpu.roll(part[half:], LANES // 2, 1))

        packed = jnp.zeros((chans, LANES), F32)
        for j, row in enumerate(shared):
            packed = jnp.where(lane < RMAX * j, packed, moved(row, RMAX * j))
        edge_ref[len(starts) * chans:, :] = beside(packed, True).astype(BF16)
        for ref, whole, part in (
            (low_ref, tiles[:EDGE - 1], beside(tiles[EDGE - 1], True)),
            (high_ref, tiles[1 - EDGE:], beside(tiles[-EDGE], False)),
        ):
            for i, tile in enumerate(whole):
                ref[i * chans:(i + 1) * chans, :] = tile.astype(BF16)
            ref[(EDGE - 1) * chans:, :] = part.astype(BF16)


def cap_of(chans):
    return RMAX * chans * 5 // 8 // 16 * 16


def edges_of(radii, x, sides):
    rows, chans, cols = x.shape
    full, cap = RMAX * chans, cap_of(chans)
    head, rest = pltpu.VMEM((cap, cols), BF16), jax.ShapeDtypeStruct((full - cap, cols), BF16)
    packed = [pltpu.VMEM((len(row_groups(rows)[0]) * chans + chans // 2, LANES), BF16)]
    packed += [pltpu.VMEM(((EDGE - 1) * chans + chans // 2, LANES), BF16)] * 2
    return pl.pallas_call(
        functools.partial(edges_kernel, sides),
        out_shape=[pltpu.SMEM((1,), jnp.int32), head, rest, head, rest] + packed * sides,
        in_specs=[SMEM, HBM],
        out_specs=[SMEM] + [VMEM, HBM] * 2 + [VMEM] * (3 * sides),
        scratch_shapes=[pltpu.VMEM(x.shape, BF16)] + [pltpu.VMEM(((RMAX + 1) * (chans + PAD), cols), F32)] * 2
        + [pltpu.VMEM((full + 2 * HALO, cols), F32)] * 2
        + [pltpu.VMEM(rest.shape, BF16)] * 2
        + [pltpu.SemaphoreType.DMA((5,))],
        compiler_params=PARAMS,
        cost_estimate=pl.CostEstimate(flops=10**6, bytes_accessed=5 * 10**6, transcendentals=0),
    )(radii, x)


def widen(tiles, j):
    lane = lax.broadcasted_iota(jnp.int32, tiles[0].shape, 1)
    value = None
    for side, part in enumerate(tiles):
        shift = (RMAX * side - RMAX * j) % LANES
        part = part if shift == 0 else pltpu.roll(part, shift, 1)
        value = part if side == 0 else jnp.where(lane < RMAX, value, part)
    return value


def inner_kernel(sides, rad_ref, x_ref, dec_ref, ra_ref, *refs):
    edge_refs, (out_ref, begun, x, own, halo, result, sem) = refs[:sides], refs[sides:]
    rows, chans, cols = x_ref.shape
    load = pltpu.make_async_copy(x_ref, x, sem)
    load.start()
    pitch = chans + PAD
    own_rows, inner = ra_ref.shape[2], rows - 2 * RMAX
    base = ra_ref.shape[1] - 2 * HALO

    starts, left_over, shared = row_groups(rows)
    for g, start in enumerate(starts):
        tiles = [ref[g * chans:(g + 1) * chans, :].astype(F32) for ref in edge_refs]
        for j in range(SLOTS):
            halo[pl.ds((start + j) * pitch, chans), :] = widen(tiles, j)
    lane = lax.broadcasted_iota(jnp.int32, (chans, LANES), 1)
    for row, g in left_over:
        tiles = []
        for ref in edge_refs:
            begin, end = (
                pltpu.roll(ref[(g + i) * chans:(g + i + 1) * chans, :].astype(F32), SPARE * (1 + i), 1) for i in range(2)
            )
            tiles.append(jnp.where(lane < SPARE, begin, end))
        halo[pl.ds(row * pitch, chans), :] = widen(tiles, 0)
    tiles = [ref[len(starts) * chans:, :].astype(F32) for ref in edge_refs]
    tiles = [jnp.concatenate([tile, pltpu.roll(tile, LANES // 2, 1)], 0) for tile in tiles]
    for j, row in enumerate(shared):
        halo[pl.ds(row * pitch, chans), :] = widen(tiles, j)

    def copy_row(i, carry):
        own[pl.ds(i * pitch, chans), :] = x[i].astype(F32)
        return carry

    load.wait()
    lax.fori_loop(0, rows, copy_row, 0)
    for i in range(rows, own_rows):
        own[pl.ds(i * pitch, chans), :] = jnp.zeros((chans, cols), F32)
        halo[pl.ds(i * pitch, chans), :] = jnp.zeros((chans, cols), F32)

    radii = [rad_ref[c] for c in range(chans)]
    partials = []
    for c, radius in enumerate(radii):
        picked = pl.ds(c, own_rows, stride=pitch)
        lhs = jnp.concatenate([own[picked, :].astype(BF16), halo[picked, :].astype(BF16)], 1)
        partials.append(jnp.dot(lhs, dec_ref[radius], preferred_element_type=F32).astype(BF16))
    for c, (radius, partial) in enumerate(zip(radii, partials)):
        smoothed = jnp.dot(ra_ref[radius], partial, preferred_element_type=F32)
        result[pl.ds(c, inner, stride=pitch), :] = smoothed[:inner]
        begun[pl.ds(c, RMAX, stride=pitch), :] = smoothed[base:base + RMAX]
        begun[pl.ds(RMAX * pitch + c, RMAX, stride=pitch), :] = smoothed[base + HALO:base + HALO + RMAX]

    def store(i, carry):
        out_ref[i] = result[pl.ds(i * pitch, chans), :].astype(BF16)
        return carry

    lax.fori_loop(0, inner, store, 0)


def smooth_inner(radii, x, halos, dec_table, ra_table):
    rows, chans, cols = x.shape
    pitch, own_rows, inner = chans + PAD, ra_table.shape[2], rows - 2 * RMAX
    operands = [x, dec_table, ra_table, *halos]
    return pl.pallas_call(
        functools.partial(inner_kernel, len(halos)),
        out_shape=[
            pltpu.VMEM((inner, chans, cols), BF16),
            pltpu.VMEM(((2 * RMAX + 1) * pitch, cols), F32),
        ],
        in_specs=[SMEM, HBM] + [VMEM] * (len(operands) - 1),
        out_specs=[VMEM] * 2,
        scratch_shapes=[
            pltpu.VMEM(x.shape, BF16),
            pltpu.VMEM(((own_rows + 1) * pitch, cols), F32),
            pltpu.VMEM(((own_rows + 1) * pitch, LANES), F32),
            pltpu.VMEM(((inner + 1) * pitch, cols), F32),
            pltpu.SemaphoreType.DMA,
        ],
        compiler_params=PARAMS,
        cost_estimate=pl.CostEstimate(flops=1, bytes_accessed=1, transcendentals=0),
    )(radii, *operands)


def reach_lanes(sides):
    return -(-sides * RMAX // 16) * 16


def outer_begin_kernel(rad_ref, order_ref, before_ref, before_rest, after_ref, after_rest, dec_ref, begun, before, after):
    chans, _, cols = begun.shape
    radii = [rad_ref[c] for c in range(chans)]
    total = functools.reduce(lambda a, b: a + b, radii)
    cap = before_ref.shape[0]
    for packed, head, rest in ((before, before_ref, before_rest), (after, after_ref, after_rest)):
        packed[:HALO, :] = jnp.zeros((HALO, cols), F32)
        packed[HALO:HALO + cap, :] = head[...].astype(F32)
        packed[HALO + cap:2 * HALO + cap, :] = jnp.zeros((HALO, cols), F32)
        packed[packed.shape[0] - HALO:, :] = jnp.zeros((HALO, cols), F32)

        @pl.when(total > cap)
        def _():
            packed[HALO + cap:HALO + cap + rest.shape[0], :] = rest[...].astype(F32)

    offset = 0
    for c, radius in enumerate(radii):
        planes = [
            before[pl.ds(HALO - RMAX + offset + radius, HALO), :],
            after[pl.ds(HALO + offset, HALO), :],
        ]
        lhs = jnp.concatenate(planes, 0).astype(BF16)
        begun[c] = jnp.dot(lhs, dec_ref[radius, :cols, :], preferred_element_type=F32)
        offset = offset + radius


def outer_begin(radii, order, before, after, dec_table):
    chans, cols = radii.shape[0], dec_table.shape[2]
    operands = [*before, *after, dec_table]
    return pl.pallas_call(
        outer_begin_kernel,
        out_shape=pltpu.VMEM((chans, 2 * HALO, cols), F32),
        in_specs=[SMEM, pl.BlockSpec(memory_space=pl.ANY)] + [VMEM] * len(operands),
        out_specs=VMEM,
        scratch_shapes=[pltpu.VMEM((RMAX * chans + 2 * HALO, cols), F32)] * 2,
        compiler_params=PARAMS,
        cost_estimate=pl.CostEstimate(flops=2 * 10**9, bytes_accessed=5 * 10**6, transcendentals=0),
    )(radii, order, *operands)


def outer_kernel(sides, rad_ref, dec_begun, ra_begun, dec_ref, ra_ref, *refs):
    corner_refs, (out_ref, corner, result) = refs[:2 * sides], refs[2 * sides:]
    rows, chans, cols = out_ref.shape
    pitch = chans + PAD
    width = reach_lanes(sides)

    for part, base in ((0, 0), (1, HALO)):
        starts = [g * SLOTS if part else g * SLOTS + RMAX - EDGE * SLOTS for g in range(EDGE)]
        shared = EDGE - 1 if part else 0
        order = [*range(EDGE - 1), EDGE - 1] if part else [EDGE - 1, *range(EDGE - 1)]
        for g, (start, place) in enumerate(zip(starts, order)):
            tiles = []
            for ref in corner_refs[part::2]:
                tile = ref[place * chans:min(place * chans + chans, ref.shape[0]), :].astype(F32)
                if g == shared:
                    tile = jnp.concatenate([tile, pltpu.roll(tile, LANES // 2, 1)], 0)
                tiles.append(tile)
            for j in range(SLOTS):
                if 0 <= start + j < RMAX:
                    corner[pl.ds((base + start + j) * pitch, chans), :] = widen(tiles, j)
        for row in range(RMAX, HALO):
            corner[pl.ds((base + row) * pitch, chans), :] = jnp.zeros((chans, LANES), F32)

    radii = [rad_ref[c] for c in range(chans)]
    partials = []
    for c, radius in enumerate(radii):
        lhs = corner[pl.ds(c, 2 * HALO, stride=pitch), :].astype(BF16)[:, :width]
        partial = jnp.dot(lhs, dec_ref[radius, cols:cols + width, :], preferred_element_type=F32) + dec_begun[c]
        partials.append(partial.astype(BF16))
    for c, (radius, partial) in enumerate(zip(radii, partials)):
        smoothed = jnp.dot(ra_ref[radius], partial, preferred_element_type=F32)
        result[pl.ds(c, RMAX, stride=pitch), :] = smoothed[:RMAX]
        result[pl.ds(RMAX * pitch + c, RMAX, stride=pitch), :] = smoothed[HALO:HALO + RMAX]

    def store(i, carry):
        picked = pl.ds(i * pitch, chans)
        out_ref[i] = (ra_begun[picked, :] + result[picked, :]).astype(BF16)
        return carry

    lax.fori_loop(0, rows, store, 0)


def smooth_outer(radii, dec_begun, ra_begun, dec_table, ra_table, corners):
    chans, _, cols = dec_begun.shape
    pitch = chans + PAD
    operands = [dec_begun, ra_begun, dec_table, ra_table] + [part for side in corners for part in side]
    return pl.pallas_call(
        functools.partial(outer_kernel, len(corners)),
        out_shape=pltpu.VMEM((2 * RMAX, chans, cols), BF16),
        in_specs=[SMEM] + [VMEM] * len(operands),
        out_specs=VMEM,
        scratch_shapes=[
            pltpu.VMEM(((2 * HALO + 1) * pitch, LANES), F32),
            pltpu.VMEM(((2 * RMAX + 1) * pitch, cols), F32),
        ],
        compiler_params=PARAMS,
        cost_estimate=pl.CostEstimate(flops=10**10, bytes_accessed=5 * 10**6, transcendentals=0),
    )(radii, *operands)


SUM_ROWS = 8


def add_products(total, row_refs, own_ref, valid_ref, first_row, rows, sums=None):
    depth = max(d for d in range(1, 27) if rows % d == 0)

    def nt(a, b):
        return lax.dot_general(a, b, (((1,), (1,)), ((), ())), preferred_element_type=F32)

    def body(i, carry):
        picked = [i * depth + j for j in range(depth)]
        line = jnp.concatenate([valid_ref[pl.ds(first_row(r), 1), :].astype(BF16) for r in picked], 1)
        own, *others = (jnp.concatenate([ref[r] for r in picked], 1) for ref in (own_ref, *row_refs))
        total[...] += nt(jnp.concatenate(others, 0), own * line)
        if sums is not None:
            sums[...] += nt(jnp.broadcast_to(line, (16, line.shape[1])), own)[:SUM_ROWS]
        return carry

    lax.fori_loop(0, rows // depth, body, 0)


def outer_row(image_rows):
    return lambda r: jnp.where(r < RMAX, r, r + image_rows - 2 * RMAX)


def own_gram_kernel(own_ref, other_ref, outer_ref, valid_ref, out_ref, cross_ref, smoothed_ref, both, sems):
    rows, chans = valid_ref.shape[0], own_ref.shape[1]
    half = chans // 2
    copies = [
        pltpu.make_async_copy(source, smoothed_ref.at[pl.ds(start, source.shape[0])], sems.at[i])
        for i, (source, start) in enumerate((
            (own_ref, RMAX),
            (outer_ref.at[pl.ds(0, RMAX)], 0),
            (outer_ref.at[pl.ds(RMAX, RMAX)], rows - RMAX),
        ))
    ]
    for copy in copies:
        copy.start()
    both[...] = jnp.zeros_like(both)
    products, own, sums = both.at[:2 * chans], both.at[:chans], both.at[2 * chans:]
    add_products(products, (own_ref, other_ref), own_ref, valid_ref, lambda r: r + RMAX, own_ref.shape[0], sums)
    add_products(own, (outer_ref,), outer_ref, valid_ref, outer_row(rows), 2 * RMAX, sums)
    cross_ref[...] = both[chans:2 * chans, :]
    low = pltpu.roll(both[half:chans, :], half, 1)
    row = lax.broadcasted_iota(jnp.int32, (half, chans), 0)
    lane = lax.broadcasted_iota(jnp.int32, (half, chans), 1)
    out_ref[:half, :] = jnp.where(lane < row, low, both[:half, :])
    diagonal = jnp.sum(jnp.where(lane == row, low, 0.0), axis=0, keepdims=True)
    row = lax.broadcasted_iota(jnp.int32, (SUM_ROWS, chans), 0)
    tail = jnp.where(row == 1, diagonal, both[2 * chans:, :])
    out_ref[half:, :] = jnp.where(row == 2, jnp.sum(valid_ref[...].astype(F32)), tail)
    for copy in copies:
        copy.wait()


def own_gram(own, other, outer, valid):
    _, chans, cols = own.shape
    return pl.pallas_call(
        own_gram_kernel,
        out_shape=[
            pltpu.VMEM((chans // 2 + SUM_ROWS, chans), F32),
            pltpu.VMEM((chans, chans), F32),
            jax.ShapeDtypeStruct((valid.shape[0], chans, cols), BF16),
        ],
        in_specs=[VMEM] * 4,
        out_specs=[VMEM, VMEM, HBM],
        scratch_shapes=[pltpu.VMEM((2 * chans + SUM_ROWS, chans), F32), pltpu.SemaphoreType.DMA((3,))],
        compiler_params=PARAMS,
        cost_estimate=pl.CostEstimate(flops=10**9, bytes_accessed=3 * 10**6, transcendentals=0),
    )(own, other, outer, valid)


def cross_gram_kernel(folded_ref, cross_ref, own_ref, other_ref, valid_ref, out_ref, total):
    chans = own_ref.shape[1]
    half = chans // 2
    total[...] = cross_ref[...]
    add_products(total, (other_ref,), own_ref, valid_ref, outer_row(valid_ref.shape[0]), 2 * RMAX)
    cross = total[...]
    out_ref[:half, :] = folded_ref[:half, :]
    out_ref[half:chans, :] = jnp.where(lax.axis_index("band") == 0, cross[:half], jnp.transpose(cross)[half:])
    out_ref[chans:, :] = folded_ref[half:, :]


def cross_gram(folded, cross, own, other, valid):
    chans = own.shape[1]
    return pl.pallas_call(
        cross_gram_kernel,
        out_shape=pltpu.VMEM((chans + SUM_ROWS, chans), F32),
        in_specs=[VMEM] * 5,
        out_specs=VMEM,
        scratch_shapes=[pltpu.VMEM((chans, chans), F32)],
        compiler_params=PARAMS,
    )(folded, cross, own, other, valid)


def finish_kernel(mine_ref, theirs_ref, mean_ref, cov_ref):
    chans = mine_ref.shape[1]
    half = chans // 2
    band = lax.axis_index("band")
    count = mine_ref[chans + 2:chans + 3, :1]
    folded = mine_ref[:half, :]
    mirror = jnp.transpose(jnp.concatenate([folded, jnp.zeros((half, chans), F32)], 0))
    row = lax.broadcasted_iota(jnp.int32, (half, chans), 0)
    lane = lax.broadcasted_iota(jnp.int32, (half, chans), 1)
    upper = jnp.where(lane < row, mirror[:half], folded)
    column = lane - half
    corner = jnp.where(column < row, pltpu.roll(folded, half, 1), pltpu.roll(mirror[:half], half, 1))
    corner = jnp.where(column == row, pltpu.roll(mine_ref[chans:chans + SUM_ROWS, :], half, 1)[1:2, :], corner)
    own = jnp.concatenate([upper, jnp.where(column < 0, mirror[half:], corner)], 0)
    mine, theirs = mine_ref[half:chans, :], theirs_ref[half:chans, :]
    cross = jnp.concatenate([jnp.where(band == 0, mine, theirs), jnp.where(band == 0, theirs, mine)], 0)
    cross = jnp.where(band == 0, cross, jnp.transpose(cross))
    mean = mine_ref[chans:chans + 1, :] / count
    other_mean = theirs_ref[chans:chans + 1, :] / count
    mean_ref[...] = mean
    for block, left, b in ((own, mean, band), (cross, other_mean, 1 - band)):
        left = jnp.transpose(jnp.broadcast_to(left, (chans, chans)))
        cov_ref[pl.ds(pl.multiple_of(b * chans, chans), chans), :] = (block - count * left * mean) / (count - 1.0)


def finish(mine, theirs):
    chans = mine.shape[1]
    mean, covariance = pl.pallas_call(
        finish_kernel,
        out_shape=[jax.ShapeDtypeStruct((1, chans), F32), jax.ShapeDtypeStruct((2 * chans, chans), F32)],
        in_specs=[VMEM] * 2,
        out_specs=[VMEM] * 2,
        compiler_params=PARAMS,
    )(mine, theirs)
    return mean.reshape(chans), covariance


def swap(array, axis, step):
    size = lax.axis_size(axis)
    return lax.ppermute(array, axis, [(i, i ^ step) for i in range(size)])


def diagonal(array, ra_step, dec_pairs):
    ra_size, dec_size = lax.axis_size("ra"), lax.axis_size("dec")
    pairs = [
        (i * dec_size + a, (i + ra_step) % ra_size * dec_size + b) for i in range(ra_size) for a, b in dec_pairs
    ]
    return lax.ppermute(array, ("ra", "dec"), pairs)


def per_device(sky_maps, radii, valid):
    x = jnp.transpose(sky_maps, (1, 0, 2))
    radii = pltpu.with_memory_space_constraint(radii, pltpu.HBM)
    x = pltpu.with_memory_space_constraint(x, pltpu.HBM)
    rows, chans, cols = x.shape
    ra_size, dec_size = lax.axis_size("ra"), lax.axis_size("dec")
    up = [(i, (i + 1) % ra_size) for i in range(ra_size)]
    down = [(j, i) for i, j in up]
    right = [(i, i + 1) for i in range(dec_size - 1)]
    left = [(j, i) for i, j in right]
    sides = [right + left] if dec_size == 2 else [right, left]
    over, up_head, up_rest, down_head, down_rest, *packed = edges_of(radii, x, len(sides))
    before_rest, after_rest = lax.switch(
        over[0],
        [lambda a, b: (a, b), lambda a, b: (lax.ppermute(a, "ra", up), lax.ppermute(b, "ra", down))],
        up_rest, down_rest,
    )
    before, after = lax.ppermute(up_head, "ra", up), lax.ppermute(down_head, "ra", down)
    packed = [packed[3 * i:3 * i + 3] for i in range(len(sides))]
    halos = [lax.ppermute(p, "dec", pairs) for (p, _, _), pairs in zip(packed, sides)]
    corners = [
        (diagonal(high, 1, pairs), diagonal(low, -1, pairs)) for (_, low, high), pairs in zip(packed, sides)
    ]
    dec_table, inner_table, outer_table = tables(rows, cols, len(sides), before_rest)
    inner, begun = smooth_inner(radii, x, halos, dec_table, inner_table)
    dec_begun = outer_begin(radii, begun, (before, before_rest), (after, after_rest), dec_table)
    outer = smooth_outer(radii, dec_begun, begun, dec_table, outer_table, corners)
    folded, cross, smoothed = own_gram(inner, swap(inner, "band", 1), outer, valid)
    total = cross_gram(folded, cross, outer, swap(outer, "band", 1), valid)
    steps = [("dec", 1 << b) for b in range(dec_size.bit_length() - 1)]
    steps += [("ra", 1 << b) for b in range(ra_size.bit_length() - 1)]
    for axis, step in steps:
        total = total + swap(total, axis, step)
    mean, covariance = finish(total, swap(total, "band", 1))
    return (jnp.transpose(smoothed, (1, 0, 2)), mean, covariance)


def solution(mesh):
    return jax.shard_map(
        per_device,
        mesh=mesh,
        in_specs=(
            P(("groups", "band"), "ra", "dec"),
            P(("groups", "band")),
            P(("groups", "ra"), "dec"),
        ),
        out_specs=(P(("groups", "band"), "ra", "dec"), P(("groups", "band")), P("groups", "band")),
        check_vma=False,
    )
```

```python
import functools

import jax
import jax.numpy as jnp
from jax import lax
from jax.experimental import pallas as pl
from jax.experimental.pallas import tpu as pltpu
from jax.sharding import PartitionSpec as P

RMAX = 17
LANES = 128
SLOTS = LANES // RMAX
EDGE = -(-RMAX // SLOTS)
PAD = 8
HALO = 24
VMEM_LIMIT = 32 * 1024 * 1024
BF16, F32 = jnp.bfloat16, jnp.float32
VMEM = pl.BlockSpec(memory_space=pltpu.VMEM)
SMEM = pl.BlockSpec(memory_space=pltpu.SMEM)
HBM = pl.BlockSpec(memory_space=pltpu.HBM)
PARAMS = pltpu.CompilerParams(vmem_limit_bytes=VMEM_LIMIT)


SPARE = LANES - SLOTS * RMAX


def row_groups(rows):
    middle = rows - 2 * EDGE * SLOTS
    small = LANES // 2 // RMAX
    count = min(n for n in range(middle + 1) if middle - n * SLOTS <= (2 * EDGE + n) // 2 + small)
    starts = [g * SLOTS for g in range(EDGE + count)] + [rows - (EDGE - g) * SLOTS for g in range(EDGE)]
    rest = list(range((EDGE + count) * SLOTS, rows - EDGE * SLOTS))
    left_over = [(row, 2 * i) for i, row in enumerate(rest[small:])]
    return starts, left_over, rest[:small]


def tables_kernel(sides, order_ref, x_ref, dec_ref, inner_ref, outer_ref, own, x, sem, *offset_refs):
    rows, chans, cols = x_ref.shape
    load = pltpu.make_async_copy(x_ref, x, sem)
    load.start()
    dec = lax.axis_index("dec")

    def offsets(offset_ref, used, offset):
        offset_ref[...] = jnp.where(used, offset, 2 * LANES).astype(F32)

    def grid(ref):
        return [lax.broadcasted_iota(jnp.int32, ref.shape, d) for d in (0, 1)]

    z, y = grid(offset_refs[0])
    before, after = z - cols - RMAX, z
    if sides == 1:
        column = jnp.where(z < cols, z, jnp.where(dec == 0, after, before))
    else:
        column = jnp.where(z < cols, z, jnp.where(z < cols + RMAX, before, after - RMAX))
    offsets(offset_refs[0], z < cols + sides * RMAX, column - y)
    out, source = grid(offset_refs[1])
    edge = out - (offset_refs[1].shape[0] - 2 * HALO)
    row = jnp.where(edge < 0, out + RMAX, jnp.where(edge < HALO, edge, edge - HALO + rows - RMAX))
    offsets(offset_refs[1], source < rows, source - row)
    out, source = grid(offset_refs[2])
    row = jnp.where(out < HALO, out, out - HALO + rows - RMAX)
    tail = source - HALO
    offsets(
        offset_refs[2], (source < RMAX) | ((tail >= 0) & (tail < RMAX)), jnp.where(tail < 0, source - RMAX, tail + rows) - row
    )
    line = (lax.broadcasted_iota(jnp.int32, (8, LANES), 1) - RMAX).astype(F32)

    def one_radius(index, carry):
        radius = jnp.full((8, LANES), index, jnp.int32).astype(F32)
        spread = 0.5 * radius
        scale = -1.0 / (2.0 * spread * spread)
        raw = jnp.where(jnp.abs(line) <= radius, jnp.exp(line * line * scale), 0.0)
        inverse = 1.0 / jnp.sum(raw, axis=1, keepdims=True)
        limit, scale, inverse = radius[:1, :1], scale[:1, :1], inverse[:1]
        for ref, offset_ref in zip((dec_ref, inner_ref, outer_ref), offset_refs):
            offset = offset_ref[...]
            taps = jnp.where(jnp.abs(offset) <= limit, jnp.exp(offset * offset * scale) * inverse, 0.0)
            ref[index] = taps.astype(BF16)
        return carry

    lax.fori_loop(1, RMAX + 1, one_radius, 0)
    pitch = chans + PAD

    def copy_row(i, carry):
        own[pl.ds(i * pitch, chans), :] = x[i].astype(F32)
        return carry

    load.wait()
    lax.fori_loop(0, rows, copy_row, 0)
    for i in range(rows, inner_ref.shape[2]):
        own[pl.ds(i * pitch, chans), :] = jnp.zeros((chans, cols), F32)


def tables(x, sides, order):
    rows, chans, cols = x.shape
    own = -(-rows // 16) * 16
    inner = -(-(rows - 2 * RMAX) // 16) * 16
    shapes = [(cols + LANES, cols), (inner + 2 * HALO, own), (2 * HALO, 2 * HALO)]
    return pl.pallas_call(
        functools.partial(tables_kernel, sides),
        out_shape=[pltpu.VMEM((RMAX + 1, *shape), BF16) for shape in shapes]
        + [pltpu.VMEM(((own + 1) * (chans + PAD), cols), F32)],
        in_specs=[pl.BlockSpec(memory_space=pl.ANY), HBM],
        out_specs=[VMEM] * 4,
        scratch_shapes=[pltpu.VMEM(x.shape, BF16), pltpu.SemaphoreType.DMA] + [pltpu.VMEM(shape, F32) for shape in shapes],
        compiler_params=PARAMS,
        cost_estimate=pl.CostEstimate(flops=10**5, bytes_accessed=10**5, transcendentals=0),
    )(order, x)


def gather_kernel(rad_ref, source_ref, over_ref, up_ref, up_rest_ref, down_ref, down_rest_ref, low, high, low_wide, high_wide, low_packed, high_packed, low_rest, high_rest, sems):
    rows, chans, cols = source_ref.shape
    pitch = chans + PAD
    cap, full = up_ref.shape[0], RMAX * chans
    copies = [
        pltpu.make_async_copy(source_ref.at[pl.ds(start, RMAX)], ref, sems.at[i])
        for i, (start, ref) in enumerate(((0, low), (rows - RMAX, high)))
    ]
    for copy in copies:
        copy.start()
    for copy, ref, wide in zip(copies, (low, high), (low_wide, high_wide)):
        copy.wait()
        for i in range(RMAX):
            wide[pl.ds(i * pitch, chans), :] = ref[i].astype(F32)

    total = 0
    for c in range(chans):
        total = total + rad_ref[c]

    def both_ways(i, carry):
        start, stop = carry
        c = chans - 1 - i
        low_packed[pl.ds(HALO + start, RMAX), :] = low_wide[pl.ds(i, RMAX, stride=pitch), :]
        high_packed[pl.ds(HALO + stop - RMAX, RMAX), :] = high_wide[pl.ds(c, RMAX, stride=pitch), :]
        return start + rad_ref[i], stop - rad_ref[c]

    lax.fori_loop(0, chans, both_ways, (0, total), unroll=16)
    rests = []
    for i, (packed, ref, rest, rest_ref) in enumerate((
        (low_packed, down_ref, low_rest, down_rest_ref), (high_packed, up_ref, high_rest, up_rest_ref)
    )):
        packed[pl.ds(HALO + total, HALO), :] = jnp.zeros((HALO, cols), F32)
        ref[...] = packed[HALO:HALO + cap, :].astype(BF16)
        rests.append(pltpu.make_async_copy(rest, rest_ref, sems.at[3 + i]))

    @pl.when(total > cap)
    def _():
        for packed, rest, copy in ((low_packed, low_rest, rests[0]), (high_packed, high_rest, rests[1])):
            rest[...] = packed[HALO + cap:HALO + full, :].astype(BF16)
            copy.start()
            copy.wait()

    over_ref[0] = jnp.where(total > cap, 1, 0)


def cap_of(chans):
    return RMAX * chans * 5 // 8 // 16 * 16


def gather(radii, x):
    rows, chans, cols = x.shape
    full, cap = RMAX * chans, cap_of(chans)
    head, rest = pltpu.VMEM((cap, cols), BF16), jax.ShapeDtypeStruct((full - cap, cols), BF16)
    return pl.pallas_call(
        gather_kernel,
        out_shape=[pltpu.SMEM((1,), jnp.int32), head, rest, head, rest],
        in_specs=[SMEM, HBM],
        out_specs=[SMEM] + [VMEM, HBM] * 2,
        scratch_shapes=[pltpu.VMEM((RMAX, chans, cols), BF16)] * 2
        + [pltpu.VMEM(((RMAX + 1) * (chans + PAD), cols), F32)] * 2
        + [pltpu.VMEM((full + 2 * HALO, cols), F32)] * 2
        + [pltpu.VMEM(rest.shape, BF16)] * 2
        + [pltpu.SemaphoreType.DMA((5,))],
        compiler_params=PARAMS,
        cost_estimate=pl.CostEstimate(flops=1, bytes_accessed=1, transcendentals=0),
    )(radii, x)


def pack_kernel(sides, order_ref, source_ref, *refs):
    edge_refs, (x_ref, sems) = refs[:3 * sides], refs[3 * sides:]
    rows, chans, cols = x_ref.shape
    starts, left_over, shared = row_groups(rows)
    edge, tail = EDGE * SLOTS, rows - EDGE * SLOTS
    middle = starts[-EDGE - 1] + SLOTS
    spans = [(middle, tail - middle), (0, edge), (edge, middle - edge), (tail, edge)]
    loads = [
        pltpu.make_async_copy(source_ref.at[pl.ds(start, n)], x_ref.at[pl.ds(start, n)], sems.at[i])
        for i, (start, n) in enumerate(spans)
    ]
    for load in loads:
        load.start()
    loads[0].wait()
    dec = lax.axis_index("dec")
    lane = lax.broadcasted_iota(jnp.int32, (chans, LANES), 1)
    for side in range(sides):
        edge_ref, low_ref, high_ref = edge_refs[3 * side:3 * side + 3]
        if sides == 1:
            first = jnp.where(dec == 0, cols - RMAX, 0)
        else:
            first = cols - RMAX if side == 0 else 0

        def moved(row, lane_of_first):
            return pltpu.roll(x_ref[row].astype(F32), lax.rem(lane_of_first - first + 2 * LANES, LANES), 1)

        tiles = []
        for g, start in enumerate(starts):
            if side == 0 and start in (0, edge, tail):
                loads[(0, edge, tail).index(start) + 1].wait()
            packed = moved(start, 0)
            for j in range(1, SLOTS):
                packed = jnp.where(lane < RMAX * j, packed, moved(start + j, RMAX * j))
            for row, tile in left_over:
                if g in (tile, tile + 1):
                    packed = jnp.where(lane < LANES - SPARE, packed, moved(row, LANES - SPARE - SPARE * (g - tile)))
            edge_ref[g * chans:(g + 1) * chans, :] = packed.astype(BF16)
            tiles.append(packed)
        half = chans // 2

        def beside(part, low):
            return jnp.where((lane[:half] < LANES // 2) == low, part[:half], pltpu.roll(part[half:], LANES // 2, 1))

        packed = jnp.zeros((chans, LANES), F32)
        for j, row in enumerate(shared):
            packed = jnp.where(lane < RMAX * j, packed, moved(row, RMAX * j))
        edge_ref[len(starts) * chans:, :] = beside(packed, True).astype(BF16)
        for ref, whole, part in (
            (low_ref, tiles[:EDGE - 1], beside(tiles[EDGE - 1], True)),
            (high_ref, tiles[1 - EDGE:], beside(tiles[-EDGE], False)),
        ):
            for i, tile in enumerate(whole):
                ref[i * chans:(i + 1) * chans, :] = tile.astype(BF16)
            ref[(EDGE - 1) * chans:, :] = part.astype(BF16)


def pack(x, sides, order):
    rows, chans, cols = x.shape
    packed = [pltpu.VMEM((len(row_groups(rows)[0]) * chans + chans // 2, LANES), BF16)]
    packed += [pltpu.VMEM(((EDGE - 1) * chans + chans // 2, LANES), BF16)] * 2
    return pl.pallas_call(
        functools.partial(pack_kernel, sides),
        out_shape=packed * sides,
        in_specs=[SMEM, HBM],
        out_specs=[VMEM] * (3 * sides),
        scratch_shapes=[pltpu.VMEM(x.shape, BF16), pltpu.SemaphoreType.DMA((4,))],
        compiler_params=PARAMS,
        cost_estimate=pl.CostEstimate(flops=1, bytes_accessed=1, transcendentals=0),
    )(order, x)


def widen(tiles, j):
    lane = lax.broadcasted_iota(jnp.int32, tiles[0].shape, 1)
    value = None
    for side, part in enumerate(tiles):
        shift = (RMAX * side - RMAX * j) % LANES
        part = part if shift == 0 else pltpu.roll(part, shift, 1)
        value = part if side == 0 else jnp.where(lane < RMAX, value, part)
    return value


def inner_kernel(sides, rad_ref, own, dec_ref, ra_ref, *refs):
    edge_refs, (out_ref, begun, halo, result) = refs[:sides], refs[sides:]
    inner, chans, cols = out_ref.shape
    rows = inner + 2 * RMAX
    pitch = chans + PAD
    own_rows = ra_ref.shape[2]
    base = ra_ref.shape[1] - 2 * HALO

    starts, left_over, shared = row_groups(rows)
    for g, start in enumerate(starts):
        tiles = [ref[g * chans:(g + 1) * chans, :].astype(F32) for ref in edge_refs]
        for j in range(SLOTS):
            halo[pl.ds((start + j) * pitch, chans), :] = widen(tiles, j)
    lane = lax.broadcasted_iota(jnp.int32, (chans, LANES), 1)
    for row, g in left_over:
        tiles = []
        for ref in edge_refs:
            begin, end = (
                pltpu.roll(ref[(g + i) * chans:(g + i + 1) * chans, :].astype(F32), SPARE * (1 + i), 1) for i in range(2)
            )
            tiles.append(jnp.where(lane < SPARE, begin, end))
        halo[pl.ds(row * pitch, chans), :] = widen(tiles, 0)
    tiles = [ref[len(starts) * chans:, :].astype(F32) for ref in edge_refs]
    tiles = [jnp.concatenate([tile, pltpu.roll(tile, LANES // 2, 1)], 0) for tile in tiles]
    for j, row in enumerate(shared):
        halo[pl.ds(row * pitch, chans), :] = widen(tiles, j)

    for i in range(rows, own_rows):
        halo[pl.ds(i * pitch, chans), :] = jnp.zeros((chans, cols), F32)

    radii = [rad_ref[c] for c in range(chans)]
    partials = []
    for c, radius in enumerate(radii):
        picked = pl.ds(c, own_rows, stride=pitch)
        lhs = jnp.concatenate([own[picked, :].astype(BF16), halo[picked, :].astype(BF16)], 1)
        partials.append(jnp.dot(lhs, dec_ref[radius], preferred_element_type=F32).astype(BF16))
    for c, (radius, partial) in enumerate(zip(radii, partials)):
        smoothed = jnp.dot(ra_ref[radius], partial, preferred_element_type=F32)
        result[pl.ds(c, inner, stride=pitch), :] = smoothed[:inner]
        begun[pl.ds(c, RMAX, stride=pitch), :] = smoothed[base:base + RMAX]
        begun[pl.ds(RMAX * pitch + c, RMAX, stride=pitch), :] = smoothed[base + HALO:base + HALO + RMAX]

    def store(i, carry):
        out_ref[i] = result[pl.ds(i * pitch, chans), :].astype(BF16)
        return carry

    lax.fori_loop(0, inner, store, 0)


def smooth_inner(radii, rows, own, halos, dec_table, ra_table):
    chans, cols = radii.shape[0], own.shape[1]
    pitch, own_rows, inner = chans + PAD, ra_table.shape[2], rows - 2 * RMAX
    operands = [own, dec_table, ra_table, *halos]
    return pl.pallas_call(
        functools.partial(inner_kernel, len(halos)),
        out_shape=[
            pltpu.VMEM((inner, chans, cols), BF16),
            pltpu.VMEM(((2 * RMAX + 1) * pitch, cols), F32),
        ],
        in_specs=[SMEM] + [VMEM] * len(operands),
        out_specs=[VMEM] * 2,
        scratch_shapes=[
            pltpu.VMEM(((own_rows + 1) * pitch, LANES), F32),
            pltpu.VMEM(((inner + 1) * pitch, cols), F32),
        ],
        compiler_params=PARAMS,
        cost_estimate=pl.CostEstimate(flops=1, bytes_accessed=1, transcendentals=0),
    )(radii, *operands)


def reach_lanes(sides):
    return -(-sides * RMAX // 16) * 16


def outer_begin_kernel(rad_ref, order_ref, before_ref, before_rest, after_ref, after_rest, dec_ref, begun, before, after):
    chans, _, cols = begun.shape
    radii = [rad_ref[c] for c in range(chans)]
    total = functools.reduce(lambda a, b: a + b, radii)
    cap = before_ref.shape[0]
    for packed, head, rest in ((before, before_ref, before_rest), (after, after_ref, after_rest)):
        packed[:HALO, :] = jnp.zeros((HALO, cols), F32)
        packed[HALO:HALO + cap, :] = head[...].astype(F32)
        packed[HALO + cap:2 * HALO + cap, :] = jnp.zeros((HALO, cols), F32)
        packed[packed.shape[0] - HALO:, :] = jnp.zeros((HALO, cols), F32)

        @pl.when(total > cap)
        def _():
            packed[HALO + cap:HALO + cap + rest.shape[0], :] = rest[...].astype(F32)

    offset = 0
    for c, radius in enumerate(radii):
        planes = [
            before[pl.ds(HALO - RMAX + offset + radius, HALO), :],
            after[pl.ds(HALO + offset, HALO), :],
        ]
        lhs = jnp.concatenate(planes, 0).astype(BF16)
        begun[c] = jnp.dot(lhs, dec_ref[radius, :cols, :], preferred_element_type=F32)
        offset = offset + radius


def outer_begin(radii, order, before, after, dec_table):
    chans, cols = radii.shape[0], dec_table.shape[2]
    operands = [*before, *after, dec_table]
    return pl.pallas_call(
        outer_begin_kernel,
        out_shape=pltpu.VMEM((chans, 2 * HALO, cols), F32),
        in_specs=[SMEM, pl.BlockSpec(memory_space=pl.ANY)] + [VMEM] * len(operands),
        out_specs=VMEM,
        scratch_shapes=[pltpu.VMEM((RMAX * chans + 2 * HALO, cols), F32)] * 2,
        compiler_params=PARAMS,
        cost_estimate=pl.CostEstimate(flops=2 * 10**9, bytes_accessed=5 * 10**6, transcendentals=0),
    )(radii, order, *operands)


def outer_kernel(sides, rad_ref, dec_begun, ra_begun, dec_ref, ra_ref, *refs):
    corner_refs, (out_ref, corner, result) = refs[:2 * sides], refs[2 * sides:]
    rows, chans, cols = out_ref.shape
    pitch = chans + PAD
    width = reach_lanes(sides)

    for part, base in ((0, 0), (1, HALO)):
        starts = [g * SLOTS if part else g * SLOTS + RMAX - EDGE * SLOTS for g in range(EDGE)]
        shared = EDGE - 1 if part else 0
        order = [*range(EDGE - 1), EDGE - 1] if part else [EDGE - 1, *range(EDGE - 1)]
        for g, (start, place) in enumerate(zip(starts, order)):
            tiles = []
            for ref in corner_refs[part::2]:
                tile = ref[place * chans:min(place * chans + chans, ref.shape[0]), :].astype(F32)
                if g == shared:
                    tile = jnp.concatenate([tile, pltpu.roll(tile, LANES // 2, 1)], 0)
                tiles.append(tile)
            for j in range(SLOTS):
                if 0 <= start + j < RMAX:
                    corner[pl.ds((base + start + j) * pitch, chans), :] = widen(tiles, j)
        for row in range(RMAX, HALO):
            corner[pl.ds((base + row) * pitch, chans), :] = jnp.zeros((chans, LANES), F32)

    radii = [rad_ref[c] for c in range(chans)]
    partials = []
    for c, radius in enumerate(radii):
        lhs = corner[pl.ds(c, 2 * HALO, stride=pitch), :].astype(BF16)[:, :width]
        partial = jnp.dot(lhs, dec_ref[radius, cols:cols + width, :], preferred_element_type=F32) + dec_begun[c]
        partials.append(partial.astype(BF16))
    for c, (radius, partial) in enumerate(zip(radii, partials)):
        smoothed = jnp.dot(ra_ref[radius], partial, preferred_element_type=F32)
        result[pl.ds(c, RMAX, stride=pitch), :] = smoothed[:RMAX]
        result[pl.ds(RMAX * pitch + c, RMAX, stride=pitch), :] = smoothed[HALO:HALO + RMAX]

    def store(i, carry):
        picked = pl.ds(i * pitch, chans)
        out_ref[i] = (ra_begun[picked, :] + result[picked, :]).astype(BF16)
        return carry

    lax.fori_loop(0, rows, store, 0)


def smooth_outer(radii, dec_begun, ra_begun, dec_table, ra_table, corners):
    chans, _, cols = dec_begun.shape
    pitch = chans + PAD
    operands = [dec_begun, ra_begun, dec_table, ra_table] + [part for side in corners for part in side]
    return pl.pallas_call(
        functools.partial(outer_kernel, len(corners)),
        out_shape=pltpu.VMEM((2 * RMAX, chans, cols), BF16),
        in_specs=[SMEM] + [VMEM] * len(operands),
        out_specs=VMEM,
        scratch_shapes=[
            pltpu.VMEM(((2 * HALO + 1) * pitch, LANES), F32),
            pltpu.VMEM(((2 * RMAX + 1) * pitch, cols), F32),
        ],
        compiler_params=PARAMS,
        cost_estimate=pl.CostEstimate(flops=10**10, bytes_accessed=5 * 10**6, transcendentals=0),
    )(radii, *operands)


SUM_ROWS = 8


def add_products(total, row_refs, own_ref, valid_ref, first_row, rows, sums=None):
    depth = max(d for d in range(1, 27) if rows % d == 0)

    def nt(a, b):
        return lax.dot_general(a, b, (((1,), (1,)), ((), ())), preferred_element_type=F32)

    def body(i, carry):
        picked = [i * depth + j for j in range(depth)]
        line = jnp.concatenate([valid_ref[pl.ds(first_row(r), 1), :].astype(BF16) for r in picked], 1)
        own, *others = (jnp.concatenate([ref[r] for r in picked], 1) for ref in (own_ref, *row_refs))
        total[...] += nt(jnp.concatenate(others, 0), own * line)
        if sums is not None:
            sums[...] += nt(jnp.broadcast_to(line, (16, line.shape[1])), own)[:SUM_ROWS]
        return carry

    lax.fori_loop(0, rows // depth, body, 0)


def outer_row(image_rows):
    return lambda r: jnp.where(r < RMAX, r, r + image_rows - 2 * RMAX)


def own_gram_kernel(own_ref, other_ref, outer_ref, valid_ref, out_ref, cross_ref, smoothed_ref, both, sems):
    rows, chans = valid_ref.shape[0], own_ref.shape[1]
    half = chans // 2
    copies = [
        pltpu.make_async_copy(source, smoothed_ref.at[pl.ds(start, source.shape[0])], sems.at[i])
        for i, (source, start) in enumerate((
            (own_ref, RMAX),
            (outer_ref.at[pl.ds(0, RMAX)], 0),
            (outer_ref.at[pl.ds(RMAX, RMAX)], rows - RMAX),
        ))
    ]
    for copy in copies:
        copy.start()
    both[...] = jnp.zeros_like(both)
    products, own, sums = both.at[:2 * chans], both.at[:chans], both.at[2 * chans:]
    add_products(products, (own_ref, other_ref), own_ref, valid_ref, lambda r: r + RMAX, own_ref.shape[0], sums)
    add_products(own, (outer_ref,), outer_ref, valid_ref, outer_row(rows), 2 * RMAX, sums)
    cross_ref[...] = both[chans:2 * chans, :]
    low = pltpu.roll(both[half:chans, :], half, 1)
    row = lax.broadcasted_iota(jnp.int32, (half, chans), 0)
    lane = lax.broadcasted_iota(jnp.int32, (half, chans), 1)
    out_ref[:half, :] = jnp.where(lane < row, low, both[:half, :])
    diagonal = jnp.sum(jnp.where(lane == row, low, 0.0), axis=0, keepdims=True)
    row = lax.broadcasted_iota(jnp.int32, (SUM_ROWS, chans), 0)
    tail = jnp.where(row == 1, diagonal, both[2 * chans:, :])
    out_ref[half:, :] = jnp.where(row == 2, jnp.sum(valid_ref[...].astype(F32)), tail)
    for copy in copies:
        copy.wait()


def own_gram(own, other, outer, valid):
    _, chans, cols = own.shape
    return pl.pallas_call(
        own_gram_kernel,
        out_shape=[
            pltpu.VMEM((chans // 2 + SUM_ROWS, chans), F32),
            pltpu.VMEM((chans, chans), F32),
            jax.ShapeDtypeStruct((valid.shape[0], chans, cols), BF16),
        ],
        in_specs=[VMEM] * 4,
        out_specs=[VMEM, VMEM, HBM],
        scratch_shapes=[pltpu.VMEM((2 * chans + SUM_ROWS, chans), F32), pltpu.SemaphoreType.DMA((3,))],
        compiler_params=PARAMS,
        cost_estimate=pl.CostEstimate(flops=10**9, bytes_accessed=3 * 10**6, transcendentals=0),
    )(own, other, outer, valid)


def cross_gram_kernel(folded_ref, cross_ref, own_ref, other_ref, valid_ref, out_ref, total):
    chans = own_ref.shape[1]
    half = chans // 2
    total[...] = cross_ref[...]
    add_products(total, (other_ref,), own_ref, valid_ref, outer_row(valid_ref.shape[0]), 2 * RMAX)
    cross = total[...]
    out_ref[:half, :] = folded_ref[:half, :]
    out_ref[half:chans, :] = jnp.where(lax.axis_index("band") == 0, cross[:half], jnp.transpose(cross)[half:])
    out_ref[chans:, :] = folded_ref[half:, :]


def cross_gram(folded, cross, own, other, valid):
    chans = own.shape[1]
    return pl.pallas_call(
        cross_gram_kernel,
        out_shape=pltpu.VMEM((chans + SUM_ROWS, chans), F32),
        in_specs=[VMEM] * 5,
        out_specs=VMEM,
        scratch_shapes=[pltpu.VMEM((chans, chans), F32)],
        compiler_params=PARAMS,
    )(folded, cross, own, other, valid)


def finish_kernel(mine_ref, theirs_ref, mean_ref, cov_ref):
    chans = mine_ref.shape[1]
    half = chans // 2
    band = lax.axis_index("band")
    count = mine_ref[chans + 2:chans + 3, :1]
    folded = mine_ref[:half, :]
    mirror = jnp.transpose(jnp.concatenate([folded, jnp.zeros((half, chans), F32)], 0))
    row = lax.broadcasted_iota(jnp.int32, (half, chans), 0)
    lane = lax.broadcasted_iota(jnp.int32, (half, chans), 1)
    upper = jnp.where(lane < row, mirror[:half], folded)
    column = lane - half
    corner = jnp.where(column < row, pltpu.roll(folded, half, 1), pltpu.roll(mirror[:half], half, 1))
    corner = jnp.where(column == row, pltpu.roll(mine_ref[chans:chans + SUM_ROWS, :], half, 1)[1:2, :], corner)
    own = jnp.concatenate([upper, jnp.where(column < 0, mirror[half:], corner)], 0)
    mine, theirs = mine_ref[half:chans, :], theirs_ref[half:chans, :]
    cross = jnp.concatenate([jnp.where(band == 0, mine, theirs), jnp.where(band == 0, theirs, mine)], 0)
    cross = jnp.where(band == 0, cross, jnp.transpose(cross))
    mean = mine_ref[chans:chans + 1, :] / count
    other_mean = theirs_ref[chans:chans + 1, :] / count
    mean_ref[...] = mean
    for block, left, b in ((own, mean, band), (cross, other_mean, 1 - band)):
        left = jnp.transpose(jnp.broadcast_to(left, (chans, chans)))
        cov_ref[pl.ds(pl.multiple_of(b * chans, chans), chans), :] = (block - count * left * mean) / (count - 1.0)


def finish(mine, theirs):
    chans = mine.shape[1]
    mean, covariance = pl.pallas_call(
        finish_kernel,
        out_shape=[jax.ShapeDtypeStruct((1, chans), F32), jax.ShapeDtypeStruct((2 * chans, chans), F32)],
        in_specs=[VMEM] * 2,
        out_specs=[VMEM] * 2,
        compiler_params=PARAMS,
    )(mine, theirs)
    return mean.reshape(chans), covariance


def swap(array, axis, step):
    size = lax.axis_size(axis)
    return lax.ppermute(array, axis, [(i, i ^ step) for i in range(size)])


def diagonal(array, ra_step, dec_pairs):
    ra_size, dec_size = lax.axis_size("ra"), lax.axis_size("dec")
    pairs = [
        (i * dec_size + a, (i + ra_step) % ra_size * dec_size + b) for i in range(ra_size) for a, b in dec_pairs
    ]
    return lax.ppermute(array, ("ra", "dec"), pairs)


def per_device(sky_maps, radii, valid):
    x = jnp.transpose(sky_maps, (1, 0, 2))
    radii = pltpu.with_memory_space_constraint(radii, pltpu.HBM)
    x = pltpu.with_memory_space_constraint(x, pltpu.HBM)
    rows, chans, cols = x.shape
    ra_size, dec_size = lax.axis_size("ra"), lax.axis_size("dec")
    up = [(i, (i + 1) % ra_size) for i in range(ra_size)]
    down = [(j, i) for i, j in up]
    right = [(i, i + 1) for i in range(dec_size - 1)]
    left = [(j, i) for i, j in right]
    sides = [right + left] if dec_size == 2 else [right, left]
    over, up_head, up_rest, down_head, down_rest = gather(radii, x)
    packed = pack(x, len(sides), over)
    before_rest, after_rest = lax.switch(
        over[0],
        [lambda a, b: (a, b), lambda a, b: (lax.ppermute(a, "ra", up), lax.ppermute(b, "ra", down))],
        up_rest, down_rest,
    )
    before, after = lax.ppermute(up_head, "ra", up), lax.ppermute(down_head, "ra", down)
    packed = [packed[3 * i:3 * i + 3] for i in range(len(sides))]
    halos = [lax.ppermute(p, "dec", pairs) for (p, _, _), pairs in zip(packed, sides)]
    corners = [
        (diagonal(high, 1, pairs), diagonal(low, -1, pairs)) for (_, low, high), pairs in zip(packed, sides)
    ]
    dec_table, inner_table, outer_table, own = tables(x, len(sides), before_rest)
    inner, begun = smooth_inner(radii, rows, own, halos, dec_table, inner_table)
    dec_begun = outer_begin(radii, begun, (before, before_rest), (after, after_rest), dec_table)
    outer = smooth_outer(radii, dec_begun, begun, dec_table, outer_table, corners)
    folded, cross, smoothed = own_gram(inner, swap(inner, "band", 1), outer, valid)
    total = cross_gram(folded, cross, outer, swap(outer, "band", 1), valid)
    steps = [("dec", 1 << b) for b in range(dec_size.bit_length() - 1)]
    steps += [("ra", 1 << b) for b in range(ra_size.bit_length() - 1)]
    for axis, step in steps:
        total = total + swap(total, axis, step)
    mean, covariance = finish(total, swap(total, "band", 1))
    return (jnp.transpose(smoothed, (1, 0, 2)), mean, covariance)


def solution(mesh):
    return jax.shard_map(
        per_device,
        mesh=mesh,
        in_specs=(
            P(("groups", "band"), "ra", "dec"),
            P(("groups", "band")),
            P(("groups", "ra"), "dec"),
        ),
        out_specs=(P(("groups", "band"), "ra", "dec"), P(("groups", "band")), P("groups", "band")),
        check_vma=False,
    )
```

```python
import functools

import jax
import jax.numpy as jnp
from jax import lax
from jax.experimental import pallas as pl
from jax.experimental.pallas import tpu as pltpu
from jax.sharding import PartitionSpec as P

RMAX = 17
LANES = 128
SLOTS = LANES // RMAX
EDGE = -(-RMAX // SLOTS)
PAD = 8
HALO = 24
VMEM_LIMIT = 32 * 1024 * 1024
BF16, F32 = jnp.bfloat16, jnp.float32
VMEM = pl.BlockSpec(memory_space=pltpu.VMEM)
SMEM = pl.BlockSpec(memory_space=pltpu.SMEM)
HBM = pl.BlockSpec(memory_space=pltpu.HBM)
PARAMS = pltpu.CompilerParams(vmem_limit_bytes=VMEM_LIMIT)


SPARE = LANES - SLOTS * RMAX


def row_groups(rows):
    middle = rows - 2 * EDGE * SLOTS
    small = LANES // 2 // RMAX
    count = min(n for n in range(middle + 1) if middle - n * SLOTS <= (2 * EDGE + n) // 2 + small)
    starts = [g * SLOTS for g in range(EDGE + count)] + [rows - (EDGE - g) * SLOTS for g in range(EDGE)]
    rest = list(range((EDGE + count) * SLOTS, rows - EDGE * SLOTS))
    left_over = [(row, 2 * i) for i, row in enumerate(rest[small:])]
    return starts, left_over, rest[:small]


def tables_kernel(sides, order_ref, x_ref, dec_ref, inner_ref, outer_ref, own, x, sem, *offset_refs):
    rows, chans, cols = x_ref.shape
    load = pltpu.make_async_copy(x_ref, x, sem)
    load.start()
    dec = lax.axis_index("dec")

    def offsets(offset_ref, used, offset):
        offset_ref[...] = jnp.where(used, offset, 2 * LANES).astype(F32)

    def grid(ref):
        return [lax.broadcasted_iota(jnp.int32, ref.shape, d) for d in (0, 1)]

    z, y = grid(offset_refs[0])
    before, after = z - cols - RMAX, z
    if sides == 1:
        column = jnp.where(z < cols, z, jnp.where(dec == 0, after, before))
    else:
        column = jnp.where(z < cols, z, jnp.where(z < cols + RMAX, before, after - RMAX))
    offsets(offset_refs[0], z < cols + sides * RMAX, column - y)
    out, source = grid(offset_refs[1])
    edge = out - (offset_refs[1].shape[0] - 2 * HALO)
    row = jnp.where(edge < 0, out + RMAX, jnp.where(edge < HALO, edge, edge - HALO + rows - RMAX))
    offsets(offset_refs[1], source < rows, source - row)
    out, source = grid(offset_refs[2])
    row = jnp.where(out < HALO, out, out - HALO + rows - RMAX)
    tail = source - HALO
    offsets(
        offset_refs[2], (source < RMAX) | ((tail >= 0) & (tail < RMAX)), jnp.where(tail < 0, source - RMAX, tail + rows) - row
    )
    line = (lax.broadcasted_iota(jnp.int32, (8, LANES), 1) - RMAX).astype(F32)

    def one_radius(index, carry):
        radius = jnp.full((8, LANES), index, jnp.int32).astype(F32)
        spread = 0.5 * radius
        scale = -1.0 / (2.0 * spread * spread)
        raw = jnp.where(jnp.abs(line) <= radius, jnp.exp(line * line * scale), 0.0)
        inverse = 1.0 / jnp.sum(raw, axis=1, keepdims=True)
        limit, scale, inverse = radius[:1, :1], scale[:1, :1], inverse[:1]
        for ref, offset_ref in zip((dec_ref, inner_ref, outer_ref), offset_refs):
            offset = offset_ref[...]
            taps = jnp.where(jnp.abs(offset) <= limit, jnp.exp(offset * offset * scale) * inverse, 0.0)
            ref[index] = taps.astype(BF16)
        return carry

    lax.fori_loop(1, RMAX + 1, one_radius, 0, unroll=True)
    pitch = chans + PAD

    def copy_row(i, carry):
        own[pl.ds(i * pitch, chans), :] = x[i].astype(F32)
        return carry

    load.wait()
    lax.fori_loop(0, rows, copy_row, 0, unroll=6)
    for i in range(rows, inner_ref.shape[2]):
        own[pl.ds(i * pitch, chans), :] = jnp.zeros((chans, cols), F32)


def tables(x, sides, order):
    rows, chans, cols = x.shape
    own = -(-rows // 16) * 16
    inner = -(-(rows - 2 * RMAX) // 16) * 16
    shapes = [(cols + LANES, cols), (inner + 2 * HALO, own), (2 * HALO, 2 * HALO)]
    return pl.pallas_call(
        functools.partial(tables_kernel, sides),
        out_shape=[pltpu.VMEM((RMAX + 1, *shape), BF16) for shape in shapes]
        + [pltpu.VMEM(((own + 1) * (chans + PAD), cols), F32)],
        in_specs=[pl.BlockSpec(memory_space=pl.ANY), HBM],
        out_specs=[VMEM] * 4,
        scratch_shapes=[pltpu.VMEM(x.shape, BF16), pltpu.SemaphoreType.DMA] + [pltpu.VMEM(shape, F32) for shape in shapes],
        compiler_params=PARAMS,
        cost_estimate=pl.CostEstimate(flops=10**5, bytes_accessed=10**5, transcendentals=0),
    )(order, x)


def gather_kernel(rad_ref, source_ref, over_ref, up_ref, up_rest_ref, down_ref, down_rest_ref, low, high, low_wide, high_wide, low_packed, high_packed, low_rest, high_rest, sems):
    rows, chans, cols = source_ref.shape
    pitch = chans + PAD
    cap, full = up_ref.shape[0], RMAX * chans
    copies = [
        pltpu.make_async_copy(source_ref.at[pl.ds(start, RMAX)], ref, sems.at[i])
        for i, (start, ref) in enumerate(((0, low), (rows - RMAX, high)))
    ]
    for copy in copies:
        copy.start()
    for copy, ref, wide in zip(copies, (low, high), (low_wide, high_wide)):
        copy.wait()
        for i in range(RMAX):
            wide[pl.ds(i * pitch, chans), :] = ref[i].astype(F32)

    total = 0
    for c in range(chans):
        total = total + rad_ref[c]

    def both_ways(i, carry):
        start, stop = carry
        c = chans - 1 - i
        low_packed[pl.ds(HALO + start, RMAX), :] = low_wide[pl.ds(i, RMAX, stride=pitch), :]
        high_packed[pl.ds(HALO + stop - RMAX, RMAX), :] = high_wide[pl.ds(c, RMAX, stride=pitch), :]
        return start + rad_ref[i], stop - rad_ref[c]

    lax.fori_loop(0, chans, both_ways, (0, total), unroll=16)
    rests = []
    for i, (packed, ref, rest, rest_ref) in enumerate((
        (low_packed, down_ref, low_rest, down_rest_ref), (high_packed, up_ref, high_rest, up_rest_ref)
    )):
        packed[pl.ds(HALO + total, HALO), :] = jnp.zeros((HALO, cols), F32)
        ref[...] = packed[HALO:HALO + cap, :].astype(BF16)
        rests.append(pltpu.make_async_copy(rest, rest_ref, sems.at[3 + i]))

    @pl.when(total > cap)
    def _():
        for packed, rest, copy in ((low_packed, low_rest, rests[0]), (high_packed, high_rest, rests[1])):
            rest[...] = packed[HALO + cap:HALO + full, :].astype(BF16)
            copy.start()
            copy.wait()

    over_ref[0] = jnp.where(total > cap, 1, 0)


def cap_of(chans):
    return RMAX * chans * 5 // 8 // 16 * 16


def gather(radii, x):
    rows, chans, cols = x.shape
    full, cap = RMAX * chans, cap_of(chans)
    head, rest = pltpu.VMEM((cap, cols), BF16), jax.ShapeDtypeStruct((full - cap, cols), BF16)
    return pl.pallas_call(
        gather_kernel,
        out_shape=[pltpu.SMEM((1,), jnp.int32), head, rest, head, rest],
        in_specs=[SMEM, HBM],
        out_specs=[SMEM] + [VMEM, HBM] * 2,
        scratch_shapes=[pltpu.VMEM((RMAX, chans, cols), BF16)] * 2
        + [pltpu.VMEM(((RMAX + 1) * (chans + PAD), cols), F32)] * 2
        + [pltpu.VMEM((full + 2 * HALO, cols), F32)] * 2
        + [pltpu.VMEM(rest.shape, BF16)] * 2
        + [pltpu.SemaphoreType.DMA((5,))],
        compiler_params=PARAMS,
        cost_estimate=pl.CostEstimate(flops=1, bytes_accessed=1, transcendentals=0),
    )(radii, x)


def pack_kernel(sides, order_ref, source_ref, *refs):
    edge_refs, (x_ref, sems) = refs[:3 * sides], refs[3 * sides:]
    rows, chans, cols = x_ref.shape
    starts, left_over, shared = row_groups(rows)
    edge, tail = EDGE * SLOTS, rows - EDGE * SLOTS
    middle = starts[-EDGE - 1] + SLOTS
    spans = [(middle, tail - middle), (0, edge), (edge, middle - edge), (tail, edge)]
    loads = [
        pltpu.make_async_copy(source_ref.at[pl.ds(start, n)], x_ref.at[pl.ds(start, n)], sems.at[i])
        for i, (start, n) in enumerate(spans)
    ]
    for load in loads:
        load.start()
    loads[0].wait()
    dec = lax.axis_index("dec")
    lane = lax.broadcasted_iota(jnp.int32, (chans, LANES), 1)
    for side in range(sides):
        edge_ref, low_ref, high_ref = edge_refs[3 * side:3 * side + 3]
        if sides == 1:
            first = jnp.where(dec == 0, cols - RMAX, 0)
        else:
            first = cols - RMAX if side == 0 else 0

        def moved(row, lane_of_first):
            return pltpu.roll(x_ref[row].astype(F32), lax.rem(lane_of_first - first + 2 * LANES, LANES), 1)

        tiles = []
        for g, start in enumerate(starts):
            if side == 0 and start in (0, edge, tail):
                loads[(0, edge, tail).index(start) + 1].wait()
            packed = moved(start, 0)
            for j in range(1, SLOTS):
                packed = jnp.where(lane < RMAX * j, packed, moved(start + j, RMAX * j))
            for row, tile in left_over:
                if g in (tile, tile + 1):
                    packed = jnp.where(lane < LANES - SPARE, packed, moved(row, LANES - SPARE - SPARE * (g - tile)))
            edge_ref[g * chans:(g + 1) * chans, :] = packed.astype(BF16)
            tiles.append(packed)
        half = chans // 2

        def beside(part, low):
            return jnp.where((lane[:half] < LANES // 2) == low, part[:half], pltpu.roll(part[half:], LANES // 2, 1))

        packed = jnp.zeros((chans, LANES), F32)
        for j, row in enumerate(shared):
            packed = jnp.where(lane < RMAX * j, packed, moved(row, RMAX * j))
        edge_ref[len(starts) * chans:, :] = beside(packed, True).astype(BF16)
        for ref, whole, part in (
            (low_ref, tiles[:EDGE - 1], beside(tiles[EDGE - 1], True)),
            (high_ref, tiles[1 - EDGE:], beside(tiles[-EDGE], False)),
        ):
            for i, tile in enumerate(whole):
                ref[i * chans:(i + 1) * chans, :] = tile.astype(BF16)
            ref[(EDGE - 1) * chans:, :] = part.astype(BF16)


def pack(x, sides, order):
    rows, chans, cols = x.shape
    packed = [pltpu.VMEM((len(row_groups(rows)[0]) * chans + chans // 2, LANES), BF16)]
    packed += [pltpu.VMEM(((EDGE - 1) * chans + chans // 2, LANES), BF16)] * 2
    return pl.pallas_call(
        functools.partial(pack_kernel, sides),
        out_shape=packed * sides,
        in_specs=[SMEM, HBM],
        out_specs=[VMEM] * (3 * sides),
        scratch_shapes=[pltpu.VMEM(x.shape, BF16), pltpu.SemaphoreType.DMA((4,))],
        compiler_params=PARAMS,
        cost_estimate=pl.CostEstimate(flops=1, bytes_accessed=1, transcendentals=0),
    )(order, x)


def widen(tiles, j):
    lane = lax.broadcasted_iota(jnp.int32, tiles[0].shape, 1)
    value = None
    for side, part in enumerate(tiles):
        shift = (RMAX * side - RMAX * j) % LANES
        part = part if shift == 0 else pltpu.roll(part, shift, 1)
        value = part if side == 0 else jnp.where(lane < RMAX, value, part)
    return value


def inner_kernel(sides, rad_ref, own, dec_ref, ra_ref, *refs):
    edge_refs, (out_ref, begun, halo, result) = refs[:sides], refs[sides:]
    inner, chans, cols = out_ref.shape
    rows = inner + 2 * RMAX
    pitch = chans + PAD
    own_rows = ra_ref.shape[2]
    base = ra_ref.shape[1] - 2 * HALO

    starts, left_over, shared = row_groups(rows)
    for g, start in enumerate(starts):
        tiles = [ref[g * chans:(g + 1) * chans, :].astype(F32) for ref in edge_refs]
        for j in range(SLOTS):
            halo[pl.ds((start + j) * pitch, chans), :] = widen(tiles, j)
    lane = lax.broadcasted_iota(jnp.int32, (chans, LANES), 1)
    for row, g in left_over:
        tiles = []
        for ref in edge_refs:
            begin, end = (
                pltpu.roll(ref[(g + i) * chans:(g + i + 1) * chans, :].astype(F32), SPARE * (1 + i), 1) for i in range(2)
            )
            tiles.append(jnp.where(lane < SPARE, begin, end))
        halo[pl.ds(row * pitch, chans), :] = widen(tiles, 0)
    tiles = [ref[len(starts) * chans:, :].astype(F32) for ref in edge_refs]
    tiles = [jnp.concatenate([tile, pltpu.roll(tile, LANES // 2, 1)], 0) for tile in tiles]
    for j, row in enumerate(shared):
        halo[pl.ds(row * pitch, chans), :] = widen(tiles, j)

    for i in range(rows, own_rows):
        halo[pl.ds(i * pitch, chans), :] = jnp.zeros((chans, cols), F32)

    radii = [rad_ref[c] for c in range(chans)]
    partials = []
    for c, radius in enumerate(radii):
        picked = pl.ds(c, own_rows, stride=pitch)
        lhs = jnp.concatenate([own[picked, :].astype(BF16), halo[picked, :].astype(BF16)], 1)
        partials.append(jnp.dot(lhs, dec_ref[radius], preferred_element_type=F32).astype(BF16))
    for c, (radius, partial) in enumerate(zip(radii, partials)):
        smoothed = jnp.dot(ra_ref[radius], partial, preferred_element_type=F32)
        result[pl.ds(c, inner, stride=pitch), :] = smoothed[:inner]
        begun[pl.ds(c, RMAX, stride=pitch), :] = smoothed[base:base + RMAX]
        begun[pl.ds(RMAX * pitch + c, RMAX, stride=pitch), :] = smoothed[base + HALO:base + HALO + RMAX]

    def store(i, carry):
        out_ref[i] = result[pl.ds(i * pitch, chans), :].astype(BF16)
        return carry

    lax.fori_loop(0, inner, store, 0, unroll=4)


def smooth_inner(radii, rows, own, halos, dec_table, ra_table):
    chans, cols = radii.shape[0], own.shape[1]
    pitch, own_rows, inner = chans + PAD, ra_table.shape[2], rows - 2 * RMAX
    operands = [own, dec_table, ra_table, *halos]
    return pl.pallas_call(
        functools.partial(inner_kernel, len(halos)),
        out_shape=[
            pltpu.VMEM((inner, chans, cols), BF16),
            pltpu.VMEM(((2 * RMAX + 1) * pitch, cols), F32),
        ],
        in_specs=[SMEM] + [VMEM] * len(operands),
        out_specs=[VMEM] * 2,
        scratch_shapes=[
            pltpu.VMEM(((own_rows + 1) * pitch, LANES), F32),
            pltpu.VMEM(((inner + 1) * pitch, cols), F32),
        ],
        compiler_params=PARAMS,
        cost_estimate=pl.CostEstimate(flops=1, bytes_accessed=1, transcendentals=0),
    )(radii, *operands)


def reach_lanes(sides):
    return -(-sides * RMAX // 16) * 16


def outer_begin_kernel(rad_ref, order_ref, before_ref, before_rest, after_ref, after_rest, dec_ref, begun, before, after):
    chans, _, cols = begun.shape
    radii = [rad_ref[c] for c in range(chans)]
    total = functools.reduce(lambda a, b: a + b, radii)
    cap = before_ref.shape[0]
    for packed, head, rest in ((before, before_ref, before_rest), (after, after_ref, after_rest)):
        packed[:HALO, :] = jnp.zeros((HALO, cols), F32)
        packed[HALO:HALO + cap, :] = head[...].astype(F32)
        packed[HALO + cap:2 * HALO + cap, :] = jnp.zeros((HALO, cols), F32)
        packed[packed.shape[0] - HALO:, :] = jnp.zeros((HALO, cols), F32)

        @pl.when(total > cap)
        def _():
            packed[HALO + cap:HALO + cap + rest.shape[0], :] = rest[...].astype(F32)

    offset = 0
    for c, radius in enumerate(radii):
        planes = [
            before[pl.ds(HALO - RMAX + offset + radius, HALO), :],
            after[pl.ds(HALO + offset, HALO), :],
        ]
        lhs = jnp.concatenate(planes, 0).astype(BF16)
        begun[c] = jnp.dot(lhs, dec_ref[radius, :cols, :], preferred_element_type=F32)
        offset = offset + radius


def outer_begin(radii, order, before, after, dec_table):
    chans, cols = radii.shape[0], dec_table.shape[2]
    operands = [*before, *after, dec_table]
    return pl.pallas_call(
        outer_begin_kernel,
        out_shape=pltpu.VMEM((chans, 2 * HALO, cols), F32),
        in_specs=[SMEM, pl.BlockSpec(memory_space=pl.ANY)] + [VMEM] * len(operands),
        out_specs=VMEM,
        scratch_shapes=[pltpu.VMEM((RMAX * chans + 2 * HALO, cols), F32)] * 2,
        compiler_params=PARAMS,
        cost_estimate=pl.CostEstimate(flops=2 * 10**9, bytes_accessed=5 * 10**6, transcendentals=0),
    )(radii, order, *operands)


def outer_kernel(sides, rad_ref, dec_begun, ra_begun, dec_ref, ra_ref, *refs):
    corner_refs, (out_ref, corner, result) = refs[:2 * sides], refs[2 * sides:]
    rows, chans, cols = out_ref.shape
    pitch = chans + PAD
    width = reach_lanes(sides)

    for part, base in ((0, 0), (1, HALO)):
        starts = [g * SLOTS if part else g * SLOTS + RMAX - EDGE * SLOTS for g in range(EDGE)]
        shared = EDGE - 1 if part else 0
        order = [*range(EDGE - 1), EDGE - 1] if part else [EDGE - 1, *range(EDGE - 1)]
        for g, (start, place) in enumerate(zip(starts, order)):
            tiles = []
            for ref in corner_refs[part::2]:
                tile = ref[place * chans:min(place * chans + chans, ref.shape[0]), :].astype(F32)
                if g == shared:
                    tile = jnp.concatenate([tile, pltpu.roll(tile, LANES // 2, 1)], 0)
                tiles.append(tile)
            for j in range(SLOTS):
                if 0 <= start + j < RMAX:
                    corner[pl.ds((base + start + j) * pitch, chans), :] = widen(tiles, j)
        for row in range(RMAX, HALO):
            corner[pl.ds((base + row) * pitch, chans), :] = jnp.zeros((chans, LANES), F32)

    radii = [rad_ref[c] for c in range(chans)]
    partials = []
    for c, radius in enumerate(radii):
        lhs = corner[pl.ds(c, 2 * HALO, stride=pitch), :].astype(BF16)[:, :width]
        partial = jnp.dot(lhs, dec_ref[radius, cols:cols + width, :], preferred_element_type=F32) + dec_begun[c]
        partials.append(partial.astype(BF16))
    for c, (radius, partial) in enumerate(zip(radii, partials)):
        smoothed = jnp.dot(ra_ref[radius], partial, preferred_element_type=F32)
        result[pl.ds(c, RMAX, stride=pitch), :] = smoothed[:RMAX]
        result[pl.ds(RMAX * pitch + c, RMAX, stride=pitch), :] = smoothed[HALO:HALO + RMAX]

    def store(i, carry):
        picked = pl.ds(i * pitch, chans)
        out_ref[i] = (ra_begun[picked, :] + result[picked, :]).astype(BF16)
        return carry

    lax.fori_loop(0, rows, store, 0, unroll=True)


def smooth_outer(radii, dec_begun, ra_begun, dec_table, ra_table, corners):
    chans, _, cols = dec_begun.shape
    pitch = chans + PAD
    operands = [dec_begun, ra_begun, dec_table, ra_table] + [part for side in corners for part in side]
    return pl.pallas_call(
        functools.partial(outer_kernel, len(corners)),
        out_shape=pltpu.VMEM((2 * RMAX, chans, cols), BF16),
        in_specs=[SMEM] + [VMEM] * len(operands),
        out_specs=VMEM,
        scratch_shapes=[
            pltpu.VMEM(((2 * HALO + 1) * pitch, LANES), F32),
            pltpu.VMEM(((2 * RMAX + 1) * pitch, cols), F32),
        ],
        compiler_params=PARAMS,
        cost_estimate=pl.CostEstimate(flops=10**10, bytes_accessed=5 * 10**6, transcendentals=0),
    )(radii, *operands)


SUM_ROWS = 8


def add_products(total, row_refs, own_ref, valid_ref, first_row, rows, sums=None):
    depth = max(d for d in range(1, 27) if rows % d == 0)

    def nt(a, b):
        return lax.dot_general(a, b, (((1,), (1,)), ((), ())), preferred_element_type=F32)

    def body(i, carry):
        picked = [i * depth + j for j in range(depth)]
        line = jnp.concatenate([valid_ref[pl.ds(first_row(r), 1), :].astype(BF16) for r in picked], 1)
        own, *others = (jnp.concatenate([ref[r] for r in picked], 1) for ref in (own_ref, *row_refs))
        total[...] += nt(jnp.concatenate(others, 0), own * line)
        if sums is not None:
            sums[...] += nt(jnp.broadcast_to(line, (16, line.shape[1])), own)[:SUM_ROWS]
        return carry

    lax.fori_loop(0, rows // depth, body, 0, unroll=True)


def outer_row(image_rows):
    return lambda r: jnp.where(r < RMAX, r, r + image_rows - 2 * RMAX)


def own_gram_kernel(own_ref, other_ref, outer_ref, valid_ref, out_ref, cross_ref, smoothed_ref, both, sems):
    rows, chans = valid_ref.shape[0], own_ref.shape[1]
    half = chans // 2
    copies = [
        pltpu.make_async_copy(source, smoothed_ref.at[pl.ds(start, source.shape[0])], sems.at[i])
        for i, (source, start) in enumerate((
            (own_ref, RMAX),
            (outer_ref.at[pl.ds(0, RMAX)], 0),
            (outer_ref.at[pl.ds(RMAX, RMAX)], rows - RMAX),
        ))
    ]
    for copy in copies:
        copy.start()
    both[...] = jnp.zeros_like(both)
    products, own, sums = both.at[:2 * chans], both.at[:chans], both.at[2 * chans:]
    add_products(products, (own_ref, other_ref), own_ref, valid_ref, lambda r: r + RMAX, own_ref.shape[0], sums)
    add_products(own, (outer_ref,), outer_ref, valid_ref, outer_row(rows), 2 * RMAX, sums)
    cross_ref[...] = both[chans:2 * chans, :]
    low = pltpu.roll(both[half:chans, :], half, 1)
    row = lax.broadcasted_iota(jnp.int32, (half, chans), 0)
    lane = lax.broadcasted_iota(jnp.int32, (half, chans), 1)
    out_ref[:half, :] = jnp.where(lane < row, low, both[:half, :])
    diagonal = jnp.sum(jnp.where(lane == row, low, 0.0), axis=0, keepdims=True)
    row = lax.broadcasted_iota(jnp.int32, (SUM_ROWS, chans), 0)
    tail = jnp.where(row == 1, diagonal, both[2 * chans:, :])
    out_ref[half:, :] = jnp.where(row == 2, jnp.sum(valid_ref[...].astype(F32)), tail)
    for copy in copies:
        copy.wait()


def own_gram(own, other, outer, valid):
    _, chans, cols = own.shape
    return pl.pallas_call(
        own_gram_kernel,
        out_shape=[
            pltpu.VMEM((chans // 2 + SUM_ROWS, chans), F32),
            pltpu.VMEM((chans, chans), F32),
            jax.ShapeDtypeStruct((valid.shape[0], chans, cols), BF16),
        ],
        in_specs=[VMEM] * 4,
        out_specs=[VMEM, VMEM, HBM],
        scratch_shapes=[pltpu.VMEM((2 * chans + SUM_ROWS, chans), F32), pltpu.SemaphoreType.DMA((3,))],
        compiler_params=PARAMS,
        cost_estimate=pl.CostEstimate(flops=10**9, bytes_accessed=3 * 10**6, transcendentals=0),
    )(own, other, outer, valid)


def cross_gram_kernel(folded_ref, cross_ref, own_ref, other_ref, valid_ref, out_ref, total):
    chans = own_ref.shape[1]
    half = chans // 2
    total[...] = cross_ref[...]
    add_products(total, (other_ref,), own_ref, valid_ref, outer_row(valid_ref.shape[0]), 2 * RMAX)
    cross = total[...]
    out_ref[:half, :] = folded_ref[:half, :]
    out_ref[half:chans, :] = jnp.where(lax.axis_index("band") == 0, cross[:half], jnp.transpose(cross)[half:])
    out_ref[chans:, :] = folded_ref[half:, :]


def cross_gram(folded, cross, own, other, valid):
    chans = own.shape[1]
    return pl.pallas_call(
        cross_gram_kernel,
        out_shape=pltpu.VMEM((chans + SUM_ROWS, chans), F32),
        in_specs=[VMEM] * 5,
        out_specs=VMEM,
        scratch_shapes=[pltpu.VMEM((chans, chans), F32)],
        compiler_params=PARAMS,
    )(folded, cross, own, other, valid)


def finish_kernel(mine_ref, theirs_ref, mean_ref, cov_ref):
    chans = mine_ref.shape[1]
    half = chans // 2
    band = lax.axis_index("band")
    count = mine_ref[chans + 2:chans + 3, :1]
    folded = mine_ref[:half, :]
    mirror = jnp.transpose(jnp.concatenate([folded, jnp.zeros((half, chans), F32)], 0))
    row = lax.broadcasted_iota(jnp.int32, (half, chans), 0)
    lane = lax.broadcasted_iota(jnp.int32, (half, chans), 1)
    upper = jnp.where(lane < row, mirror[:half], folded)
    column = lane - half
    corner = jnp.where(column < row, pltpu.roll(folded, half, 1), pltpu.roll(mirror[:half], half, 1))
    corner = jnp.where(column == row, pltpu.roll(mine_ref[chans:chans + SUM_ROWS, :], half, 1)[1:2, :], corner)
    own = jnp.concatenate([upper, jnp.where(column < 0, mirror[half:], corner)], 0)
    mine, theirs = mine_ref[half:chans, :], theirs_ref[half:chans, :]
    cross = jnp.concatenate([jnp.where(band == 0, mine, theirs), jnp.where(band == 0, theirs, mine)], 0)
    cross = jnp.where(band == 0, cross, jnp.transpose(cross))
    mean = mine_ref[chans:chans + 1, :] / count
    other_mean = theirs_ref[chans:chans + 1, :] / count
    mean_ref[...] = mean
    for block, left, b in ((own, mean, band), (cross, other_mean, 1 - band)):
        left = jnp.transpose(jnp.broadcast_to(left, (chans, chans)))
        cov_ref[pl.ds(pl.multiple_of(b * chans, chans), chans), :] = (block - count * left * mean) / (count - 1.0)


def finish(mine, theirs):
    chans = mine.shape[1]
    mean, covariance = pl.pallas_call(
        finish_kernel,
        out_shape=[jax.ShapeDtypeStruct((1, chans), F32), jax.ShapeDtypeStruct((2 * chans, chans), F32)],
        in_specs=[VMEM] * 2,
        out_specs=[VMEM] * 2,
        compiler_params=PARAMS,
    )(mine, theirs)
    return mean.reshape(chans), covariance


def swap(array, axis, step):
    size = lax.axis_size(axis)
    return lax.ppermute(array, axis, [(i, i ^ step) for i in range(size)])


def diagonal(array, ra_step, dec_pairs):
    ra_size, dec_size = lax.axis_size("ra"), lax.axis_size("dec")
    pairs = [
        (i * dec_size + a, (i + ra_step) % ra_size * dec_size + b) for i in range(ra_size) for a, b in dec_pairs
    ]
    return lax.ppermute(array, ("ra", "dec"), pairs)


def per_device(sky_maps, radii, valid):
    x = jnp.transpose(sky_maps, (1, 0, 2))
    radii = pltpu.with_memory_space_constraint(radii, pltpu.HBM)
    x = pltpu.with_memory_space_constraint(x, pltpu.HBM)
    rows, chans, cols = x.shape
    ra_size, dec_size = lax.axis_size("ra"), lax.axis_size("dec")
    up = [(i, (i + 1) % ra_size) for i in range(ra_size)]
    down = [(j, i) for i, j in up]
    right = [(i, i + 1) for i in range(dec_size - 1)]
    left = [(j, i) for i, j in right]
    sides = [right + left] if dec_size == 2 else [right, left]
    over, up_head, up_rest, down_head, down_rest = gather(radii, x)
    packed = pack(x, len(sides), over)
    before_rest, after_rest = lax.switch(
        over[0],
        [lambda a, b: (a, b), lambda a, b: (lax.ppermute(a, "ra", up), lax.ppermute(b, "ra", down))],
        up_rest, down_rest,
    )
    before, after = lax.ppermute(up_head, "ra", up), lax.ppermute(down_head, "ra", down)
    packed = [packed[3 * i:3 * i + 3] for i in range(len(sides))]
    halos = [lax.ppermute(p, "dec", pairs) for (p, _, _), pairs in zip(packed, sides)]
    corners = [
        (diagonal(high, 1, pairs), diagonal(low, -1, pairs)) for (_, low, high), pairs in zip(packed, sides)
    ]
    dec_table, inner_table, outer_table, own = tables(x, len(sides), before_rest)
    inner, begun = smooth_inner(radii, rows, own, halos, dec_table, inner_table)
    dec_begun = outer_begin(radii, begun, (before, before_rest), (after, after_rest), dec_table)
    outer = smooth_outer(radii, dec_begun, begun, dec_table, outer_table, corners)
    folded, cross, smoothed = own_gram(inner, swap(inner, "band", 1), outer, valid)
    total = cross_gram(folded, cross, outer, swap(outer, "band", 1), valid)
    steps = [("dec", 1 << b) for b in range(dec_size.bit_length() - 1)]
    steps += [("ra", 1 << b) for b in range(ra_size.bit_length() - 1)]
    for axis, step in steps:
        total = total + swap(total, axis, step)
    mean, covariance = finish(total, swap(total, "band", 1))
    return (jnp.transpose(smoothed, (1, 0, 2)), mean, covariance)


def solution(mesh):
    return jax.shard_map(
        per_device,
        mesh=mesh,
        in_specs=(
            P(("groups", "band"), "ra", "dec"),
            P(("groups", "band")),
            P(("groups", "ra"), "dec"),
        ),
        out_specs=(P(("groups", "band"), "ra", "dec"), P(("groups", "band")), P("groups", "band")),
        check_vma=False,
    )
```

```python
import functools

import jax
import jax.numpy as jnp
from jax import lax
from jax.experimental import pallas as pl
from jax.experimental.pallas import tpu as pltpu
from jax.sharding import PartitionSpec as P

RMAX = 17
LANES = 128
SLOTS = LANES // RMAX
EDGE = -(-RMAX // SLOTS)
PAD = 4
HALO = 24
VMEM_LIMIT = 32 * 1024 * 1024
BF16, F32 = jnp.bfloat16, jnp.float32
VMEM = pl.BlockSpec(memory_space=pltpu.VMEM)
SMEM = pl.BlockSpec(memory_space=pltpu.SMEM)
HBM = pl.BlockSpec(memory_space=pltpu.HBM)
PARAMS = pltpu.CompilerParams(vmem_limit_bytes=VMEM_LIMIT)


SPARE = LANES - SLOTS * RMAX


def row_groups(rows):
    middle = rows - 2 * EDGE * SLOTS
    small = LANES // 2 // RMAX
    count = min(n for n in range(middle + 1) if middle - n * SLOTS <= (2 * EDGE + n) // 2 + small)
    starts = [g * SLOTS for g in range(EDGE + count)] + [rows - (EDGE - g) * SLOTS for g in range(EDGE)]
    rest = list(range((EDGE + count) * SLOTS, rows - EDGE * SLOTS))
    left_over = [(row, 2 * i) for i, row in enumerate(rest[small:])]
    return starts, left_over, rest[:small]


def tables_kernel(sides, order_ref, x_ref, dec_ref, inner_ref, outer_ref, own, x, sem, *offset_refs):
    rows, chans, cols = x_ref.shape
    load = pltpu.make_async_copy(x_ref, x, sem)
    load.start()
    dec = lax.axis_index("dec")

    def offsets(offset_ref, used, offset):
        offset_ref[...] = jnp.where(used, offset, 2 * LANES).astype(F32)

    def grid(ref):
        return [lax.broadcasted_iota(jnp.int32, ref.shape, d) for d in (0, 1)]

    z, y = grid(offset_refs[0])
    before, after = z - cols - RMAX, z
    if sides == 1:
        column = jnp.where(z < cols, z, jnp.where(dec == 0, after, before))
    else:
        column = jnp.where(z < cols, z, jnp.where(z < cols + RMAX, before, after - RMAX))
    offsets(offset_refs[0], z < cols + sides * RMAX, column - y)
    out, source = grid(offset_refs[1])
    edge = out - (offset_refs[1].shape[0] - 2 * HALO)
    row = jnp.where(edge < 0, out + RMAX, jnp.where(edge < HALO, edge, edge - HALO + rows - RMAX))
    offsets(offset_refs[1], source < rows, source - row)
    out, source = grid(offset_refs[2])
    row = jnp.where(out < HALO, out, out - HALO + rows - RMAX)
    tail = source - HALO
    offsets(
        offset_refs[2], (source < RMAX) | ((tail >= 0) & (tail < RMAX)), jnp.where(tail < 0, source - RMAX, tail + rows) - row
    )
    line = (lax.broadcasted_iota(jnp.int32, (8, LANES), 1) - RMAX).astype(F32)

    def one_radius(index, carry):
        radius = jnp.full((8, LANES), index, jnp.int32).astype(F32)
        spread = 0.5 * radius
        scale = -1.0 / (2.0 * spread * spread)
        raw = jnp.where(jnp.abs(line) <= radius, jnp.exp(line * line * scale), 0.0)
        inverse = 1.0 / jnp.sum(raw, axis=1, keepdims=True)
        limit, scale, inverse = radius[:1, :1], scale[:1, :1], inverse[:1]
        for ref, offset_ref in zip((dec_ref, inner_ref, outer_ref), offset_refs):
            offset = offset_ref[...]
            taps = jnp.where(jnp.abs(offset) <= limit, jnp.exp(offset * offset * scale) * inverse, 0.0)
            ref[index] = taps.astype(BF16)
        return carry

    lax.fori_loop(1, RMAX + 1, one_radius, 0, unroll=True)
    pitch = chans + PAD

    def copy_row(i, carry):
        own[pl.ds(i * pitch, chans), :] = x[i].astype(F32)
        return carry

    load.wait()
    lax.fori_loop(0, rows, copy_row, 0, unroll=6)
    for i in range(rows, inner_ref.shape[2]):
        own[pl.ds(i * pitch, chans), :] = jnp.zeros((chans, cols), F32)


def tables(x, sides, order):
    rows, chans, cols = x.shape
    own = -(-rows // 16) * 16
    inner = -(-(rows - 2 * RMAX) // 16) * 16
    shapes = [(cols + LANES, cols), (inner + 2 * HALO, own), (2 * HALO, 2 * HALO)]
    return pl.pallas_call(
        functools.partial(tables_kernel, sides),
        out_shape=[pltpu.VMEM((RMAX + 1, *shape), BF16) for shape in shapes]
        + [pltpu.VMEM(((own + 1) * (chans + PAD), cols), F32)],
        in_specs=[pl.BlockSpec(memory_space=pl.ANY), HBM],
        out_specs=[VMEM] * 4,
        scratch_shapes=[pltpu.VMEM(x.shape, BF16), pltpu.SemaphoreType.DMA] + [pltpu.VMEM(shape, F32) for shape in shapes],
        compiler_params=PARAMS,
        cost_estimate=pl.CostEstimate(flops=10**5, bytes_accessed=10**5, transcendentals=0),
    )(order, x)


def gather_kernel(rad_ref, source_ref, over_ref, up_ref, up_rest_ref, down_ref, down_rest_ref, low, high, low_wide, high_wide, low_packed, high_packed, low_rest, high_rest, sems):
    rows, chans, cols = source_ref.shape
    pitch = chans + PAD
    cap, full = up_ref.shape[0], RMAX * chans
    copies = [
        pltpu.make_async_copy(source_ref.at[pl.ds(start, RMAX)], ref, sems.at[i])
        for i, (start, ref) in enumerate(((0, low), (rows - RMAX, high)))
    ]
    for copy in copies:
        copy.start()
    for copy, ref, wide in zip(copies, (low, high), (low_wide, high_wide)):
        copy.wait()
        for i in range(RMAX):
            wide[pl.ds(i * pitch, chans), :] = ref[i].astype(F32)

    total = 0
    for c in range(chans):
        total = total + rad_ref[c]

    def both_ways(i, carry):
        start, stop = carry
        c = chans - 1 - i
        low_packed[pl.ds(HALO + start, RMAX), :] = low_wide[pl.ds(i, RMAX, stride=pitch), :]
        high_packed[pl.ds(HALO + stop - RMAX, RMAX), :] = high_wide[pl.ds(c, RMAX, stride=pitch), :]
        return start + rad_ref[i], stop - rad_ref[c]

    lax.fori_loop(0, chans, both_ways, (0, total), unroll=16)
    rests = []
    for i, (packed, ref, rest, rest_ref) in enumerate((
        (low_packed, down_ref, low_rest, down_rest_ref), (high_packed, up_ref, high_rest, up_rest_ref)
    )):
        packed[pl.ds(HALO + total, HALO), :] = jnp.zeros((HALO, cols), F32)
        ref[...] = packed[HALO:HALO + cap, :].astype(BF16)
        rests.append(pltpu.make_async_copy(rest, rest_ref, sems.at[3 + i]))

    @pl.when(total > cap)
    def _():
        for packed, rest, copy in ((low_packed, low_rest, rests[0]), (high_packed, high_rest, rests[1])):
            rest[...] = packed[HALO + cap:HALO + full, :].astype(BF16)
            copy.start()
            copy.wait()

    over_ref[0] = jnp.where(total > cap, 1, 0)


def cap_of(chans):
    return RMAX * chans * 5 // 8 // 16 * 16


def gather(radii, x):
    rows, chans, cols = x.shape
    full, cap = RMAX * chans, cap_of(chans)
    head, rest = pltpu.VMEM((cap, cols), BF16), jax.ShapeDtypeStruct((full - cap, cols), BF16)
    return pl.pallas_call(
        gather_kernel,
        out_shape=[pltpu.SMEM((1,), jnp.int32), head, rest, head, rest],
        in_specs=[SMEM, HBM],
        out_specs=[SMEM] + [VMEM, HBM] * 2,
        scratch_shapes=[pltpu.VMEM((RMAX, chans, cols), BF16)] * 2
        + [pltpu.VMEM(((RMAX + 1) * (chans + PAD), cols), F32)] * 2
        + [pltpu.VMEM((full + 2 * HALO, cols), F32)] * 2
        + [pltpu.VMEM(rest.shape, BF16)] * 2
        + [pltpu.SemaphoreType.DMA((5,))],
        compiler_params=PARAMS,
        cost_estimate=pl.CostEstimate(flops=1, bytes_accessed=1, transcendentals=0),
    )(radii, x)


def pack_kernel(sides, order_ref, source_ref, *refs):
    edge_refs, (x_ref, sems) = refs[:3 * sides], refs[3 * sides:]
    rows, chans, cols = x_ref.shape
    starts, left_over, shared = row_groups(rows)
    edge, tail = EDGE * SLOTS, rows - EDGE * SLOTS
    middle = starts[-EDGE - 1] + SLOTS
    spans = [(middle, tail - middle), (0, edge), (edge, middle - edge), (tail, edge)]
    loads = [
        pltpu.make_async_copy(source_ref.at[pl.ds(start, n)], x_ref.at[pl.ds(start, n)], sems.at[i])
        for i, (start, n) in enumerate(spans)
    ]
    for load in loads:
        load.start()
    loads[0].wait()
    dec = lax.axis_index("dec")
    lane = lax.broadcasted_iota(jnp.int32, (chans, LANES), 1)
    for side in range(sides):
        edge_ref, low_ref, high_ref = edge_refs[3 * side:3 * side + 3]
        if sides == 1:
            first = jnp.where(dec == 0, cols - RMAX, 0)
        else:
            first = cols - RMAX if side == 0 else 0

        def moved(row, lane_of_first):
            return pltpu.roll(x_ref[row].astype(F32), lax.rem(lane_of_first - first + 2 * LANES, LANES), 1)

        tiles = []
        for g, start in enumerate(starts):
            if side == 0 and start in (0, edge, tail):
                loads[(0, edge, tail).index(start) + 1].wait()
            packed = moved(start, 0)
            for j in range(1, SLOTS):
                packed = jnp.where(lane < RMAX * j, packed, moved(start + j, RMAX * j))
            for row, tile in left_over:
                if g in (tile, tile + 1):
                    packed = jnp.where(lane < LANES - SPARE, packed, moved(row, LANES - SPARE - SPARE * (g - tile)))
            edge_ref[g * chans:(g + 1) * chans, :] = packed.astype(BF16)
            tiles.append(packed)
        half = chans // 2

        def beside(part, low):
            return jnp.where((lane[:half] < LANES // 2) == low, part[:half], pltpu.roll(part[half:], LANES // 2, 1))

        packed = jnp.zeros((chans, LANES), F32)
        for j, row in enumerate(shared):
            packed = jnp.where(lane < RMAX * j, packed, moved(row, RMAX * j))
        edge_ref[len(starts) * chans:, :] = beside(packed, True).astype(BF16)
        for ref, whole, part in (
            (low_ref, tiles[:EDGE - 1], beside(tiles[EDGE - 1], True)),
            (high_ref, tiles[1 - EDGE:], beside(tiles[-EDGE], False)),
        ):
            for i, tile in enumerate(whole):
                ref[i * chans:(i + 1) * chans, :] = tile.astype(BF16)
            ref[(EDGE - 1) * chans:, :] = part.astype(BF16)


def pack(x, sides, order):
    rows, chans, cols = x.shape
    packed = [pltpu.VMEM((len(row_groups(rows)[0]) * chans + chans // 2, LANES), BF16)]
    packed += [pltpu.VMEM(((EDGE - 1) * chans + chans // 2, LANES), BF16)] * 2
    return pl.pallas_call(
        functools.partial(pack_kernel, sides),
        out_shape=packed * sides,
        in_specs=[SMEM, HBM],
        out_specs=[VMEM] * (3 * sides),
        scratch_shapes=[pltpu.VMEM(x.shape, BF16), pltpu.SemaphoreType.DMA((4,))],
        compiler_params=PARAMS,
        cost_estimate=pl.CostEstimate(flops=1, bytes_accessed=1, transcendentals=0),
    )(order, x)


def widen(tiles, j):
    lane = lax.broadcasted_iota(jnp.int32, tiles[0].shape, 1)
    value = None
    for side, part in enumerate(tiles):
        shift = (RMAX * side - RMAX * j) % LANES
        part = part if shift == 0 else pltpu.roll(part, shift, 1)
        value = part if side == 0 else jnp.where(lane < RMAX, value, part)
    return value


def inner_kernel(sides, rad_ref, own, dec_ref, ra_ref, *refs):
    edge_refs, (out_ref, begun, halo, result) = refs[:sides], refs[sides:]
    inner, chans, cols = out_ref.shape
    rows = inner + 2 * RMAX
    pitch = chans + PAD
    own_rows = ra_ref.shape[2]
    base = ra_ref.shape[1] - 2 * HALO

    starts, left_over, shared = row_groups(rows)
    for g, start in enumerate(starts):
        tiles = [ref[g * chans:(g + 1) * chans, :].astype(F32) for ref in edge_refs]
        for j in range(SLOTS):
            halo[pl.ds((start + j) * pitch, chans), :] = widen(tiles, j)
    lane = lax.broadcasted_iota(jnp.int32, (chans, LANES), 1)
    for row, g in left_over:
        tiles = []
        for ref in edge_refs:
            begin, end = (
                pltpu.roll(ref[(g + i) * chans:(g + i + 1) * chans, :].astype(F32), SPARE * (1 + i), 1) for i in range(2)
            )
            tiles.append(jnp.where(lane < SPARE, begin, end))
        halo[pl.ds(row * pitch, chans), :] = widen(tiles, 0)
    tiles = [ref[len(starts) * chans:, :].astype(F32) for ref in edge_refs]
    tiles = [jnp.concatenate([tile, pltpu.roll(tile, LANES // 2, 1)], 0) for tile in tiles]
    for j, row in enumerate(shared):
        halo[pl.ds(row * pitch, chans), :] = widen(tiles, j)

    for i in range(rows, own_rows):
        halo[pl.ds(i * pitch, chans), :] = jnp.zeros((chans, cols), F32)

    radii = [rad_ref[c] for c in range(chans)]
    partials = []
    for c, radius in enumerate(radii):
        picked = pl.ds(c, own_rows, stride=pitch)
        lhs = jnp.concatenate([own[picked, :].astype(BF16), halo[picked, :].astype(BF16)], 1)
        partials.append(jnp.dot(lhs, dec_ref[radius], preferred_element_type=F32).astype(BF16))
    for c, (radius, partial) in enumerate(zip(radii, partials)):
        smoothed = jnp.dot(ra_ref[radius], partial, preferred_element_type=F32)
        result[pl.ds(c, inner, stride=pitch), :] = smoothed[:inner]
        begun[pl.ds(c, RMAX, stride=pitch), :] = smoothed[base:base + RMAX]
        begun[pl.ds(RMAX * pitch + c, RMAX, stride=pitch), :] = smoothed[base + HALO:base + HALO + RMAX]

    def store(i, carry):
        out_ref[i] = result[pl.ds(i * pitch, chans), :].astype(BF16)
        return carry

    lax.fori_loop(0, inner, store, 0, unroll=4)


def smooth_inner(radii, rows, own, halos, dec_table, ra_table):
    chans, cols = radii.shape[0], own.shape[1]
    pitch, own_rows, inner = chans + PAD, ra_table.shape[2], rows - 2 * RMAX
    operands = [own, dec_table, ra_table, *halos]
    return pl.pallas_call(
        functools.partial(inner_kernel, len(halos)),
        out_shape=[
            pltpu.VMEM((inner, chans, cols), BF16),
            pltpu.VMEM(((2 * RMAX + 1) * pitch, cols), F32),
        ],
        in_specs=[SMEM] + [VMEM] * len(operands),
        out_specs=[VMEM] * 2,
        scratch_shapes=[
            pltpu.VMEM(((own_rows + 1) * pitch, LANES), F32),
            pltpu.VMEM(((inner + 1) * pitch, cols), F32),
        ],
        compiler_params=PARAMS,
        cost_estimate=pl.CostEstimate(flops=1, bytes_accessed=1, transcendentals=0),
    )(radii, *operands)


def reach_lanes(sides):
    return -(-sides * RMAX // 16) * 16


def outer_begin_kernel(rad_ref, order_ref, before_ref, before_rest, after_ref, after_rest, dec_ref, begun, before, after):
    chans, _, cols = begun.shape
    radii = [rad_ref[c] for c in range(chans)]
    total = functools.reduce(lambda a, b: a + b, radii)
    cap = before_ref.shape[0]
    for packed, head, rest in ((before, before_ref, before_rest), (after, after_ref, after_rest)):
        packed[:HALO, :] = jnp.zeros((HALO, cols), F32)
        packed[HALO:HALO + cap, :] = head[...].astype(F32)
        packed[HALO + cap:2 * HALO + cap, :] = jnp.zeros((HALO, cols), F32)
        packed[packed.shape[0] - HALO:, :] = jnp.zeros((HALO, cols), F32)

        @pl.when(total > cap)
        def _():
            packed[HALO + cap:HALO + cap + rest.shape[0], :] = rest[...].astype(F32)

    offset = 0
    for c, radius in enumerate(radii):
        planes = [
            before[pl.ds(HALO - RMAX + offset + radius, HALO), :],
            after[pl.ds(HALO + offset, HALO), :],
        ]
        lhs = jnp.concatenate(planes, 0).astype(BF16)
        begun[c] = jnp.dot(lhs, dec_ref[radius, :cols, :], preferred_element_type=F32)
        offset = offset + radius


def outer_begin(radii, order, before, after, dec_table):
    chans, cols = radii.shape[0], dec_table.shape[2]
    operands = [*before, *after, dec_table]
    return pl.pallas_call(
        outer_begin_kernel,
        out_shape=pltpu.VMEM((chans, 2 * HALO, cols), F32),
        in_specs=[SMEM, pl.BlockSpec(memory_space=pl.ANY)] + [VMEM] * len(operands),
        out_specs=VMEM,
        scratch_shapes=[pltpu.VMEM((RMAX * chans + 2 * HALO, cols), F32)] * 2,
        compiler_params=PARAMS,
        cost_estimate=pl.CostEstimate(flops=2 * 10**9, bytes_accessed=5 * 10**6, transcendentals=0),
    )(radii, order, *operands)


def outer_kernel(sides, rad_ref, dec_begun, ra_begun, dec_ref, ra_ref, *refs):
    corner_refs, (out_ref, corner, result) = refs[:2 * sides], refs[2 * sides:]
    rows, chans, cols = out_ref.shape
    pitch = chans + PAD
    width = reach_lanes(sides)

    for part, base in ((0, 0), (1, HALO)):
        starts = [g * SLOTS if part else g * SLOTS + RMAX - EDGE * SLOTS for g in range(EDGE)]
        shared = EDGE - 1 if part else 0
        order = [*range(EDGE - 1), EDGE - 1] if part else [EDGE - 1, *range(EDGE - 1)]
        for g, (start, place) in enumerate(zip(starts, order)):
            tiles = []
            for ref in corner_refs[part::2]:
                tile = ref[place * chans:min(place * chans + chans, ref.shape[0]), :].astype(F32)
                if g == shared:
                    tile = jnp.concatenate([tile, pltpu.roll(tile, LANES // 2, 1)], 0)
                tiles.append(tile)
            for j in range(SLOTS):
                if 0 <= start + j < RMAX:
                    corner[pl.ds((base + start + j) * pitch, chans), :] = widen(tiles, j)
        for row in range(RMAX, HALO):
            corner[pl.ds((base + row) * pitch, chans), :] = jnp.zeros((chans, LANES), F32)

    radii = [rad_ref[c] for c in range(chans)]
    partials = []
    for c, radius in enumerate(radii):
        lhs = corner[pl.ds(c, 2 * HALO, stride=pitch), :].astype(BF16)[:, :width]
        partial = jnp.dot(lhs, dec_ref[radius, cols:cols + width, :], preferred_element_type=F32) + dec_begun[c]
        partials.append(partial.astype(BF16))
    for c, (radius, partial) in enumerate(zip(radii, partials)):
        smoothed = jnp.dot(ra_ref[radius], partial, preferred_element_type=F32)
        result[pl.ds(c, RMAX, stride=pitch), :] = smoothed[:RMAX]
        result[pl.ds(RMAX * pitch + c, RMAX, stride=pitch), :] = smoothed[HALO:HALO + RMAX]

    def store(i, carry):
        picked = pl.ds(i * pitch, chans)
        out_ref[i] = (ra_begun[picked, :] + result[picked, :]).astype(BF16)
        return carry

    lax.fori_loop(0, rows, store, 0, unroll=True)


def smooth_outer(radii, dec_begun, ra_begun, dec_table, ra_table, corners):
    chans, _, cols = dec_begun.shape
    pitch = chans + PAD
    operands = [dec_begun, ra_begun, dec_table, ra_table] + [part for side in corners for part in side]
    return pl.pallas_call(
        functools.partial(outer_kernel, len(corners)),
        out_shape=pltpu.VMEM((2 * RMAX, chans, cols), BF16),
        in_specs=[SMEM] + [VMEM] * len(operands),
        out_specs=VMEM,
        scratch_shapes=[
            pltpu.VMEM(((2 * HALO + 1) * pitch, LANES), F32),
            pltpu.VMEM(((2 * RMAX + 1) * pitch, cols), F32),
        ],
        compiler_params=PARAMS,
        cost_estimate=pl.CostEstimate(flops=10**10, bytes_accessed=5 * 10**6, transcendentals=0),
    )(radii, *operands)


SUM_ROWS = 8


def add_products(total, row_refs, own_ref, valid_ref, first_row, rows, sums=None):
    depth = max(d for d in range(1, 27) if rows % d == 0)

    def nt(a, b):
        return lax.dot_general(a, b, (((1,), (1,)), ((), ())), preferred_element_type=F32)

    def body(i, carry):
        picked = [i * depth + j for j in range(depth)]
        line = jnp.concatenate([valid_ref[pl.ds(first_row(r), 1), :].astype(BF16) for r in picked], 1)
        own, *others = (jnp.concatenate([ref[r] for r in picked], 1) for ref in (own_ref, *row_refs))
        total[...] += nt(jnp.concatenate(others, 0), own * line)
        if sums is not None:
            sums[...] += nt(jnp.broadcast_to(line, (16, line.shape[1])), own)[:SUM_ROWS]
        return carry

    lax.fori_loop(0, rows // depth, body, 0, unroll=True)


def outer_row(image_rows):
    return lambda r: jnp.where(r < RMAX, r, r + image_rows - 2 * RMAX)


def own_gram_kernel(own_ref, other_ref, outer_ref, valid_ref, out_ref, cross_ref, smoothed_ref, both, sems):
    rows, chans = valid_ref.shape[0], own_ref.shape[1]
    half = chans // 2
    copies = [
        pltpu.make_async_copy(source, smoothed_ref.at[pl.ds(start, source.shape[0])], sems.at[i])
        for i, (source, start) in enumerate((
            (own_ref, RMAX),
            (outer_ref.at[pl.ds(0, RMAX)], 0),
            (outer_ref.at[pl.ds(RMAX, RMAX)], rows - RMAX),
        ))
    ]
    for copy in copies:
        copy.start()
    both[...] = jnp.zeros_like(both)
    products, own, sums = both.at[:2 * chans], both.at[:chans], both.at[2 * chans:]
    add_products(products, (own_ref, other_ref), own_ref, valid_ref, lambda r: r + RMAX, own_ref.shape[0], sums)
    add_products(own, (outer_ref,), outer_ref, valid_ref, outer_row(rows), 2 * RMAX, sums)
    cross_ref[...] = both[chans:2 * chans, :]
    low = pltpu.roll(both[half:chans, :], half, 1)
    row = lax.broadcasted_iota(jnp.int32, (half, chans), 0)
    lane = lax.broadcasted_iota(jnp.int32, (half, chans), 1)
    out_ref[:half, :] = jnp.where(lane < row, low, both[:half, :])
    diagonal = jnp.sum(jnp.where(lane == row, low, 0.0), axis=0, keepdims=True)
    row = lax.broadcasted_iota(jnp.int32, (SUM_ROWS, chans), 0)
    tail = jnp.where(row == 1, diagonal, both[2 * chans:, :])
    out_ref[half:, :] = jnp.where(row == 2, jnp.sum(valid_ref[...].astype(F32)), tail)
    for copy in copies:
        copy.wait()


def own_gram(own, other, outer, valid):
    _, chans, cols = own.shape
    return pl.pallas_call(
        own_gram_kernel,
        out_shape=[
            pltpu.VMEM((chans // 2 + SUM_ROWS, chans), F32),
            pltpu.VMEM((chans, chans), F32),
            jax.ShapeDtypeStruct((valid.shape[0], chans, cols), BF16),
        ],
        in_specs=[VMEM] * 4,
        out_specs=[VMEM, VMEM, HBM],
        scratch_shapes=[pltpu.VMEM((2 * chans + SUM_ROWS, chans), F32), pltpu.SemaphoreType.DMA((3,))],
        compiler_params=PARAMS,
        cost_estimate=pl.CostEstimate(flops=10**9, bytes_accessed=3 * 10**6, transcendentals=0),
    )(own, other, outer, valid)


def cross_gram_kernel(folded_ref, cross_ref, own_ref, other_ref, valid_ref, out_ref, total):
    chans = own_ref.shape[1]
    half = chans // 2
    total[...] = cross_ref[...]
    add_products(total, (other_ref,), own_ref, valid_ref, outer_row(valid_ref.shape[0]), 2 * RMAX)
    cross = total[...]
    out_ref[:half, :] = folded_ref[:half, :]
    out_ref[half:chans, :] = jnp.where(lax.axis_index("band") == 0, cross[:half], jnp.transpose(cross)[half:])
    out_ref[chans:, :] = folded_ref[half:, :]


def cross_gram(folded, cross, own, other, valid):
    chans = own.shape[1]
    return pl.pallas_call(
        cross_gram_kernel,
        out_shape=pltpu.VMEM((chans + SUM_ROWS, chans), F32),
        in_specs=[VMEM] * 5,
        out_specs=VMEM,
        scratch_shapes=[pltpu.VMEM((chans, chans), F32)],
        compiler_params=PARAMS,
    )(folded, cross, own, other, valid)


def finish_kernel(mine_ref, theirs_ref, mean_ref, cov_ref):
    chans = mine_ref.shape[1]
    half = chans // 2
    band = lax.axis_index("band")
    count = mine_ref[chans + 2:chans + 3, :1]
    folded = mine_ref[:half, :]
    mirror = jnp.transpose(jnp.concatenate([folded, jnp.zeros((half, chans), F32)], 0))
    row = lax.broadcasted_iota(jnp.int32, (half, chans), 0)
    lane = lax.broadcasted_iota(jnp.int32, (half, chans), 1)
    upper = jnp.where(lane < row, mirror[:half], folded)
    column = lane - half
    corner = jnp.where(column < row, pltpu.roll(folded, half, 1), pltpu.roll(mirror[:half], half, 1))
    corner = jnp.where(column == row, pltpu.roll(mine_ref[chans:chans + SUM_ROWS, :], half, 1)[1:2, :], corner)
    own = jnp.concatenate([upper, jnp.where(column < 0, mirror[half:], corner)], 0)
    mine, theirs = mine_ref[half:chans, :], theirs_ref[half:chans, :]
    cross = jnp.concatenate([jnp.where(band == 0, mine, theirs), jnp.where(band == 0, theirs, mine)], 0)
    cross = jnp.where(band == 0, cross, jnp.transpose(cross))
    mean = mine_ref[chans:chans + 1, :] / count
    other_mean = theirs_ref[chans:chans + 1, :] / count
    mean_ref[...] = mean
    for block, left, b in ((own, mean, band), (cross, other_mean, 1 - band)):
        left = jnp.transpose(jnp.broadcast_to(left, (chans, chans)))
        cov_ref[pl.ds(pl.multiple_of(b * chans, chans), chans), :] = (block - count * left * mean) / (count - 1.0)


def finish(mine, theirs):
    chans = mine.shape[1]
    mean, covariance = pl.pallas_call(
        finish_kernel,
        out_shape=[jax.ShapeDtypeStruct((1, chans), F32), jax.ShapeDtypeStruct((2 * chans, chans), F32)],
        in_specs=[VMEM] * 2,
        out_specs=[VMEM] * 2,
        compiler_params=PARAMS,
    )(mine, theirs)
    return mean.reshape(chans), covariance


def swap(array, axis, step):
    size = lax.axis_size(axis)
    return lax.ppermute(array, axis, [(i, i ^ step) for i in range(size)])


def diagonal(array, ra_step, dec_pairs):
    ra_size, dec_size = lax.axis_size("ra"), lax.axis_size("dec")
    pairs = [
        (i * dec_size + a, (i + ra_step) % ra_size * dec_size + b) for i in range(ra_size) for a, b in dec_pairs
    ]
    return lax.ppermute(array, ("ra", "dec"), pairs)


def per_device(sky_maps, radii, valid):
    x = jnp.transpose(sky_maps, (1, 0, 2))
    radii = pltpu.with_memory_space_constraint(radii, pltpu.HBM)
    x = pltpu.with_memory_space_constraint(x, pltpu.HBM)
    rows, chans, cols = x.shape
    ra_size, dec_size = lax.axis_size("ra"), lax.axis_size("dec")
    up = [(i, (i + 1) % ra_size) for i in range(ra_size)]
    down = [(j, i) for i, j in up]
    right = [(i, i + 1) for i in range(dec_size - 1)]
    left = [(j, i) for i, j in right]
    sides = [right + left] if dec_size == 2 else [right, left]
    over, up_head, up_rest, down_head, down_rest = gather(radii, x)
    packed = pack(x, len(sides), over)
    before_rest, after_rest = lax.switch(
        over[0],
        [lambda a, b: (a, b), lambda a, b: (lax.ppermute(a, "ra", up), lax.ppermute(b, "ra", down))],
        up_rest, down_rest,
    )
    before, after = lax.ppermute(up_head, "ra", up), lax.ppermute(down_head, "ra", down)
    packed = [packed[3 * i:3 * i + 3] for i in range(len(sides))]
    halos = [lax.ppermute(p, "dec", pairs) for (p, _, _), pairs in zip(packed, sides)]
    corners = [
        (diagonal(high, 1, pairs), diagonal(low, -1, pairs)) for (_, low, high), pairs in zip(packed, sides)
    ]
    dec_table, inner_table, outer_table, own = tables(x, len(sides), before_rest)
    inner, begun = smooth_inner(radii, rows, own, halos, dec_table, inner_table)
    dec_begun = outer_begin(radii, begun, (before, before_rest), (after, after_rest), dec_table)
    outer = smooth_outer(radii, dec_begun, begun, dec_table, outer_table, corners)
    folded, cross, smoothed = own_gram(inner, swap(inner, "band", 1), outer, valid)
    total = cross_gram(folded, cross, outer, swap(outer, "band", 1), valid)
    steps = [("dec", 1 << b) for b in range(dec_size.bit_length() - 1)]
    steps += [("ra", 1 << b) for b in range(ra_size.bit_length() - 1)]
    for axis, step in steps:
        total = total + swap(total, axis, step)
    mean, covariance = finish(total, swap(total, "band", 1))
    return (jnp.transpose(smoothed, (1, 0, 2)), mean, covariance)


def solution(mesh):
    return jax.shard_map(
        per_device,
        mesh=mesh,
        in_specs=(
            P(("groups", "band"), "ra", "dec"),
            P(("groups", "band")),
            P(("groups", "ra"), "dec"),
        ),
        out_specs=(P(("groups", "band"), "ra", "dec"), P(("groups", "band")), P("groups", "band")),
        check_vma=False,
    )
```

```python
import functools

import jax
import jax.numpy as jnp
from jax import lax
from jax.experimental import pallas as pl
from jax.experimental.pallas import tpu as pltpu
from jax.sharding import PartitionSpec as P

RMAX = 17
LANES = 128
SLOTS = LANES // RMAX
EDGE = -(-RMAX // SLOTS)
PAD = 4
HALO = 24
VMEM_LIMIT = 32 * 1024 * 1024
BF16, F32 = jnp.bfloat16, jnp.float32
VMEM = pl.BlockSpec(memory_space=pltpu.VMEM)
SMEM = pl.BlockSpec(memory_space=pltpu.SMEM)
HBM = pl.BlockSpec(memory_space=pltpu.HBM)
PARAMS = pltpu.CompilerParams(vmem_limit_bytes=VMEM_LIMIT)


SPARE = LANES - SLOTS * RMAX


def row_groups(rows):
    middle = rows - 2 * EDGE * SLOTS
    small = LANES // 2 // RMAX
    count = min(n for n in range(middle + 1) if middle - n * SLOTS <= (2 * EDGE + n) // 2 + small)
    starts = [g * SLOTS for g in range(EDGE + count)] + [rows - (EDGE - g) * SLOTS for g in range(EDGE)]
    rest = list(range((EDGE + count) * SLOTS, rows - EDGE * SLOTS))
    left_over = [(row, 2 * i) for i, row in enumerate(rest[small:])]
    return starts, left_over, rest[:small]


def tables_kernel(sides, order_ref, x_ref, dec_ref, inner_ref, outer_ref, own, x, sem, *offset_refs):
    rows, chans, cols = x_ref.shape
    load = pltpu.make_async_copy(x_ref, x, sem)
    load.start()
    dec = lax.axis_index("dec")

    def offsets(offset_ref, used, offset):
        offset_ref[...] = jnp.where(used, offset, 2 * LANES).astype(F32)

    def grid(ref):
        return [lax.broadcasted_iota(jnp.int32, ref.shape, d) for d in (0, 1)]

    z, y = grid(offset_refs[0])
    before, after = z - cols - RMAX, z
    if sides == 1:
        column = jnp.where(z < cols, z, jnp.where(dec == 0, after, before))
    else:
        column = jnp.where(z < cols, z, jnp.where(z < cols + RMAX, before, after - RMAX))
    offsets(offset_refs[0], z < cols + sides * RMAX, column - y)
    out, source = grid(offset_refs[1])
    edge = out - (offset_refs[1].shape[0] - 2 * HALO)
    row = jnp.where(edge < 0, out + RMAX, jnp.where(edge < HALO, edge, edge - HALO + rows - RMAX))
    offsets(offset_refs[1], source < rows, source - row)
    out, source = grid(offset_refs[2])
    row = jnp.where(out < HALO, out, out - HALO + rows - RMAX)
    tail = source - HALO
    offsets(
        offset_refs[2], (source < RMAX) | ((tail >= 0) & (tail < RMAX)), jnp.where(tail < 0, source - RMAX, tail + rows) - row
    )
    line = (lax.broadcasted_iota(jnp.int32, (8, LANES), 1) - RMAX).astype(F32)

    def one_radius(index, carry):
        radius = jnp.full((8, LANES), index, jnp.int32).astype(F32)
        spread = 0.5 * radius
        scale = -1.0 / (2.0 * spread * spread)
        raw = jnp.where(jnp.abs(line) <= radius, jnp.exp(line * line * scale), 0.0)
        inverse = 1.0 / jnp.sum(raw, axis=1, keepdims=True)
        limit, scale, inverse = radius[:1, :1], scale[:1, :1], inverse[:1]
        for ref, offset_ref in zip((dec_ref, inner_ref, outer_ref), offset_refs):
            offset = offset_ref[...]
            taps = jnp.where(jnp.abs(offset) <= limit, jnp.exp(offset * offset * scale) * inverse, 0.0)
            ref[index] = taps.astype(BF16)
        return carry

    lax.fori_loop(1, RMAX + 1, one_radius, 0, unroll=True)
    pitch = chans + PAD

    def copy_row(i, carry):
        own[pl.ds(i * pitch, chans), :] = x[i].astype(F32)
        return carry

    load.wait()
    lax.fori_loop(0, rows, copy_row, 0, unroll=6)
    for i in range(rows, inner_ref.shape[2]):
        own[pl.ds(i * pitch, chans), :] = jnp.zeros((chans, cols), F32)


def tables(x, sides, order):
    rows, chans, cols = x.shape
    own = -(-rows // 16) * 16
    inner = -(-(rows - 2 * RMAX) // 16) * 16
    shapes = [(cols + LANES, cols), (inner + 2 * HALO, own), (2 * HALO, 2 * HALO)]
    return pl.pallas_call(
        functools.partial(tables_kernel, sides),
        out_shape=[pltpu.VMEM((RMAX + 1, *shape), BF16) for shape in shapes]
        + [pltpu.VMEM(((own + 1) * (chans + PAD), cols), F32)],
        in_specs=[pl.BlockSpec(memory_space=pl.ANY), HBM],
        out_specs=[VMEM] * 4,
        scratch_shapes=[pltpu.VMEM(x.shape, BF16), pltpu.SemaphoreType.DMA] + [pltpu.VMEM(shape, F32) for shape in shapes],
        compiler_params=PARAMS,
        cost_estimate=pl.CostEstimate(flops=10**5, bytes_accessed=10**5, transcendentals=0),
    )(order, x)


def gather_kernel(rad_ref, source_ref, over_ref, up_ref, up_rest_ref, down_ref, down_rest_ref, low, high, low_wide, high_wide, low_packed, high_packed, low_rest, high_rest, sems):
    rows, chans, cols = source_ref.shape
    pitch = chans + PAD
    cap, full = up_ref.shape[0], RMAX * chans
    copies = [
        pltpu.make_async_copy(source_ref.at[pl.ds(start, RMAX)], ref, sems.at[i])
        for i, (start, ref) in enumerate(((0, low), (rows - RMAX, high)))
    ]
    for copy in copies:
        copy.start()
    for copy, ref, wide in zip(copies, (low, high), (low_wide, high_wide)):
        copy.wait()
        for i in range(RMAX):
            wide[pl.ds(i * pitch, chans), :] = ref[i].astype(F32)

    total = 0
    for c in range(chans):
        total = total + rad_ref[c]

    def both_ways(i, carry):
        start, stop = carry
        c = chans - 1 - i
        low_packed[pl.ds(HALO + start, RMAX), :] = low_wide[pl.ds(i, RMAX, stride=pitch), :]
        high_packed[pl.ds(HALO + stop - RMAX, RMAX), :] = high_wide[pl.ds(c, RMAX, stride=pitch), :]
        return start + rad_ref[i], stop - rad_ref[c]

    lax.fori_loop(0, chans, both_ways, (0, total), unroll=16)
    rests = []
    for i, (packed, ref, rest, rest_ref) in enumerate((
        (low_packed, down_ref, low_rest, down_rest_ref), (high_packed, up_ref, high_rest, up_rest_ref)
    )):
        packed[pl.ds(HALO + total, HALO), :] = jnp.zeros((HALO, cols), F32)
        ref[...] = packed[HALO:HALO + cap, :].astype(BF16)
        rests.append(pltpu.make_async_copy(rest, rest_ref, sems.at[3 + i]))

    @pl.when(total > cap)
    def _():
        for packed, rest, copy in ((low_packed, low_rest, rests[0]), (high_packed, high_rest, rests[1])):
            rest[...] = packed[HALO + cap:HALO + full, :].astype(BF16)
            copy.start()
            copy.wait()

    over_ref[0] = jnp.where(total > cap, 1, 0)


def cap_of(chans):
    return RMAX * chans * 5 // 8 // 16 * 16


def gather(radii, x):
    rows, chans, cols = x.shape
    full, cap = RMAX * chans, cap_of(chans)
    head, rest = pltpu.VMEM((cap, cols), BF16), jax.ShapeDtypeStruct((full - cap, cols), BF16)
    return pl.pallas_call(
        gather_kernel,
        out_shape=[pltpu.SMEM((1,), jnp.int32), head, rest, head, rest],
        in_specs=[SMEM, HBM],
        out_specs=[SMEM] + [VMEM, HBM] * 2,
        scratch_shapes=[pltpu.VMEM((RMAX, chans, cols), BF16)] * 2
        + [pltpu.VMEM(((RMAX + 1) * (chans + PAD), cols), F32)] * 2
        + [pltpu.VMEM((full + 2 * HALO, cols), F32)] * 2
        + [pltpu.VMEM(rest.shape, BF16)] * 2
        + [pltpu.SemaphoreType.DMA((5,))],
        compiler_params=PARAMS,
        cost_estimate=pl.CostEstimate(flops=1, bytes_accessed=1, transcendentals=0),
    )(radii, x)


def pack_kernel(sides, order_ref, source_ref, *refs):
    edge_refs, (x_ref, sems) = refs[:3 * sides], refs[3 * sides:]
    rows, chans, cols = x_ref.shape
    starts, left_over, shared = row_groups(rows)
    edge, tail = EDGE * SLOTS, rows - EDGE * SLOTS
    middle = starts[-EDGE - 1] + SLOTS
    spans = [(middle, tail - middle), (0, edge), (edge, middle - edge), (tail, edge)]
    loads = [
        pltpu.make_async_copy(source_ref.at[pl.ds(start, n)], x_ref.at[pl.ds(start, n)], sems.at[i])
        for i, (start, n) in enumerate(spans)
    ]
    for load in loads:
        load.start()
    loads[0].wait()
    dec = lax.axis_index("dec")
    lane = lax.broadcasted_iota(jnp.int32, (chans, LANES), 1)
    for side in range(sides):
        edge_ref, low_ref, high_ref = edge_refs[3 * side:3 * side + 3]
        if sides == 1:
            first = jnp.where(dec == 0, cols - RMAX, 0)
        else:
            first = cols - RMAX if side == 0 else 0

        def moved(row, lane_of_first):
            return pltpu.roll(x_ref[row].astype(F32), lax.rem(lane_of_first - first + 2 * LANES, LANES), 1)

        tiles = []
        for g, start in enumerate(starts):
            if side == 0 and start in (0, edge, tail):
                loads[(0, edge, tail).index(start) + 1].wait()
            packed = moved(start, 0)
            for j in range(1, SLOTS):
                packed = jnp.where(lane < RMAX * j, packed, moved(start + j, RMAX * j))
            for row, tile in left_over:
                if g in (tile, tile + 1):
                    packed = jnp.where(lane < LANES - SPARE, packed, moved(row, LANES - SPARE - SPARE * (g - tile)))
            edge_ref[g * chans:(g + 1) * chans, :] = packed.astype(BF16)
            tiles.append(packed)
        half = chans // 2

        def beside(part, low):
            return jnp.where((lane[:half] < LANES // 2) == low, part[:half], pltpu.roll(part[half:], LANES // 2, 1))

        packed = jnp.zeros((chans, LANES), F32)
        for j, row in enumerate(shared):
            packed = jnp.where(lane < RMAX * j, packed, moved(row, RMAX * j))
        edge_ref[len(starts) * chans:, :] = beside(packed, True).astype(BF16)
        for ref, whole, part in (
            (low_ref, tiles[:EDGE - 1], beside(tiles[EDGE - 1], True)),
            (high_ref, tiles[1 - EDGE:], beside(tiles[-EDGE], False)),
        ):
            for i, tile in enumerate(whole):
                ref[i * chans:(i + 1) * chans, :] = tile.astype(BF16)
            ref[(EDGE - 1) * chans:, :] = part.astype(BF16)


def pack(x, sides, order):
    rows, chans, cols = x.shape
    packed = [pltpu.VMEM((len(row_groups(rows)[0]) * chans + chans // 2, LANES), BF16)]
    packed += [pltpu.VMEM(((EDGE - 1) * chans + chans // 2, LANES), BF16)] * 2
    return pl.pallas_call(
        functools.partial(pack_kernel, sides),
        out_shape=packed * sides,
        in_specs=[SMEM, HBM],
        out_specs=[VMEM] * (3 * sides),
        scratch_shapes=[pltpu.VMEM(x.shape, BF16), pltpu.SemaphoreType.DMA((4,))],
        compiler_params=PARAMS,
        cost_estimate=pl.CostEstimate(flops=1, bytes_accessed=1, transcendentals=0),
    )(order, x)


def widen(tiles, j):
    lane = lax.broadcasted_iota(jnp.int32, tiles[0].shape, 1)
    value = None
    for side, part in enumerate(tiles):
        shift = (RMAX * side - RMAX * j) % LANES
        part = part if shift == 0 else pltpu.roll(part, shift, 1)
        value = part if side == 0 else jnp.where(lane < RMAX, value, part)
    return value


def inner_kernel(sides, rad_ref, own, dec_ref, ra_ref, *refs):
    edge_refs, (out_ref, begun, halo, result) = refs[:sides], refs[sides:]
    inner, chans, cols = out_ref.shape
    rows = inner + 2 * RMAX
    pitch = chans + PAD
    own_rows = ra_ref.shape[2]
    base = ra_ref.shape[1] - 2 * HALO

    starts, left_over, shared = row_groups(rows)
    for g, start in enumerate(starts):
        tiles = [ref[g * chans:(g + 1) * chans, :].astype(F32) for ref in edge_refs]
        for j in range(SLOTS):
            halo[pl.ds((start + j) * pitch, chans), :] = widen(tiles, j)
    lane = lax.broadcasted_iota(jnp.int32, (chans, LANES), 1)
    for row, g in left_over:
        tiles = []
        for ref in edge_refs:
            begin, end = (
                pltpu.roll(ref[(g + i) * chans:(g + i + 1) * chans, :].astype(F32), SPARE * (1 + i), 1) for i in range(2)
            )
            tiles.append(jnp.where(lane < SPARE, begin, end))
        halo[pl.ds(row * pitch, chans), :] = widen(tiles, 0)
    tiles = [ref[len(starts) * chans:, :].astype(F32) for ref in edge_refs]
    tiles = [jnp.concatenate([tile, pltpu.roll(tile, LANES // 2, 1)], 0) for tile in tiles]
    for j, row in enumerate(shared):
        halo[pl.ds(row * pitch, chans), :] = widen(tiles, j)

    for i in range(rows, own_rows):
        halo[pl.ds(i * pitch, chans), :] = jnp.zeros((chans, cols), F32)

    radii = [rad_ref[c] for c in range(chans)]
    partials = []
    for c, radius in enumerate(radii):
        picked = pl.ds(c, own_rows, stride=pitch)
        lhs = jnp.concatenate([own[picked, :].astype(BF16), halo[picked, :].astype(BF16)], 1)
        partials.append(jnp.dot(lhs, dec_ref[radius], preferred_element_type=F32).astype(BF16))
    for c, (radius, partial) in enumerate(zip(radii, partials)):
        smoothed = jnp.dot(ra_ref[radius], partial, preferred_element_type=F32)
        result[pl.ds(c, inner, stride=pitch), :] = smoothed[:inner]
        begun[pl.ds(c, RMAX, stride=pitch), :] = smoothed[base:base + RMAX]
        begun[pl.ds(RMAX * pitch + c, RMAX, stride=pitch), :] = smoothed[base + HALO:base + HALO + RMAX]

    def store(i, carry):
        out_ref[i] = result[pl.ds(i * pitch, chans), :].astype(BF16)
        return carry

    lax.fori_loop(0, inner, store, 0, unroll=4)


def smooth_inner(radii, rows, own, halos, dec_table, ra_table):
    chans, cols = radii.shape[0], own.shape[1]
    pitch, own_rows, inner = chans + PAD, ra_table.shape[2], rows - 2 * RMAX
    operands = [own, dec_table, ra_table, *halos]
    return pl.pallas_call(
        functools.partial(inner_kernel, len(halos)),
        out_shape=[
            pltpu.VMEM((inner, chans, cols), BF16),
            pltpu.VMEM(((2 * RMAX + 1) * pitch, cols), F32),
        ],
        in_specs=[SMEM] + [VMEM] * len(operands),
        out_specs=[VMEM] * 2,
        scratch_shapes=[
            pltpu.VMEM(((own_rows + 1) * pitch, LANES), F32),
            pltpu.VMEM(((inner + 1) * pitch, cols), F32),
        ],
        compiler_params=PARAMS,
        cost_estimate=pl.CostEstimate(flops=1, bytes_accessed=1, transcendentals=0),
    )(radii, *operands)


def reach_lanes(sides):
    return -(-sides * RMAX // 16) * 16


def outer_begin_kernel(rad_ref, order_ref, before_ref, before_rest, after_ref, after_rest, dec_ref, begun, before, after):
    chans, _, cols = begun.shape
    radii = [rad_ref[c] for c in range(chans)]
    total = functools.reduce(lambda a, b: a + b, radii)
    cap = before_ref.shape[0]
    for packed, head, rest in ((before, before_ref, before_rest), (after, after_ref, after_rest)):
        packed[:HALO, :] = jnp.zeros((HALO, cols), F32)
        packed[HALO:HALO + cap, :] = head[...].astype(F32)
        packed[HALO + cap:2 * HALO + cap, :] = jnp.zeros((HALO, cols), F32)
        packed[packed.shape[0] - HALO:, :] = jnp.zeros((HALO, cols), F32)

        @pl.when(total > cap)
        def _():
            packed[HALO + cap:HALO + cap + rest.shape[0], :] = rest[...].astype(F32)

    offset = 0
    for c, radius in enumerate(radii):
        planes = [
            before[pl.ds(HALO - RMAX + offset + radius, HALO), :],
            after[pl.ds(HALO + offset, HALO), :],
        ]
        lhs = jnp.concatenate(planes, 0).astype(BF16)
        begun[c] = jnp.dot(lhs, dec_ref[radius, :cols, :], preferred_element_type=F32)
        offset = offset + radius


def outer_begin(radii, order, before, after, dec_table):
    chans, cols = radii.shape[0], dec_table.shape[2]
    operands = [*before, *after, dec_table]
    return pl.pallas_call(
        outer_begin_kernel,
        out_shape=pltpu.VMEM((chans, 2 * HALO, cols), F32),
        in_specs=[SMEM, pl.BlockSpec(memory_space=pl.ANY)] + [VMEM] * len(operands),
        out_specs=VMEM,
        scratch_shapes=[pltpu.VMEM((RMAX * chans + 2 * HALO, cols), F32)] * 2,
        compiler_params=PARAMS,
        cost_estimate=pl.CostEstimate(flops=2 * 10**9, bytes_accessed=5 * 10**6, transcendentals=0),
    )(radii, order, *operands)


def outer_kernel(sides, rad_ref, dec_begun, ra_begun, dec_ref, ra_ref, *refs):
    corner_refs, (out_ref, corner, result) = refs[:2 * sides], refs[2 * sides:]
    rows, chans, cols = out_ref.shape
    pitch = chans + PAD
    width = reach_lanes(sides)

    for part, base in ((0, 0), (1, HALO)):
        starts = [g * SLOTS if part else g * SLOTS + RMAX - EDGE * SLOTS for g in range(EDGE)]
        shared = EDGE - 1 if part else 0
        order = [*range(EDGE - 1), EDGE - 1] if part else [EDGE - 1, *range(EDGE - 1)]
        for g, (start, place) in enumerate(zip(starts, order)):
            tiles = []
            for ref in corner_refs[part::2]:
                tile = ref[place * chans:min(place * chans + chans, ref.shape[0]), :].astype(F32)
                if g == shared:
                    tile = jnp.concatenate([tile, pltpu.roll(tile, LANES // 2, 1)], 0)
                tiles.append(tile)
            for j in range(SLOTS):
                if 0 <= start + j < RMAX:
                    corner[pl.ds((base + start + j) * pitch, chans), :] = widen(tiles, j)
        for row in range(RMAX, HALO):
            corner[pl.ds((base + row) * pitch, chans), :] = jnp.zeros((chans, LANES), F32)

    radii = [rad_ref[c] for c in range(chans)]
    partials = []
    for c, radius in enumerate(radii):
        lhs = corner[pl.ds(c, 2 * HALO, stride=pitch), :].astype(BF16)[:, :width]
        partial = jnp.dot(lhs, dec_ref[radius, cols:cols + width, :], preferred_element_type=F32) + dec_begun[c]
        partials.append(partial.astype(BF16))
    for c, (radius, partial) in enumerate(zip(radii, partials)):
        smoothed = jnp.dot(ra_ref[radius], partial, preferred_element_type=F32)
        result[pl.ds(c, RMAX, stride=pitch), :] = smoothed[:RMAX]
        result[pl.ds(RMAX * pitch + c, RMAX, stride=pitch), :] = smoothed[HALO:HALO + RMAX]

    def store(i, carry):
        picked = pl.ds(i * pitch, chans)
        out_ref[i] = (ra_begun[picked, :] + result[picked, :]).astype(BF16)
        return carry

    lax.fori_loop(0, rows, store, 0, unroll=True)


def smooth_outer(radii, dec_begun, ra_begun, dec_table, ra_table, corners):
    chans, _, cols = dec_begun.shape
    pitch = chans + PAD
    operands = [dec_begun, ra_begun, dec_table, ra_table] + [part for side in corners for part in side]
    return pl.pallas_call(
        functools.partial(outer_kernel, len(corners)),
        out_shape=pltpu.VMEM((2 * RMAX, chans, cols), BF16),
        in_specs=[SMEM] + [VMEM] * len(operands),
        out_specs=VMEM,
        scratch_shapes=[
            pltpu.VMEM(((2 * HALO + 1) * pitch, LANES), F32),
            pltpu.VMEM(((2 * RMAX + 1) * pitch, cols), F32),
        ],
        compiler_params=PARAMS,
        cost_estimate=pl.CostEstimate(flops=10**10, bytes_accessed=5 * 10**6, transcendentals=0),
    )(radii, *operands)


SUM_ROWS = 8


def add_products(total, row_refs, own_ref, valid_ref, first_row, rows, sums=None):
    depth = max(d for d in range(1, 65) if rows % d == 0)

    def nt(a, b):
        return lax.dot_general(a, b, (((1,), (1,)), ((), ())), preferred_element_type=F32)

    def body(i, carry):
        picked = [i * depth + j for j in range(depth)]
        line = jnp.concatenate([valid_ref[pl.ds(first_row(r), 1), :].astype(BF16) for r in picked], 1)
        own, *others = (jnp.concatenate([ref[r] for r in picked], 1) for ref in (own_ref, *row_refs))
        total[...] += nt(jnp.concatenate(others, 0), own * line)
        if sums is not None:
            sums[...] += nt(jnp.broadcast_to(line, (16, line.shape[1])), own)[:SUM_ROWS]
        return carry

    lax.fori_loop(0, rows // depth, body, 0, unroll=True)


def outer_row(image_rows):
    return lambda r: jnp.where(r < RMAX, r, r + image_rows - 2 * RMAX)


def own_gram_kernel(own_ref, other_ref, outer_ref, valid_ref, out_ref, cross_ref, smoothed_ref, both, sems):
    rows, chans = valid_ref.shape[0], own_ref.shape[1]
    half = chans // 2
    copies = [
        pltpu.make_async_copy(source, smoothed_ref.at[pl.ds(start, source.shape[0])], sems.at[i])
        for i, (source, start) in enumerate((
            (own_ref, RMAX),
            (outer_ref.at[pl.ds(0, RMAX)], 0),
            (outer_ref.at[pl.ds(RMAX, RMAX)], rows - RMAX),
        ))
    ]
    for copy in copies:
        copy.start()
    both[...] = jnp.zeros_like(both)
    products, own, sums = both.at[:2 * chans], both.at[:chans], both.at[2 * chans:]
    add_products(products, (own_ref, other_ref), own_ref, valid_ref, lambda r: r + RMAX, own_ref.shape[0], sums)
    add_products(own, (outer_ref,), outer_ref, valid_ref, outer_row(rows), 2 * RMAX, sums)
    cross_ref[...] = both[chans:2 * chans, :]
    low = pltpu.roll(both[half:chans, :], half, 1)
    row = lax.broadcasted_iota(jnp.int32, (half, chans), 0)
    lane = lax.broadcasted_iota(jnp.int32, (half, chans), 1)
    out_ref[:half, :] = jnp.where(lane < row, low, both[:half, :])
    diagonal = jnp.sum(jnp.where(lane == row, low, 0.0), axis=0, keepdims=True)
    row = lax.broadcasted_iota(jnp.int32, (SUM_ROWS, chans), 0)
    tail = jnp.where(row == 1, diagonal, both[2 * chans:, :])
    out_ref[half:, :] = jnp.where(row == 2, jnp.sum(valid_ref[...].astype(F32)), tail)
    for copy in copies:
        copy.wait()


def own_gram(own, other, outer, valid):
    _, chans, cols = own.shape
    return pl.pallas_call(
        own_gram_kernel,
        out_shape=[
            pltpu.VMEM((chans // 2 + SUM_ROWS, chans), F32),
            pltpu.VMEM((chans, chans), F32),
            jax.ShapeDtypeStruct((valid.shape[0], chans, cols), BF16),
        ],
        in_specs=[VMEM] * 4,
        out_specs=[VMEM, VMEM, HBM],
        scratch_shapes=[pltpu.VMEM((2 * chans + SUM_ROWS, chans), F32), pltpu.SemaphoreType.DMA((3,))],
        compiler_params=PARAMS,
        cost_estimate=pl.CostEstimate(flops=10**9, bytes_accessed=3 * 10**6, transcendentals=0),
    )(own, other, outer, valid)


def cross_gram_kernel(folded_ref, cross_ref, own_ref, other_ref, valid_ref, out_ref, total):
    chans = own_ref.shape[1]
    half = chans // 2
    total[...] = cross_ref[...]
    add_products(total, (other_ref,), own_ref, valid_ref, outer_row(valid_ref.shape[0]), 2 * RMAX)
    cross = total[...]
    out_ref[:half, :] = folded_ref[:half, :]
    out_ref[half:chans, :] = jnp.where(lax.axis_index("band") == 0, cross[:half], jnp.transpose(cross)[half:])
    out_ref[chans:, :] = folded_ref[half:, :]


def cross_gram(folded, cross, own, other, valid):
    chans = own.shape[1]
    return pl.pallas_call(
        cross_gram_kernel,
        out_shape=pltpu.VMEM((chans + SUM_ROWS, chans), F32),
        in_specs=[VMEM] * 5,
        out_specs=VMEM,
        scratch_shapes=[pltpu.VMEM((chans, chans), F32)],
        compiler_params=PARAMS,
    )(folded, cross, own, other, valid)


def finish_kernel(mine_ref, theirs_ref, mean_ref, cov_ref):
    chans = mine_ref.shape[1]
    half = chans // 2
    band = lax.axis_index("band")
    count = mine_ref[chans + 2:chans + 3, :1]
    folded = mine_ref[:half, :]
    mirror = jnp.transpose(jnp.concatenate([folded, jnp.zeros((half, chans), F32)], 0))
    row = lax.broadcasted_iota(jnp.int32, (half, chans), 0)
    lane = lax.broadcasted_iota(jnp.int32, (half, chans), 1)
    upper = jnp.where(lane < row, mirror[:half], folded)
    column = lane - half
    corner = jnp.where(column < row, pltpu.roll(folded, half, 1), pltpu.roll(mirror[:half], half, 1))
    corner = jnp.where(column == row, pltpu.roll(mine_ref[chans:chans + SUM_ROWS, :], half, 1)[1:2, :], corner)
    own = jnp.concatenate([upper, jnp.where(column < 0, mirror[half:], corner)], 0)
    mine, theirs = mine_ref[half:chans, :], theirs_ref[half:chans, :]
    cross = jnp.concatenate([jnp.where(band == 0, mine, theirs), jnp.where(band == 0, theirs, mine)], 0)
    cross = jnp.where(band == 0, cross, jnp.transpose(cross))
    mean = mine_ref[chans:chans + 1, :] / count
    other_mean = theirs_ref[chans:chans + 1, :] / count
    mean_ref[...] = mean
    for block, left, b in ((own, mean, band), (cross, other_mean, 1 - band)):
        left = jnp.transpose(jnp.broadcast_to(left, (chans, chans)))
        cov_ref[pl.ds(pl.multiple_of(b * chans, chans), chans), :] = (block - count * left * mean) / (count - 1.0)


def finish(mine, theirs):
    chans = mine.shape[1]
    mean, covariance = pl.pallas_call(
        finish_kernel,
        out_shape=[jax.ShapeDtypeStruct((1, chans), F32), jax.ShapeDtypeStruct((2 * chans, chans), F32)],
        in_specs=[VMEM] * 2,
        out_specs=[VMEM] * 2,
        compiler_params=PARAMS,
    )(mine, theirs)
    return mean.reshape(chans), covariance


def swap(array, axis, step):
    size = lax.axis_size(axis)
    return lax.ppermute(array, axis, [(i, i ^ step) for i in range(size)])


def diagonal(array, ra_step, dec_pairs):
    ra_size, dec_size = lax.axis_size("ra"), lax.axis_size("dec")
    pairs = [
        (i * dec_size + a, (i + ra_step) % ra_size * dec_size + b) for i in range(ra_size) for a, b in dec_pairs
    ]
    return lax.ppermute(array, ("ra", "dec"), pairs)


def per_device(sky_maps, radii, valid):
    x = jnp.transpose(sky_maps, (1, 0, 2))
    radii = pltpu.with_memory_space_constraint(radii, pltpu.HBM)
    x = pltpu.with_memory_space_constraint(x, pltpu.HBM)
    rows, chans, cols = x.shape
    ra_size, dec_size = lax.axis_size("ra"), lax.axis_size("dec")
    up = [(i, (i + 1) % ra_size) for i in range(ra_size)]
    down = [(j, i) for i, j in up]
    right = [(i, i + 1) for i in range(dec_size - 1)]
    left = [(j, i) for i, j in right]
    sides = [right + left] if dec_size == 2 else [right, left]
    over, up_head, up_rest, down_head, down_rest = gather(radii, x)
    packed = pack(x, len(sides), over)
    before_rest, after_rest = lax.switch(
        over[0],
        [lambda a, b: (a, b), lambda a, b: (lax.ppermute(a, "ra", up), lax.ppermute(b, "ra", down))],
        up_rest, down_rest,
    )
    before, after = lax.ppermute(up_head, "ra", up), lax.ppermute(down_head, "ra", down)
    packed = [packed[3 * i:3 * i + 3] for i in range(len(sides))]
    halos = [lax.ppermute(p, "dec", pairs) for (p, _, _), pairs in zip(packed, sides)]
    corners = [
        (diagonal(high, 1, pairs), diagonal(low, -1, pairs)) for (_, low, high), pairs in zip(packed, sides)
    ]
    dec_table, inner_table, outer_table, own = tables(x, len(sides), before_rest)
    inner, begun = smooth_inner(radii, rows, own, halos, dec_table, inner_table)
    dec_begun = outer_begin(radii, begun, (before, before_rest), (after, after_rest), dec_table)
    outer = smooth_outer(radii, dec_begun, begun, dec_table, outer_table, corners)
    folded, cross, smoothed = own_gram(inner, swap(inner, "band", 1), outer, valid)
    total = cross_gram(folded, cross, outer, swap(outer, "band", 1), valid)
    steps = [("dec", 1 << b) for b in range(dec_size.bit_length() - 1)]
    steps += [("ra", 1 << b) for b in range(ra_size.bit_length() - 1)]
    for axis, step in steps:
        total = total + swap(total, axis, step)
    mean, covariance = finish(total, swap(total, "band", 1))
    return (jnp.transpose(smoothed, (1, 0, 2)), mean, covariance)


def solution(mesh):
    return jax.shard_map(
        per_device,
        mesh=mesh,
        in_specs=(
            P(("groups", "band"), "ra", "dec"),
            P(("groups", "band")),
            P(("groups", "ra"), "dec"),
        ),
        out_specs=(P(("groups", "band"), "ra", "dec"), P(("groups", "band")), P("groups", "band")),
        check_vma=False,
    )
```
